32 devices in a mesh: sp: 8 (over z, x), ch: 4 (over y, core).
Axes of the slice: x: 2, y: 2, z: 4, core: 2. Of those that a mesh axis runs over, the one named last changes fastest.
Arguments:
- features: bfloat16 [4, 48, 48, 2048], P(None, 'sp'), may hold values from -80 to 80
- heights: int32 [4, 1], replicated, may hold values from 24 to 48, as said below
- widths: int32 [4, 1], replicated, may hold values from 24 to 48, as said below
- w_point: bfloat16 [256, 2048], P('ch'), may hold values from -0.125 to 0.125
- atrous_weight: bfloat16 [3, 3, 3, 256, 2048], P(None, None, None, 'ch'), may hold values from -0.046875 to 0.046875
- w_pool: bfloat16 [256, 2048], P('ch'), may hold values from -0.125 to 0.125
- w_proj: bfloat16 [5, 256, 256], P(None, 'ch'), may hold values from -0.15625 to 0.15625
- bn_gains: float32 [6, 256], P(None, 'ch'), may hold values from 0.25 to 1.75
- bn_shifts: float32 [6, 256], P(None, 'ch'), may hold values from -2.5 to 2.5
- out_grad: bfloat16 [4, 48, 48, 256], P(None, 'sp'), may hold values from -6 to 6
Outputs:
- output: bfloat16 [4, 48, 48, 256], P(None, 'sp', None, 'ch')
- in_grad: bfloat16 [4, 48, 48, 2048], P(None, 'sp', None, 'ch')
- g_point: float32 [256, 2048], P('ch')
- g_atrous: float32 [3, 3, 3, 256, 2048], P(None, None, None, 'ch')
- g_pool: float32 [256, 2048], P('ch')
- g_proj: float32 [5, 256, 256], P(None, 'ch')
- g_gains: float32 [6, 256], P(None, 'ch')
- g_shifts: float32 [6, 256], P(None, 'ch')
The draws below stay inside these ranges and needn't reach their ends.
Inputs may be any that keep to these rules, and one draw needn't show every extreme that they name: `heights`: in every column g one image has height 48. `widths`: in every column g one image has width 48.
All inputs are finite; a program needn't handle non-finite values.
Results may differ from the reference program's by a relative error of at most 0.014.
Values may be sent and summed in bfloat16 or wider, within the bound.
No kernel may reach another device: no remote copies, remote signals or barrier semaphores. Data moves between devices by JAX's collectives and lax.ppermute only.
A program may use at most 256 MiB of HBM per device.

```python
import jax
import jax.numpy as jnp
from jax import lax

INPUT_CHANNELS = 2048
F = 256
K = 4
ROWS = 6
GRID_COLUMNS = 48
GRID_ROWS = 48
GROUPS = 1
IMAGES = 4


def draw_features(key, part):
    key = jax.random.fold_in(key, 11)
    key_noise, key_offset = jax.random.split(key, 2)
    full_shape = (K, GROUPS, GRID_ROWS, GRID_COLUMNS, INPUT_CHANNELS)
    row_index = jnp.arange(GRID_ROWS).astype(jnp.float32)
    row_ramp = jnp.exp(jnp.log(3.0) * row_index / (GRID_ROWS - 1))[None, None, :, None, None]
    offset = 0.5 * jax.random.normal(key_offset, (K, GROUPS, 1, 1, INPUT_CHANNELS), jnp.float32)
    noise_vals = jax.random.normal(key_noise, full_shape, jnp.float32)
    values = noise_vals * row_ramp + offset
    return values.reshape(K, GROUPS * GRID_ROWS, GRID_COLUMNS, INPUT_CHANNELS).astype(jnp.bfloat16)


def extent_draw(key, largest):
    key_random, key_chosen = jax.random.split(key)
    random_base = jax.random.randint(key_random, (K, GROUPS), largest // 2, largest + 1)
    chosen = jax.random.randint(key_chosen, (GROUPS,), 0, K)
    is_full = jnp.arange(K)[:, None] == chosen[None, :]
    return jnp.where(is_full, largest, random_base).astype(jnp.int32)


def draw_heights(key, part):
    key = jax.random.fold_in(key, 21)
    return extent_draw(key, GRID_ROWS)


def draw_widths(key, part):
    key = jax.random.fold_in(key, 22)
    return extent_draw(key, GRID_COLUMNS)


def shard_levels(key, shape, cuts, smallest, high):
    level = 1.0
    for dim, parts in cuts:
        draws = jax.random.uniform(jax.random.fold_in(jax.random.fold_in(key, 6), dim), (parts,), jnp.float32, smallest / len(cuts), high / len(cuts))
        level = level * jnp.repeat(jnp.exp(draws), shape[dim] // parts).reshape((-1,) + (1,) * (len(shape) - 1 - dim))
    return level


def normal_values(key, shape, scale, bound, shards=(), kind=jnp.bfloat16):
    values = scale * jax.random.normal(key, shape, jnp.float32)
    if shards:
        values = values * shard_levels(key, shape, shards, -0.22, 0.18)
    return jnp.clip(values, -bound, bound).astype(kind)


def setup_inputs(seed: int = 0) -> dict:
    keys = jax.random.split(jax.random.key(seed), 11)
    return {
        "features": draw_features(jax.random.fold_in(keys[10], 71), 0),
        "heights": draw_heights(jax.random.fold_in(keys[10], 71), 0),
        "widths": draw_widths(jax.random.fold_in(keys[10], 71), 0),
        "w_point": normal_values(keys[3], (F, INPUT_CHANNELS), INPUT_CHANNELS ** -0.5, 0.125, ((0, 4),)),
        "atrous_weight": normal_values(keys[4], (3, 3, 3, F, INPUT_CHANNELS), (9 * INPUT_CHANNELS) ** -0.5, 0.046875, ((3, 4),)),
        "w_pool": normal_values(keys[5], (F, INPUT_CHANNELS), INPUT_CHANNELS ** -0.5, 0.125, ((0, 4),)),
        "w_proj": normal_values(keys[6], (5, F, F), (5 * F) ** -0.5, 0.15625, ((1, 4),)),
        "bn_gains": jnp.clip(1.0 + 0.15 * jax.random.normal(keys[7], (6, F), jnp.float32), 0.25, 1.75),
        "bn_shifts": normal_values(keys[8], (6, F), 0.5, 2.5, ((1, 4),), jnp.float32),
        "out_grad": normal_values(keys[9], (K, GROUPS * GRID_ROWS, GRID_COLUMNS, F), 1.0, 6.0, ((1, 8),)),
    }


epsilon = 1e-05
dilation_factors = (1, 2, 3)
highest_precision = lax.Precision.HIGHEST

@jax.custom_vjp
def low(v):
    return lax.optimization_barrier(v.astype(jnp.bfloat16)).astype(jnp.float32)

@jax.custom_vjp
def low_back(v):
    return v

def low_keep(v):
    return (low(v), None)

def low_pass(kept, grad):
    return (grad,)

def back_keep(v):
    return (v, None)

def back_low(kept, grad):
    return (low(grad),)
low.defvjp(low_keep, low_pass)
low_back.defvjp(back_keep, back_low)

def batch_norm(values, weights, total, gain, shift, axes):
    mean_val = lax.optimization_barrier(jnp.sum(values * weights, axis=axes, keepdims=True)) / total
    square = lax.optimization_barrier(jnp.sum(values * values * weights, axis=axes, keepdims=True)) / total
    normed = (values - mean_val) * lax.rsqrt(square - mean_val * mean_val + epsilon)
    return gain * normed + shift

def forward(feats, w_point, atrous_weight, w_pool, w_proj, bn_gains, bn_shifts, pix_mask):
    masked_values = feats * pix_mask

    def per_image(one_image):
        flat_pix = one_image.reshape(GRID_ROWS * GRID_COLUMNS, INPUT_CHANNELS)
        branch_outs = [jnp.dot(flat_pix, w_point.T, precision=highest_precision)]
        for dilation_index, dilation_factor in enumerate(dilation_factors):
            dilation_rate = ROWS * dilation_factor
            padded = jnp.pad(one_image, ((dilation_rate, dilation_rate), (dilation_rate, dilation_rate), (0, 0)))
            running_total = jnp.zeros((GRID_ROWS * GRID_COLUMNS, F), jnp.float32)
            for row_offset_tap in range(3):
                for column_offset_tap in range(3):
                    shifted_window = lax.slice(padded, (row_offset_tap * dilation_rate, column_offset_tap * dilation_rate, 0), (row_offset_tap * dilation_rate + GRID_ROWS, column_offset_tap * dilation_rate + GRID_COLUMNS, INPUT_CHANNELS))
                    running_total = running_total + jnp.dot(shifted_window.reshape(GRID_ROWS * GRID_COLUMNS, INPUT_CHANNELS), atrous_weight[dilation_index, row_offset_tap, column_offset_tap].T, precision=highest_precision)
            branch_outs.append(running_total)
        return (jnp.stack(branch_outs), lax.optimization_barrier(jnp.sum(flat_pix, axis=0)))
    conv_out, pixel_sums = lax.map(jax.checkpoint(per_image), masked_values)
    conv_out = low_back(conv_out)
    weights = pix_mask.reshape(IMAGES, 1, GRID_ROWS * GRID_COLUMNS, 1)
    valid_count = jnp.sum(pix_mask)
    pre_act = batch_norm(conv_out, weights, valid_count, bn_gains[:4][None, :, None, :], bn_shifts[:4][None, :, None, :], (0, 2))
    branch_act = low(weights * jax.nn.silu(pre_act))
    image_count = lax.optimization_barrier(jnp.sum(pix_mask, axis=(1, 2, 3)))
    pooled = pixel_sums / image_count[:, None]
    projected = jnp.dot(pooled, w_pool.T, precision=highest_precision)
    pool_pre = batch_norm(projected, 1.0, IMAGES, bn_gains[4], bn_shifts[4], (0,))
    pool_act = low(jax.nn.silu(pool_pre))
    pool_branch = pool_act[:, None, None, :] * weights
    stacked = jnp.concatenate([branch_act, pool_branch], axis=1)
    mixed_sum = low_back(jnp.einsum('ibpf,bfo->ipo', stacked, w_proj, precision=highest_precision))
    final_weights = pix_mask.reshape(IMAGES, GRID_ROWS * GRID_COLUMNS, 1)
    final_pre = batch_norm(mixed_sum, final_weights, valid_count, bn_gains[5], bn_shifts[5], (0, 1))
    return final_weights * jax.nn.silu(final_pre)

def reference(features, heights, widths, w_point, atrous_weight, w_pool, w_proj, bn_gains, bn_shifts, out_grad):
    row_ids = jnp.arange(GRID_ROWS, dtype=jnp.int32)
    col_ids = jnp.arange(GRID_COLUMNS, dtype=jnp.int32)
    image_heights = heights.reshape(IMAGES)
    image_widths = widths.reshape(IMAGES)
    inside = (row_ids[None, :, None] < image_heights[:, None, None]) & (col_ids[None, None, :] < image_widths[:, None, None])
    pix_mask = inside.astype(jnp.float32)[..., None]
    feats = features.astype(jnp.float32).reshape(IMAGES, GRID_ROWS, GRID_COLUMNS, INPUT_CHANNELS)

    def with_mask(feat_arg, point_arg, atrous_arg, pool_arg, proj_arg, gain_arg, shift_arg):
        return forward(feat_arg, point_arg, atrous_arg, pool_arg, proj_arg, gain_arg, shift_arg, pix_mask)
    result, pullback = jax.vjp(with_mask, feats, w_point.astype(jnp.float32), atrous_weight.astype(jnp.float32), w_pool.astype(jnp.float32), w_proj.astype(jnp.float32), bn_gains.astype(jnp.float32), bn_shifts.astype(jnp.float32))
    cotangent = out_grad.astype(jnp.float32).reshape(IMAGES, GRID_ROWS * GRID_COLUMNS, F)
    grads = pullback(cotangent)
    output = result.reshape(K, GROUPS * GRID_ROWS, GRID_COLUMNS, F).astype(jnp.bfloat16)
    in_grad = grads[0].reshape(K, GROUPS * GRID_ROWS, GRID_COLUMNS, INPUT_CHANNELS).astype(jnp.bfloat16)
    return (output, in_grad, grads[1], grads[2], grads[3], grads[4], grads[5], grads[6])
```

```python
import functools

import jax
import jax.numpy as jnp
from jax import lax
from jax.experimental import pallas as pl
from jax.experimental.pallas import tpu as pltpu
from jax.sharding import PartitionSpec as P

BLOCKS = 8
BRANCHES = 4
epsilon = 1e-05
dilation_factors = (1, 2, 3)
highest_precision = lax.Precision.HIGHEST
f32 = jnp.float32
bf16 = jnp.bfloat16
MIB = 1 << 20
VMEM = pl.BlockSpec(memory_space=pltpu.VMEM)
SMEM = pl.BlockSpec(memory_space=pltpu.SMEM)
NT = (((1,), (1,)), ((), ()))
NN = (((1,), (0,)), ((), ()))
TN = (((0,), (0,)), ((), ()))


def dot(a, b, dims):
    return lax.dot_general(a, b, dims, preferred_element_type=f32)


def params(mib=48, **kw):
    return pltpu.CompilerParams(vmem_limit_bytes=mib * MIB, **kw)


def cost(flops, nbytes):
    return pl.CostEstimate(flops=int(flops), bytes_accessed=int(nbytes), transcendentals=0)


def cell_mask(lim_ref, slabs, cols, width):
    col = lax.broadcasted_iota(jnp.int32, (cols, width), 0)
    return jnp.concatenate([(col < lim_ref[i]).astype(f32) for i in range(slabs)], axis=0)


def column_ids(slabs, cols, width):
    return lax.broadcasted_iota(jnp.int32, (slabs, cols, width), 1).reshape(slabs * cols, width)


def from_left(a, d, col):
    return jnp.where(col >= d, pltpu.roll(a, d, 0), 0.0)


def from_right(a, d, col, cols):
    return jnp.where(col < cols - d, pltpu.roll(a, a.shape[0] - d, 0), 0.0)


def silu_parts(t):
    s = 1.0 / (1.0 + jnp.exp(-t))
    return s, t * s


def slope(t, s):
    return s * (1.0 + t * (1.0 - s))


def column_sums(*rows):
    sums = [jnp.sum(r, axis=0, keepdims=True) for r in rows]
    width = sums[0].shape[1]
    return jnp.concatenate(sums + [jnp.zeros((8 - len(sums), width), f32)], axis=0)


def side_kernel(lim_ref, x_ref, wm_ref, wp_ref, *refs, steps, slabs, cols, rates):
    outs, (wcat, acc) = refs[:6], refs[6:]
    k = pl.program_id(0)
    L = wm_ref.shape[3]
    for j in range(3):
        for v in range(3):
            t = (j * 3 + v) * 2 * L
            wcat[t : t + L] = wm_ref[j, 0, v]
            wcat[t + L : t + 2 * L] = wp_ref[j, 0, v]

    @pl.when(k == 0)
    def _():
        acc[...] = jnp.zeros_like(acc)

    x = x_ref[...]
    total = 18 * L
    for n in range(0, total, 256):
        e = min(n + 256, total)
        acc[:, n:e] += dot(x, wcat[n:e], NT)

    @pl.when(k == steps - 1)
    def _():
        cells = slabs * cols
        half = cells // 2
        mask = cell_mask(lim_ref, slabs, cols, 2 * L)
        col = column_ids(slabs, cols, 2 * L)
        low = lax.broadcasted_iota(jnp.int32, (half, 2 * L), 1) < L
        for j in range(3):
            a = [acc[:, (j * 3 + v) * 2 * L : (j * 3 + v + 1) * 2 * L] * mask for v in range(3)]
            s = a[1] + from_left(a[0], rates[j], col) + from_right(a[2], rates[j], col, cols)
            top, bottom = s[:half], s[half:]
            outs[2 * j][...] = jnp.where(low, top, pltpu.roll(bottom, L, 1)).astype(bf16)
            outs[2 * j + 1][...] = jnp.where(low, pltpu.roll(top, L, 1), bottom).astype(bf16)


def centre_kernel(
    lim_ref, x_ref, wc_ref, wpoint_ref, out_ref, sums_ref, wcat, acc, *, steps, slabs, cols, rates, images
):
    k = pl.program_id(0)
    L = wpoint_ref.shape[0]
    order = [None, (0, 1), (1, 1), (2, 1), (1, 0), (2, 0), (1, 2), (2, 2), (0, 0), (0, 2)]
    for i, tap in enumerate(order):
        wcat[i * L : (i + 1) * L] = wpoint_ref[...] if tap is None else wc_ref[tap[0], 0, tap[1]]

    @pl.when(k == 0)
    def _():
        acc[...] = jnp.zeros_like(acc)

    x = x_ref[...]
    total = 10 * L
    for n in range(0, total, 256):
        e = min(n + 256, total)
        acc[:, n:e] += dot(x, wcat[n:e], NT)

    width = x_ref.shape[1]
    cid = lax.broadcasted_iota(jnp.int32, (cols, width), 0)
    per = slabs // images
    sums = []
    for image in range(images):
        part = jnp.zeros((cols, width), f32)
        for i in range(image * per, (image + 1) * per):
            part += jnp.where(cid < lim_ref[i], x_ref[i * cols : (i + 1) * cols].astype(f32), 0.0)
        sums.append(jnp.sum(part, axis=0, keepdims=True))
    sums_ref[...] = jnp.concatenate(sums + [jnp.zeros((8 - images, width), f32)], axis=0)

    @pl.when(k == steps - 1)
    def _():
        cells = slabs * cols
        mask = cell_mask(lim_ref, slabs, cols, 2 * L)
        col = column_ids(slabs, cols, 2 * L)
        low = lax.broadcasted_iota(jnp.int32, (cells, 2 * L), 1) < L
        b = [acc[:, i * 2 * L : (i + 1) * 2 * L] * mask for i in range(5)]
        d0, d1, d2 = rates
        t = jnp.where(low, from_left(b[4], d0, col), from_right(b[4], d0, col, cols))
        out_ref[:, : 2 * L] = b[0] + jnp.where(low, 0.0, t + pltpu.roll(t, L, 1))
        out_ref[:, 2 * L :] = (
            b[1]
            + jnp.where(low, from_left(b[2], d1, col), from_left(b[2], d2, col))
            + jnp.where(low, from_right(b[3], d1, col, cols), from_right(b[3], d2, col, cols))
        )


def combine_kernel(lim_ref, centre_ref, *refs, slabs, cols):
    halo, (conv_ref, send_ref, stat_ref) = refs[:6], refs[6:]
    cells = slabs * cols
    half = cells // 2
    W = centre_ref.shape[1]
    L = W // 4
    h = [halo[2 * j][...].astype(f32) + halo[2 * j + 1][...].astype(f32) for j in range(3)]
    turned = [pltpu.roll(a, L, 1) for a in h]
    low = lax.broadcasted_iota(jnp.int32, (cells, 2 * L), 1) < L
    h0 = jnp.concatenate([turned[0], h[0]], axis=0)
    h1 = jnp.concatenate([h[1], turned[1]], axis=0)
    h2 = jnp.concatenate([turned[2], h[2]], axis=0)
    left = centre_ref[:, : 2 * L] + jnp.where(low, 0.0, h0)
    right = centre_ref[:, 2 * L :] + jnp.where(low, h1, h2)
    conv_ref[:, : 2 * L] = left
    conv_ref[:, 2 * L :] = right
    mask = cell_mask(lim_ref, slabs, cols, 2 * L)
    own = lim_ref[0]
    for i in range(1, slabs):
        own = own + lim_ref[i]
    own = jnp.maximum(own, 1).astype(f32)
    for lo, part in ((0, left), (2 * L, right)):
        s = jnp.sum(part * mask, axis=0, keepdims=True)
        q = jnp.sum(part * part * mask, axis=0, keepdims=True)
        local = s / own
        send_ref[:, lo : lo + 2 * L] = (part - local).astype(bf16)
        stat_ref[:, lo : lo + 2 * L] = jnp.concatenate([s, q, local, jnp.zeros((5, 2 * L), f32)], axis=0)


def mix_kernel(
    lim_ref, conv_ref, c1_ref, c2_ref, c3_ref, stat_ref, gain_ref, wbranch_ref, pool_ref, wpool_ref,
    mixed_ref, act_ref, sums_ref, scratch, *, slabs, cols, images
):
    cells = slabs * cols
    per = slabs // images
    for d, ref in enumerate((conv_ref, c1_ref, c2_ref, c3_ref)):
        mean, rstd, local = stat_ref[d, 0:1], stat_ref[d, 1:2], stat_ref[d, 2:3]
        offset = mean if d == 0 else mean - local
        scale = rstd * gain_ref[d, 0:1]
        shift = gain_ref[d, 1:2]
        dest = act_ref if d == 0 else scratch
        width = ref.shape[1]
        cid = lax.broadcasted_iota(jnp.int32, (cols, width), 0)
        for i in range(slabs):
            rows = slice(i * cols, (i + 1) * cols)
            pre = (ref[rows].astype(f32) - offset) * scale + shift
            _, act = silu_parts(pre)
            dest[rows] = jnp.where(cid < lim_ref[i], act, 0.0).astype(bf16)
        part = dot(dest[...], wbranch_ref[d], NN)
        if d == 0:
            mixed_ref[...] = part
        else:
            mixed_ref[...] += part
    pooled = dot(pool_ref[0], wpool_ref[0], NN)
    for d in range(1, 4):
        pooled += dot(pool_ref[d], wpool_ref[d], NN)
    F = mixed_ref.shape[1]
    cid = lax.broadcasted_iota(jnp.int32, (cols, F), 0)
    s = jnp.zeros((cols, F), f32)
    q = jnp.zeros((cols, F), f32)
    for i in range(slabs):
        rows = slice(i * cols, (i + 1) * cols)
        image = i // per
        value = mixed_ref[rows] + jnp.where(cid < lim_ref[i], pooled[image : image + 1], 0.0)
        mixed_ref[rows] = value
        s += value
        q += value * value
    sums_ref[...] = column_sums(s, q)


def final_kernel(lim_ref, mixed_ref, grad_ref, stat_ref, out_ref, dt_ref, sums_ref, *, slabs, cols):
    F = mixed_ref.shape[1]
    mean, rstd, gain, shift = (stat_ref[i : i + 1] for i in range(4))
    cid = lax.broadcasted_iota(jnp.int32, (cols, F), 0)
    s = jnp.zeros((cols, F), f32)
    q = jnp.zeros((cols, F), f32)
    for i in range(slabs):
        rows = slice(i * cols, (i + 1) * cols)
        valid = cid < lim_ref[i]
        normed = (mixed_ref[rows] - mean) * rstd
        pre = gain * normed + shift
        sig, act = silu_parts(pre)
        out_ref[rows] = jnp.where(valid, act, 0.0).astype(bf16)
        dt = jnp.where(valid, grad_ref[rows].astype(f32) * slope(pre, sig), 0.0)
        dt_ref[rows] = dt
        s += dt
        q += dt * normed
    sums_ref[...] = column_sums(s, q)


def branch_kernel(
    lim_ref, mixed_ref, fdt_ref, fstat_ref, conv_ref, act_ref, stat_ref, wbranch_ref,
    dt_ref, gproj_ref, image_ref, sums_ref, grad, *, slabs, cols, images
):
    F = mixed_ref.shape[1]
    W = conv_ref.shape[1]
    per = slabs // images
    mean, rstd, scale, beta, gamma = (fstat_ref[i : i + 1] for i in range(5))
    cid = lax.broadcasted_iota(jnp.int32, (cols, F), 0)
    image_sums = []
    for image in range(images):
        total = jnp.zeros((cols, F), f32)
        for i in range(image * per, (image + 1) * per):
            rows = slice(i * cols, (i + 1) * cols)
            normed = (mixed_ref[rows] - mean) * rstd
            g = jnp.where(cid < lim_ref[i], scale * (fdt_ref[rows] - beta - normed * gamma), 0.0)
            g = g.astype(bf16)
            grad[rows] = g
            total += g.astype(f32)
        image_sums.append(jnp.sum(total, axis=0, keepdims=True))
    image_ref[...] = jnp.concatenate(image_sums + [jnp.zeros((8 - images, F), f32)], axis=0)
    dt_ref[...] = dot(grad[...], wbranch_ref[...], NT)
    gproj_ref[...] = dot(act_ref[...], grad[...], TN)
    bmean, brstd, bgain, bshift = (stat_ref[i : i + 1] for i in range(4))
    cid = lax.broadcasted_iota(jnp.int32, (cols, W), 0)
    s = jnp.zeros((cols, W), f32)
    q = jnp.zeros((cols, W), f32)
    for i in range(slabs):
        rows = slice(i * cols, (i + 1) * cols)
        normed = (conv_ref[rows] - bmean) * brstd
        pre = bgain * normed + bshift
        sig, _ = silu_parts(pre)
        dt = jnp.where(cid < lim_ref[i], dt_ref[rows] * slope(pre, sig), 0.0)
        dt_ref[rows] = dt
        s += dt
        q += dt * normed
    sums_ref[...] = column_sums(s, q)


def grad_kernel(lim_ref, dt_ref, conv_ref, stat_ref, cg_ref, *, slabs, cols):
    W = conv_ref.shape[1]
    mean, rstd, scale, beta, gamma = (stat_ref[i : i + 1] for i in range(5))
    cid = lax.broadcasted_iota(jnp.int32, (cols, W), 0)
    for i in range(slabs):
        rows = slice(i * cols, (i + 1) * cols)
        normed = (conv_ref[rows] - mean) * rstd
        g = scale * (dt_ref[rows] - beta - normed * gamma)
        cg_ref[rows] = jnp.where(cid < lim_ref[i], g, 0.0).astype(bf16)


def grouped(pairs, size):
    return [(g * BLOCKS + a, g * BLOCKS + b) for g in range(size // BLOCKS) for a, b in pairs]


def from_behind(block, axis, distance):
    size = lax.axis_size(axis)
    pairs = [(i - distance, i) for i in range(BLOCKS) if 0 <= i - distance < BLOCKS]
    return lax.ppermute(block, axis, grouped(pairs, size))


def swap(block, axis, bits):
    return lax.ppermute(block, axis, [(i, i ^ bits) for i in range(lax.axis_size(axis))])


def sum_over_sp(x):
    x = x + swap(x, "sp", 1)
    parts = [swap(x, "sp", b) for b in (2, 4, 6)]
    return x + parts[0] + parts[1] + parts[2]


def plain_from_behind(block, axis, distance):
    devices = range(lax.axis_size(axis))
    route = [(i - distance, i) for i in devices if i - distance in devices]
    return lax.ppermute(block, axis, route)


def shift_cols(values, offset):
    margin = abs(offset)
    padded = jnp.pad(values, ((0, 0), (0, 0), (margin, margin), (0, 0)))
    return lax.slice_in_dim(padded, margin + offset, margin + offset + values.shape[2], axis=2)


def silu_slope(pre_act):
    sigmoid_val = jax.nn.sigmoid(pre_act)
    return sigmoid_val * (1.0 + pre_act * (1.0 - sigmoid_val))


def source_inside(block_id, shift_amount):
    source = block_id - shift_amount
    return (source >= 0) & (source < BLOCKS)


def move_features(values, shift_amount):
    return plain_from_behind(values, "sp", shift_amount)


def shifted_gradients(values, shift_amount):
    return plain_from_behind(values, "sp", shift_amount)


def tap_partials(source, weight_taps, dilation_rate):
    count_k, rows_dev, grid_width, channel_total = source.shape
    local_output = weight_taps.shape[1]
    products = jnp.einsum(
        "pc,tc->pt",
        source.reshape(-1, channel_total),
        weight_taps.reshape(3 * local_output, channel_total),
        preferred_element_type=jnp.float32,
    ).reshape(count_k, rows_dev, grid_width, 3, local_output)
    return (
        shift_cols(products[:, :, :, 0, :], -dilation_rate)
        + products[:, :, :, 1, :]
        + shift_cols(products[:, :, :, 2, :], dilation_rate)
    )


def plain_body(
    features, heights, widths, w_point, atrous_weight, w_pool, w_proj, bn_gains, bn_shifts, out_grad
):
    count_k, rows_dev, grid_width, channel_total = features.shape
    local_output = w_point.shape[0]
    full_out = w_proj.shape[2]
    groups = heights.shape[1]
    images = count_k * groups
    pixels = count_k * rows_dev * grid_width
    position = lax.axis_index("sp")
    block_id = position % BLOCKS
    group_id = position // BLOCKS
    channel_start = lax.axis_index("ch") * local_output
    own_out_grad = lax.dynamic_slice_in_dim(out_grad, channel_start, local_output, 3)
    group_pick = jnp.arange(groups, dtype=jnp.int32) == group_id
    group_onehot = group_pick.astype(jnp.float32)
    own_heights = jnp.sum(jnp.where(group_pick[None, :], heights, 0), axis=1)
    own_widths = jnp.sum(jnp.where(group_pick[None, :], widths, 0), axis=1)
    row_ids = block_id * rows_dev + jnp.arange(rows_dev, dtype=jnp.int32)
    col_ids = jnp.arange(grid_width, dtype=jnp.int32)
    inside = (row_ids[None, :, None] < own_heights[:, None, None]) & (
        col_ids[None, None, :] < own_widths[:, None, None]
    )
    pix_mask = inside.astype(jnp.float32)[..., None]
    valid_count = jnp.sum((heights * widths).astype(jnp.float32))
    own_count = (own_heights * own_widths).astype(jnp.float32)
    masked_values = features * pix_mask.astype(jnp.bfloat16)
    flat_pix = masked_values.reshape(pixels, channel_total)
    point_conv = jnp.einsum("pc,fc->pf", flat_pix, w_point, preferred_element_type=jnp.float32)
    conv_list = [point_conv.reshape(count_k, rows_dev, grid_width, local_output)]
    for dilation_index, dilation_factor in enumerate(dilation_factors):
        dilation_rate = rows_dev * dilation_factor
        running_total = tap_partials(masked_values, atrous_weight[dilation_index, 1], dilation_rate)
        for row_offset_tap in (0, 2):
            shift_amount = (1 - row_offset_tap) * dilation_factor
            keep_rows = source_inside(block_id, shift_amount)
            received_part = move_features(masked_values, shift_amount) * keep_rows.astype(
                jnp.bfloat16
            )
            running_total = running_total + tap_partials(
                received_part, atrous_weight[dilation_index, row_offset_tap], dilation_rate
            )
        conv_list.append(running_total)
    conv_out = jnp.stack(conv_list)
    stat_sum, stat_square = lax.psum(
        (
            jnp.sum(conv_out * pix_mask, axis=(1, 2, 3)),
            jnp.sum(conv_out * conv_out * pix_mask, axis=(1, 2, 3)),
        ),
        "sp",
    )
    branch_mean = stat_sum / valid_count
    branch_inv = lax.rsqrt(stat_square / valid_count - branch_mean * branch_mean + epsilon)
    normed = (conv_out - branch_mean[:, None, None, None, :]) * branch_inv[:, None, None, None, :]
    pre_act = bn_gains[:4][:, None, None, None, :] * normed + bn_shifts[:4][:, None, None, None, :]
    branch_act = (pix_mask * jax.nn.silu(pre_act)).astype(jnp.bfloat16)
    own_sums = jnp.sum(masked_values, axis=(1, 2), dtype=jnp.float32)
    own_pooled = own_sums / own_count[:, None]
    pool_weight = w_pool.astype(jnp.float32)
    pooled = lax.psum(own_pooled[:, None, :] * group_onehot[None, :, None], "sp")
    projected = jnp.dot(
        pooled.reshape(images, channel_total), pool_weight.T, precision=highest_precision
    )
    pool_mean = jnp.mean(projected, axis=0)
    pool_inv = lax.rsqrt(jnp.mean(projected * projected, axis=0) - pool_mean * pool_mean + epsilon)
    pool_normed = (projected - pool_mean) * pool_inv
    pool_pre = bn_gains[4] * pool_normed + bn_shifts[4]
    pool_act = jax.nn.silu(pool_pre).astype(jnp.bfloat16)
    own_act = jnp.sum(
        pool_act.astype(jnp.float32).reshape(count_k, groups, local_output)
        * group_onehot[None, :, None],
        axis=1,
    )
    pool_pixels = (own_act[:, None, None, :] * pix_mask).astype(jnp.bfloat16)
    stacked = jnp.concatenate([branch_act, pool_pixels[None]], axis=0).reshape(
        5, pixels, local_output
    )
    partial_value = jnp.einsum("bpf,bfo->po", stacked, w_proj, preferred_element_type=jnp.float32)
    mixed_sum = lax.psum_scatter(
        partial_value.reshape(count_k, rows_dev, grid_width, full_out),
        "ch",
        scatter_dimension=3,
        tiled=True,
    )
    final_sum, final_square = lax.psum(
        (
            jnp.sum(mixed_sum * pix_mask, axis=(0, 1, 2)),
            jnp.sum(mixed_sum * mixed_sum * pix_mask, axis=(0, 1, 2)),
        ),
        "sp",
    )
    final_mean = final_sum / valid_count
    final_inv = lax.rsqrt(final_square / valid_count - final_mean * final_mean + epsilon)
    final_normed = (mixed_sum - final_mean) * final_inv
    final_pre = bn_gains[5] * final_normed + bn_shifts[5]
    output = (pix_mask * jax.nn.silu(final_pre)).astype(jnp.bfloat16)
    final_dt = pix_mask * own_out_grad.astype(jnp.float32) * silu_slope(final_pre)
    final_beta, final_gamma = lax.psum(
        (jnp.sum(final_dt, axis=(0, 1, 2)), jnp.sum(final_dt * final_normed, axis=(0, 1, 2))), "sp"
    )
    mixed_grad = (
        pix_mask
        * final_inv
        * bn_gains[5]
        * (final_dt - final_beta / valid_count - final_normed * final_gamma / valid_count)
    ).astype(jnp.bfloat16)
    full_grad = lax.all_gather(mixed_grad, "ch", axis=3, tiled=True).reshape(pixels, full_out)
    g_proj = jnp.einsum("bpf,po->bfo", stacked, full_grad, preferred_element_type=jnp.float32)
    act_grads = jnp.einsum(
        "po,bfo->bpf", full_grad, w_proj, preferred_element_type=jnp.float32
    ).reshape(5, count_k, rows_dev, grid_width, local_output)
    branch_dt = pix_mask * act_grads[:4] * silu_slope(pre_act)
    pool_own_grad = jnp.sum(act_grads[4] * pix_mask, axis=(1, 2))
    branch_beta, branch_gamma, pool_grad = lax.psum(
        (
            jnp.sum(branch_dt, axis=(1, 2, 3)),
            jnp.sum(branch_dt * normed, axis=(1, 2, 3)),
            pool_own_grad[:, None, :] * group_onehot[None, :, None],
        ),
        "sp",
    )
    convolution_gradients = (
        pix_mask
        * branch_inv[:, None, None, None, :]
        * bn_gains[:4][:, None, None, None, :]
        * (
            branch_dt
            - branch_beta[:, None, None, None, :] / valid_count
            - normed * branch_gamma[:, None, None, None, :] / valid_count
        )
    ).astype(jnp.bfloat16)
    pool_dt = pool_grad.reshape(images, local_output) * silu_slope(pool_pre)
    pool_beta = jnp.sum(pool_dt, axis=0)
    pool_gamma = jnp.sum(pool_dt * pool_normed, axis=0)
    proj_grad = (
        pool_inv * bn_gains[4] * (pool_dt - pool_beta / images - pool_normed * pool_gamma / images)
    )
    own_proj_grad = jnp.sum(
        proj_grad.reshape(count_k, groups, local_output) * group_onehot[None, :, None], axis=1
    )
    g_pool = jnp.einsum("kf,kc->fc", own_proj_grad, own_pooled, precision=highest_precision)
    pooled_grad = (
        jnp.einsum("kf,fc->kc", own_proj_grad, pool_weight, precision=highest_precision)
        / own_count[:, None]
    )
    point_grad = convolution_gradients[0].reshape(pixels, local_output)
    g_point = jnp.einsum("pf,pc->fc", point_grad, flat_pix, preferred_element_type=jnp.float32)
    input_term = jnp.einsum("pf,fc->pc", point_grad, w_point, preferred_element_type=jnp.float32)
    input_term = (
        input_term.reshape(count_k, rows_dev, grid_width, channel_total)
        + pooled_grad[:, None, None, :]
    )
    atrous_list = []
    for dilation_index, dilation_factor in enumerate(dilation_factors):
        dilation_rate = rows_dev * dilation_factor
        tap_list = []
        for row_offset_tap in range(3):
            shift_amount = (row_offset_tap - 1) * dilation_factor
            if shift_amount == 0:
                received_part = convolution_gradients[dilation_index + 1]
            else:
                received_part = shifted_gradients(
                    convolution_gradients[dilation_index + 1], shift_amount
                ) * source_inside(block_id, shift_amount).astype(jnp.bfloat16)
            spread = jnp.stack(
                [
                    shift_cols(received_part, dilation_rate),
                    received_part,
                    shift_cols(received_part, -dilation_rate),
                ],
                axis=3,
            ).reshape(pixels, 3 * local_output)
            tap_list.append(
                jnp.einsum(
                    "pt,pc->tc", spread, flat_pix, preferred_element_type=jnp.float32
                ).reshape(3, local_output, channel_total)
            )
            tap_weight_slice = atrous_weight[dilation_index, row_offset_tap].reshape(
                3 * local_output, channel_total
            )
            input_term = input_term + jnp.einsum(
                "pt,tc->pc", spread, tap_weight_slice, preferred_element_type=jnp.float32
            ).reshape(count_k, rows_dev, grid_width, channel_total)
        atrous_list.append(jnp.stack(tap_list))
    g_atrous = jnp.stack(atrous_list)
    in_grad = lax.psum_scatter(
        (input_term * pix_mask).astype(jnp.bfloat16), "ch", scatter_dimension=3, tiled=True
    )
    g_point, g_atrous, g_proj, g_pool = (
        lax.psum(g_point.astype(jnp.bfloat16), "sp").astype(jnp.float32),
        lax.psum(g_atrous.astype(jnp.bfloat16), "sp").astype(jnp.float32),
        lax.psum(g_proj.astype(jnp.bfloat16), "sp").astype(jnp.float32),
        lax.psum(g_pool.astype(jnp.bfloat16), "sp").astype(jnp.float32),
    )
    g_gains = jnp.concatenate([branch_gamma, pool_gamma[None], final_gamma[None]], axis=0)
    g_shifts = jnp.concatenate([branch_beta, pool_beta[None], final_beta[None]], axis=0)
    return (output, in_grad, g_point, g_atrous, g_pool, g_proj, g_gains, g_shifts)


def body(
    features, heights, widths, w_point, atrous_weight, w_pool, w_proj, bn_gains, bn_shifts, out_grad
):
    images, rows_dev, cols, C = features.shape
    L = w_point.shape[0]
    if lax.axis_size("sp") != BLOCKS or lax.axis_size("ch") != 4 or L != 64:
        return plain_body(
            features, heights, widths, w_point, atrous_weight, w_pool, w_proj, bn_gains, bn_shifts, out_grad
        )
    F = w_proj.shape[2]
    W = BRANCHES * L
    slabs = images * rows_dev
    cells = slabs * cols
    rates = tuple(rows_dev * f for f in dilation_factors)
    block_id = lax.axis_index("sp")
    own = lax.axis_index("ch")
    h, w = heights[:, 0], widths[:, 0]
    row_ids = block_id * rows_dev + jnp.arange(rows_dev, dtype=jnp.int32)
    lim = jnp.where(row_ids[None, :] < h[:, None], w[:, None], 0).reshape(slabs)
    own_count = (h * w).astype(f32)
    n = jnp.sum(own_count)
    x = features.reshape(cells, C)
    og = out_grad.reshape(cells, F)

    norms = jnp.concatenate([bn_gains, bn_shifts, jnp.zeros((4, L), f32)], axis=0)
    wp = w_proj.reshape(5 * L, F)
    norms_all = jnp.stack([norms] + [swap(norms, "ch", b) for b in (1, 2, 3)])
    wp_all = jnp.stack([wp] + [swap(wp, "ch", b) for b in (1, 2, 3)])
    wbranch_all, wpool_all = wp_all[:, :W], wp_all[:, W:]
    natural = (own ^ jnp.arange(4))[:, None] == jnp.arange(4)[None, :]
    final_par = jnp.sum(
        jnp.where(natural[:, :, None, None], norms_all[None, :, (5, 11), :], 0.0), axis=1
    )
    final_gain, final_shift = final_par[:, 0].reshape(F), final_par[:, 1].reshape(F)

    KT = 512
    steps = C // KT
    x_spec = pl.BlockSpec((cells, KT), lambda k: (0, k))
    side = pl.pallas_call(
        functools.partial(side_kernel, steps=steps, slabs=slabs, cols=cols, rates=rates),
        grid=(steps,),
        in_specs=[
            SMEM,
            x_spec,
            pl.BlockSpec((3, 1, 3, L, KT), lambda k: (0, 0, 0, 0, k)),
            pl.BlockSpec((3, 1, 3, L, KT), lambda k: (0, 2, 0, 0, k)),
        ],
        out_specs=[pl.BlockSpec((cells // 2, 2 * L), lambda k: (0, 0))] * 6,
        out_shape=[jax.ShapeDtypeStruct((cells // 2, 2 * L), bf16)] * 6,
        scratch_shapes=[pltpu.VMEM((18 * L, KT), bf16), pltpu.VMEM((cells, 18 * L), f32)],
        compiler_params=params(),
        cost_estimate=cost(2 * cells * C * 18 * L, 10e6),
        name="side_taps",
    )(lim, x, atrous_weight, atrous_weight)
    halo = [from_behind(side[i], "sp", (1 - 2 * (i % 2)) * dilation_factors[i // 2]) for i in range(6)]
    centre, sums = pl.pallas_call(
        functools.partial(centre_kernel, steps=steps, slabs=slabs, cols=cols, rates=rates, images=images),
        grid=(steps,),
        in_specs=[
            SMEM,
            x_spec,
            pl.BlockSpec((3, 1, 3, L, KT), lambda k: (0, 1, 0, 0, k)),
            pl.BlockSpec((L, KT), lambda k: (0, k)),
        ],
        out_specs=[pl.BlockSpec((cells, W), lambda k: (0, 0)), pl.BlockSpec((8, KT), lambda k: (0, k))],
        out_shape=[jax.ShapeDtypeStruct((cells, W), f32), jax.ShapeDtypeStruct((8, C), f32)],
        scratch_shapes=[pltpu.VMEM((10 * L, KT), bf16), pltpu.VMEM((cells, 10 * L), f32)],
        compiler_params=params(),
        cost_estimate=cost(2 * cells * C * 10 * L, 8e6),
        name="centre_taps",
    )(lim, x, atrous_weight, w_point)
    own_pooled = sums[:images] / own_count[:, None]
    proj_part = lax.dot_general(own_pooled, w_pool.astype(f32), NT, precision=highest_precision)

    conv, conv_send, stat = pl.pallas_call(
        functools.partial(combine_kernel, slabs=slabs, cols=cols),
        in_specs=[SMEM] + [VMEM] * 7,
        out_specs=[VMEM] * 3,
        out_shape=[
            jax.ShapeDtypeStruct((cells, W), f32),
            jax.ShapeDtypeStruct((cells, W), bf16),
            jax.ShapeDtypeStruct((8, W), f32),
        ],
        compiler_params=params(),
        cost_estimate=cost(2e6, 4e6),
        name="combine_taps",
    )(lim, centre, *halo)
    conv_y = swap(conv_send, "ch", 2)
    conv_core = swap(conv_send, "ch", 1)
    conv_diag = swap(conv_y, "ch", 1)
    tile = jnp.concatenate([stat[:4], jnp.pad(proj_part, ((0, 0), (0, W - L)))], axis=0)
    tile = sum_over_sp(tile)
    tile = jnp.concatenate([tile[:2], stat[2:3], tile[3:]], axis=0)
    tiles = jnp.stack([tile] + [swap(tile, "ch", b) for b in (1, 2, 3)])
    mean = tiles[:, 0] / n
    rstd = lax.rsqrt(tiles[:, 1] / n - mean * mean + epsilon)
    branch_stat = jnp.stack([mean, rstd, tiles[:, 2]], axis=1)
    branch_par = jnp.stack([norms_all[:, :4].reshape(4, W), norms_all[:, 6:10].reshape(4, W)], axis=1)
    projected = tiles[:, 4 : 4 + images, :L]
    pool_mean = jnp.mean(projected, axis=1, keepdims=True)
    pool_rstd = lax.rsqrt(
        jnp.mean(projected * projected, axis=1, keepdims=True) - pool_mean * pool_mean + epsilon
    )
    pool_normed = (projected - pool_mean) * pool_rstd
    pool_pre = norms_all[:, 4:5] * pool_normed + norms_all[:, 10:11]
    pool_act = jax.nn.silu(pool_pre).astype(bf16)
    pool_in = jnp.pad(pool_act, ((0, 0), (0, 8 - images), (0, 0)))

    mixed, act, mixed_stat = pl.pallas_call(
        functools.partial(mix_kernel, slabs=slabs, cols=cols, images=images),
        in_specs=[SMEM] + [VMEM] * 9,
        out_specs=[VMEM] * 3,
        out_shape=[
            jax.ShapeDtypeStruct((cells, F), f32),
            jax.ShapeDtypeStruct((cells, W), bf16),
            jax.ShapeDtypeStruct((8, F), f32),
        ],
        scratch_shapes=[pltpu.VMEM((cells, W), bf16)],
        compiler_params=params(),
        cost_estimate=cost(2 * cells * 4 * W * F, 6e6),
        name="mix_branches",
    )(lim, conv, conv_core, conv_y, conv_diag, branch_stat, branch_par, wbranch_all, pool_in, wpool_all)
    total = sum_over_sp(mixed_stat)
    fmean = total[0] / n
    frstd = lax.rsqrt(total[1] / n - fmean * fmean + epsilon)
    final_stat = jnp.stack([fmean, frstd, final_gain, final_shift])
    out_all, fdt, fsums = pl.pallas_call(
        functools.partial(final_kernel, slabs=slabs, cols=cols),
        in_specs=[SMEM] + [VMEM] * 3,
        out_specs=[VMEM] * 3,
        out_shape=[
            jax.ShapeDtypeStruct((cells, F), bf16),
            jax.ShapeDtypeStruct((cells, F), f32),
            jax.ShapeDtypeStruct((8, F), f32),
        ],
        compiler_params=params(),
        cost_estimate=cost(2e6, 4e6),
        name="final_norm",
    )(lim, mixed, og, final_stat)
    ftotal = sum_over_sp(fsums)
    final_beta, final_gamma = ftotal[0], ftotal[1]
    fgrad_stat = jnp.stack([fmean, frstd, frstd * final_gain, final_beta / n, final_gamma / n])
    own_gain, own_shift = branch_par[0, 0], branch_par[0, 1]
    own_mean, own_rstd = branch_stat[0, 0], branch_stat[0, 1]
    dt, gproj, image_sums, bsums = pl.pallas_call(
        functools.partial(branch_kernel, slabs=slabs, cols=cols, images=images),
        in_specs=[SMEM] + [VMEM] * 7,
        out_specs=[VMEM] * 4,
        out_shape=[
            jax.ShapeDtypeStruct((cells, W), f32),
            jax.ShapeDtypeStruct((W, F), f32),
            jax.ShapeDtypeStruct((8, F), f32),
            jax.ShapeDtypeStruct((8, W), f32),
        ],
        scratch_shapes=[pltpu.VMEM((cells, F), bf16)],
        compiler_params=params(),
        cost_estimate=cost(4 * cells * W * F, 8e6),
        name="branch_grads",
    )(
        lim, mixed, fdt, fgrad_stat, conv, act,
        jnp.stack([own_mean, own_rstd, own_gain, own_shift]), wp[:W],
    )
    image_sums = image_sums[:images]
    pool_part = lax.dot_general(image_sums, w_proj[4].astype(f32), NT, precision=highest_precision)
    gproj_pool = lax.dot_general(pool_act[0].astype(f32), image_sums, TN, precision=highest_precision)
    btile = sum_over_sp(
        jnp.concatenate([bsums[:4], jnp.pad(pool_part, ((0, 0), (0, W - L)))], axis=0)
    )
    branch_beta, branch_gamma = btile[0], btile[1]
    cg = pl.pallas_call(
        functools.partial(grad_kernel, slabs=slabs, cols=cols),
        in_specs=[SMEM] + [VMEM] * 3,
        out_specs=VMEM,
        out_shape=jax.ShapeDtypeStruct((cells, W), bf16),
        compiler_params=params(),
        cost_estimate=cost(2e6, 4e6),
        name="conv_grads",
    )(lim, dt, conv, jnp.stack([own_mean, own_rstd, own_rstd * own_gain, branch_beta / n, branch_gamma / n]))
    pool_dt = btile[4 : 4 + images, :L] * silu_slope(pool_pre[0])
    pool_beta = jnp.sum(pool_dt, axis=0)
    pool_gamma = jnp.sum(pool_dt * pool_normed[0], axis=0)
    proj_grad = (
        pool_rstd[0] * bn_gains[4] * (pool_dt - pool_beta / images - pool_normed[0] * pool_gamma / images)
    )
    g_gains = jnp.concatenate([branch_gamma.reshape(4, L), pool_gamma[None],
        lax.dynamic_slice_in_dim(final_gamma, own * L, L)[None]], axis=0)
    g_shifts = jnp.concatenate([branch_beta.reshape(4, L), pool_beta[None],
        lax.dynamic_slice_in_dim(final_beta, own * L, L)[None]], axis=0)
    output = lax.dynamic_slice_in_dim(out_all, own * L, L, 1).reshape(images, rows_dev, cols, L)
    g_proj = jnp.concatenate([gproj.reshape(4, L, F), gproj_pool[None]], axis=0)
    pooled_grad = (
        jnp.einsum("kf,fc->kc", proj_grad, w_pool.astype(f32), precision=highest_precision)
        / own_count[:, None]
    )
    g_pool = jnp.einsum("kf,kc->fc", proj_grad, own_pooled, precision=highest_precision)
    col_ids = jnp.arange(cols, dtype=jnp.int32)
    pix_mask = (col_ids[None, :] < lim[:, None]).astype(f32).reshape(images, rows_dev, cols, 1)
    flat_pix = (features * pix_mask.astype(bf16)).reshape(cells, C)
    grads = [cg[:, i * L : (i + 1) * L].reshape(images, rows_dev, cols, L) for i in range(4)]
    point_grad = grads[0].reshape(cells, L)
    g_point = jnp.einsum("pf,pc->fc", point_grad, flat_pix, preferred_element_type=f32)
    input_term = jnp.einsum("pf,fc->pc", point_grad, w_point, preferred_element_type=f32)
    input_term = input_term.reshape(images, rows_dev, cols, C) + pooled_grad[:, None, None, :]
    atrous_list = []
    for j, factor in enumerate(dilation_factors):
        tap_list = []
        for u in range(3):
            g = grads[j + 1] if u == 1 else from_behind(grads[j + 1], "sp", (u - 1) * factor)
            spread = jnp.stack(
                [shift_cols(g, rates[j]), g, shift_cols(g, -rates[j])], axis=3
            ).reshape(cells, 3 * L)
            tap_list.append(
                jnp.einsum("pt,pc->tc", spread, flat_pix, preferred_element_type=f32).reshape(3, L, C)
            )
            input_term = input_term + jnp.einsum(
                "pt,tc->pc", spread, atrous_weight[j, u].reshape(3 * L, C), preferred_element_type=f32
            ).reshape(images, rows_dev, cols, C)
        atrous_list.append(jnp.stack(tap_list))
    g_atrous = jnp.stack(atrous_list)
    in_grad = lax.psum_scatter(
        (input_term * pix_mask).astype(bf16), "ch", scatter_dimension=3, tiled=True
    )
    g_point, g_atrous, g_proj, g_pool = (
        lax.psum(t.astype(bf16), "sp").astype(f32) for t in (g_point, g_atrous, g_proj, g_pool)
    )
    return (output, in_grad, g_point, g_atrous, g_pool, g_proj, g_gains, g_shifts)


def solution(mesh):
    placed = (
        P(None, "sp", None, None),
        P(),
        P(),
        P("ch", None),
        P(None, None, None, "ch", None),
        P("ch", None),
        P(None, "ch", None),
        P(None, "ch"),
        P(None, "ch"),
        P(None, "sp", None, None),
    )
    return jax.shard_map(
        body,
        mesh=mesh,
        in_specs=placed,
        out_specs=(
            P(None, "sp", None, "ch"),
            P(None, "sp", None, "ch"),
            P("ch", None),
            P(None, None, None, "ch", None),
            P("ch", None),
            P(None, "ch", None),
            P(None, "ch"),
            P(None, "ch"),
        ),
        check_vma=False,
    )
```

```python
import functools

import jax
import jax.numpy as jnp
from jax import lax
from jax.experimental import pallas as pl
from jax.experimental.pallas import tpu as pltpu
from jax.sharding import PartitionSpec as P

BLOCKS = 8
BRANCHES = 4
epsilon = 1e-05
dilation_factors = (1, 2, 3)
highest_precision = lax.Precision.HIGHEST
f32 = jnp.float32
bf16 = jnp.bfloat16
MIB = 1 << 20
VMEM = pl.BlockSpec(memory_space=pltpu.VMEM)
SMEM = pl.BlockSpec(memory_space=pltpu.SMEM)
NT = (((1,), (1,)), ((), ()))
NN = (((1,), (0,)), ((), ()))
TN = (((0,), (0,)), ((), ()))


def dot(a, b, dims):
    return lax.dot_general(a, b, dims, preferred_element_type=f32)


def params(mib=60, **kw):
    return pltpu.CompilerParams(vmem_limit_bytes=mib * MIB, **kw)


def cost(flops, nbytes):
    return pl.CostEstimate(flops=int(flops), bytes_accessed=int(nbytes), transcendentals=0)


def cell_mask(lim_ref, slabs, cols, width):
    col = lax.broadcasted_iota(jnp.int32, (cols, width), 0)
    return jnp.concatenate([(col < lim_ref[i]).astype(f32) for i in range(slabs)], axis=0)


def column_ids(slabs, cols, width):
    return lax.broadcasted_iota(jnp.int32, (slabs, cols, width), 1).reshape(slabs * cols, width)


def from_left(a, d, col):
    return jnp.where(col >= d, pltpu.roll(a, d, 0), 0.0)


def from_right(a, d, col, cols):
    return jnp.where(col < cols - d, pltpu.roll(a, a.shape[0] - d, 0), 0.0)


def silu_parts(t):
    s = 1.0 / (1.0 + jnp.exp(-t))
    return s, t * s


def slope(t, s):
    return s * (1.0 + t * (1.0 - s))


def column_sums(*rows):
    sums = [jnp.sum(r, axis=0, keepdims=True) for r in rows]
    width = sums[0].shape[1]
    return jnp.concatenate(sums + [jnp.zeros((8 - len(sums), width), f32)], axis=0)


def side_kernel(lim_ref, low_ref, x_ref, *refs, steps, slabs, cols, rates):
    n_rates = len(rates)
    weights, outs, (wcat, acc) = refs[: 2 * n_rates], refs[2 * n_rates : 4 * n_rates], refs[4 * n_rates :]
    k = pl.program_id(0)
    L = weights[0].shape[3]
    for j in range(n_rates):
        for v in range(3):
            t = (j * 3 + v) * 2 * L
            wcat[t : t + L] = weights[2 * j][0, 0, v]
            wcat[t + L : t + 2 * L] = weights[2 * j + 1][0, 0, v]

    @pl.when(k == 0)
    def _():
        acc[...] = jnp.zeros_like(acc)

    x = x_ref[...]
    total = 6 * n_rates * L
    for n in range(0, total, 256):
        e = min(n + 256, total)
        acc[:, n:e] += dot(x, wcat[n:e], NT)

    @pl.when(k == steps - 1)
    def _():
        cells = slabs * cols
        half = cells // 2
        mask = cell_mask(lim_ref, slabs, cols, 2 * L)
        col = column_ids(slabs, cols, 2 * L)
        low = lax.broadcasted_iota(jnp.int32, (half, 2 * L), 1) < L
        for j in range(n_rates):
            a = [acc[:, (j * 3 + v) * 2 * L : (j * 3 + v + 1) * 2 * L] * mask for v in range(3)]
            s = a[1] + from_left(a[0], rates[j], col) + from_right(a[2], rates[j], col, cols)
            top, bottom = s[:half], s[half:]
            up = jnp.where(low, top, pltpu.roll(bottom, L, 1))
            down = jnp.where(low, pltpu.roll(top, L, 1), bottom)
            first = low_ref[j] == 1
            outs[2 * j][...] = jnp.where(first, up, down).astype(bf16)
            outs[2 * j + 1][...] = jnp.where(first, down, up).astype(bf16)


def centre_kernel(
    lim_ref, x_ref, wc_ref, wpoint_ref, out_ref, sums_ref, wcat, acc, *, steps, slabs, cols, rates, images
):
    k = pl.program_id(0)
    L = wpoint_ref.shape[0]
    order = [None, (0, 1), (1, 1), (2, 1), (1, 0), (2, 0), (1, 2), (2, 2), (0, 0), (0, 2)]
    for i, tap in enumerate(order):
        wcat[i * L : (i + 1) * L] = wpoint_ref[...] if tap is None else wc_ref[tap[0], 0, tap[1]]

    @pl.when(k == 0)
    def _():
        acc[...] = jnp.zeros_like(acc)

    x = x_ref[...]
    total = 10 * L
    for n in range(0, total, 256):
        e = min(n + 256, total)
        acc[:, n:e] += dot(x, wcat[n:e], NT)

    width = x_ref.shape[1]
    cid = lax.broadcasted_iota(jnp.int32, (cols, width), 0)
    per = slabs // images
    sums = []
    for image in range(images):
        part = jnp.zeros((cols, width), f32)
        for i in range(image * per, (image + 1) * per):
            part += jnp.where(cid < lim_ref[i], x_ref[i * cols : (i + 1) * cols].astype(f32), 0.0)
        sums.append(jnp.sum(part, axis=0, keepdims=True))
    sums_ref[...] = jnp.concatenate(sums + [jnp.zeros((8 - images, width), f32)], axis=0)

    @pl.when(k == steps - 1)
    def _():
        cells = slabs * cols
        mask = cell_mask(lim_ref, slabs, cols, 2 * L)
        col = column_ids(slabs, cols, 2 * L)
        low = lax.broadcasted_iota(jnp.int32, (cells, 2 * L), 1) < L
        b = [acc[:, i * 2 * L : (i + 1) * 2 * L] * mask for i in range(5)]
        d0, d1, d2 = rates
        t = jnp.where(low, from_left(b[4], d0, col), from_right(b[4], d0, col, cols))
        out_ref[:, : 2 * L] = b[0] + jnp.where(low, 0.0, t + pltpu.roll(t, L, 1))
        out_ref[:, 2 * L :] = (
            b[1]
            + jnp.where(low, from_left(b[2], d1, col), from_left(b[2], d2, col))
            + jnp.where(low, from_right(b[3], d1, col, cols), from_right(b[3], d2, col, cols))
        )


def combine_kernel(lim_ref, centre_ref, *refs, slabs, cols):
    halo, (conv_ref, send_ref, stat_ref) = refs[:6], refs[6:]
    cells = slabs * cols
    half = cells // 2
    W = centre_ref.shape[1]
    L = W // 4
    h = [halo[2 * j][...].astype(f32) + halo[2 * j + 1][...].astype(f32) for j in range(3)]
    turned = [pltpu.roll(a, L, 1) for a in h]
    low = lax.broadcasted_iota(jnp.int32, (cells, 2 * L), 1) < L
    h0 = jnp.concatenate([turned[0], h[0]], axis=0)
    h1 = jnp.concatenate([h[1], turned[1]], axis=0)
    h2 = jnp.concatenate([turned[2], h[2]], axis=0)
    left = centre_ref[:, : 2 * L] + jnp.where(low, 0.0, h0)
    right = centre_ref[:, 2 * L :] + jnp.where(low, h1, h2)
    conv_ref[:, : 2 * L] = left
    conv_ref[:, 2 * L :] = right
    mask = cell_mask(lim_ref, slabs, cols, 2 * L)
    own = lim_ref[0]
    for i in range(1, slabs):
        own = own + lim_ref[i]
    own = jnp.maximum(own, 1).astype(f32)
    for lo, part in ((0, left), (2 * L, right)):
        s = jnp.sum(part * mask, axis=0, keepdims=True)
        q = jnp.sum(part * part * mask, axis=0, keepdims=True)
        local = s / own
        send_ref[:, lo : lo + 2 * L] = (part - local).astype(bf16)
        stat_ref[:, lo : lo + 2 * L] = jnp.concatenate([s, q, local, jnp.zeros((5, 2 * L), f32)], axis=0)


def mix_kernel(
    lim_ref, conv_ref, c1_ref, c2_ref, c3_ref, stat_ref, gain_ref, wbranch_ref, pool_ref, wpool_ref,
    mixed_ref, act_ref, sums_ref, scratch, *, slabs, cols, images
):
    cells = slabs * cols
    per = slabs // images
    for d, ref in enumerate((conv_ref, c1_ref, c2_ref, c3_ref)):
        mean, rstd, local = stat_ref[d, 0:1], stat_ref[d, 1:2], stat_ref[d, 2:3]
        offset = mean if d == 0 else mean - local
        scale = rstd * gain_ref[d, 0:1]
        shift = gain_ref[d, 1:2]
        dest = act_ref if d == 0 else scratch
        width = ref.shape[1]
        cid = lax.broadcasted_iota(jnp.int32, (cols, width), 0)
        for i in range(slabs):
            rows = slice(i * cols, (i + 1) * cols)
            pre = (ref[rows].astype(f32) - offset) * scale + shift
            _, act = silu_parts(pre)
            dest[rows] = jnp.where(cid < lim_ref[i], act, 0.0).astype(bf16)
        part = dot(dest[...], wbranch_ref[d], NN)
        if d == 0:
            mixed_ref[...] = part
        else:
            mixed_ref[...] += part
    pooled = dot(pool_ref[0], wpool_ref[0], NN)
    for d in range(1, 4):
        pooled += dot(pool_ref[d], wpool_ref[d], NN)
    F = mixed_ref.shape[1]
    cid = lax.broadcasted_iota(jnp.int32, (cols, F), 0)
    s = jnp.zeros((cols, F), f32)
    q = jnp.zeros((cols, F), f32)
    for i in range(slabs):
        rows = slice(i * cols, (i + 1) * cols)
        image = i // per
        value = mixed_ref[rows] + jnp.where(cid < lim_ref[i], pooled[image : image + 1], 0.0)
        mixed_ref[rows] = value
        s += value
        q += value * value
    sums_ref[...] = column_sums(s, q)


def final_kernel(lim_ref, mixed_ref, grad_ref, stat_ref, out_ref, dt_ref, sums_ref, *, slabs, cols):
    F = mixed_ref.shape[1]
    mean, rstd, gain, shift = (stat_ref[i : i + 1] for i in range(4))
    cid = lax.broadcasted_iota(jnp.int32, (cols, F), 0)
    s = jnp.zeros((cols, F), f32)
    q = jnp.zeros((cols, F), f32)
    for i in range(slabs):
        rows = slice(i * cols, (i + 1) * cols)
        valid = cid < lim_ref[i]
        normed = (mixed_ref[rows] - mean) * rstd
        pre = gain * normed + shift
        sig, act = silu_parts(pre)
        out_ref[rows] = jnp.where(valid, act, 0.0).astype(bf16)
        dt = jnp.where(valid, grad_ref[rows].astype(f32) * slope(pre, sig), 0.0)
        dt_ref[rows] = dt
        s += dt
        q += dt * normed
    sums_ref[...] = column_sums(s, q)


def branch_kernel(
    lim_ref, mixed_ref, fdt_ref, fstat_ref, conv_ref, act_ref, stat_ref, wbranch_ref,
    dt_ref, gproj_ref, image_ref, sums_ref, grad, *, slabs, cols, images
):
    F = mixed_ref.shape[1]
    W = conv_ref.shape[1]
    per = slabs // images
    mean, rstd, scale, beta, gamma = (fstat_ref[i : i + 1] for i in range(5))
    cid = lax.broadcasted_iota(jnp.int32, (cols, F), 0)
    image_sums = []
    for image in range(images):
        total = jnp.zeros((cols, F), f32)
        for i in range(image * per, (image + 1) * per):
            rows = slice(i * cols, (i + 1) * cols)
            normed = (mixed_ref[rows] - mean) * rstd
            g = jnp.where(cid < lim_ref[i], scale * (fdt_ref[rows] - beta - normed * gamma), 0.0)
            g = g.astype(bf16)
            grad[rows] = g
            total += g.astype(f32)
        image_sums.append(jnp.sum(total, axis=0, keepdims=True))
    image_ref[...] = jnp.concatenate(image_sums + [jnp.zeros((8 - images, F), f32)], axis=0)
    dt_ref[...] = dot(grad[...], wbranch_ref[...], NT)
    gproj_ref[...] = dot(act_ref[...], grad[...], TN)
    bmean, brstd, bgain, bshift = (stat_ref[i : i + 1] for i in range(4))
    cid = lax.broadcasted_iota(jnp.int32, (cols, W), 0)
    s = jnp.zeros((cols, W), f32)
    q = jnp.zeros((cols, W), f32)
    for i in range(slabs):
        rows = slice(i * cols, (i + 1) * cols)
        normed = (conv_ref[rows] - bmean) * brstd
        pre = bgain * normed + bshift
        sig, _ = silu_parts(pre)
        dt = jnp.where(cid < lim_ref[i], dt_ref[rows] * slope(pre, sig), 0.0)
        dt_ref[rows] = dt
        s += dt
        q += dt * normed
    sums_ref[...] = column_sums(s, q)


def grad_kernel(lim_ref, dt_ref, conv_ref, stat_ref, cg_ref, scratch, *, slabs, cols):
    W = conv_ref.shape[1]
    mean, rstd, scale, beta, gamma = (stat_ref[i : i + 1] for i in range(5))
    cid = lax.broadcasted_iota(jnp.int32, (cols, W), 0)
    for i in range(slabs):
        rows = slice(i * cols, (i + 1) * cols)
        normed = (conv_ref[rows] - mean) * rstd
        g = scale * (dt_ref[rows] - beta - normed * gamma)
        scratch[rows] = jnp.where(cid < lim_ref[i], g, 0.0)
    cg_ref[...] = scratch[...].T.astype(bf16)


def shifted(f, v, d, col, cols):
    if v == 1:
        return f
    if v == 2:
        return jnp.where(col >= d, pltpu.roll(f, d, 1), 0.0)
    return jnp.where(col < cols - d, pltpu.roll(f, f.shape[1] - d, 1), 0.0)


def expand_kernel(col_ref, cg_ref, out_ref, *, cols, rates):
    L = cg_ref.shape[0] // 4
    for j in range(3):
        raw = cg_ref[(j + 1) * L : (j + 2) * L]
        f = raw.astype(f32)
        col = jnp.broadcast_to(col_ref[0:1], f.shape)
        base = 3 * j * L
        out_ref[base : base + L] = shifted(f, 0, rates[j], col, cols).astype(bf16)
        out_ref[base + L : base + 2 * L] = raw
        out_ref[base + 2 * L : base + 3 * L] = shifted(f, 2, rates[j], col, cols).astype(bf16)
    out_ref[9 * L :] = cg_ref[:L]


def fetch_blocks(pos, blocks, dest, sems, lanes=False):
    copies = []
    for d, ref in enumerate(blocks):
        place = pos ^ d
        if lanes:
            cells = ref.shape[1]
            spot = dest.at[:, pl.ds(pl.multiple_of(place * cells, 128), cells)]
        else:
            spot = dest.at[place]
        copies.append(pltpu.make_async_copy(ref, spot, sems.at[d]))
    for c in copies:
        c.start()
    return copies


def tap_products(store, taps, x_rows, L):
    cells = taps.shape[1] // BLOCKS
    own_row = dot(taps[...], x_rows(0, BLOCKS), NN)
    for j in range(3):
        lo = (j * 3 + 1) * 3 * L
        store(lo, own_row[3 * j * L : 3 * (j + 1) * L])
    store(27 * L, own_row[9 * L :])
    for j in range(3):
        rows = slice(3 * j * L, 3 * (j + 1) * L)
        span = (BLOCKS - 1 - j) * cells
        far = (j + 1) * cells
        store(j * 9 * L, dot(taps[rows, far:], x_rows(0, BLOCKS - 1 - j), NN))
        store((j * 3 + 2) * 3 * L, dot(taps[rows, :span], x_rows(j + 1, BLOCKS), NN))


def narrow_kernel(pos_ref, *refs, parts):
    blocks, (x_ref, out_ref, taps, x, sems, xsems) = refs[:BLOCKS], refs[BLOCKS:]
    pos, ch = pos_ref[0], pos_ref[2]
    L = taps.shape[0] // 10
    cells = taps.shape[1] // BLOCKS
    rows = x_ref.shape[2]
    copies = fetch_blocks(pos, blocks, taps, sems, lanes=True)
    for e in range(parts):
        for d in range(BLOCKS):
            place = pl.ds(pl.multiple_of((pos ^ d) * cells + (ch ^ e) * rows, 16), rows)
            c = pltpu.make_async_copy(x_ref.at[e, d], x.at[place], xsems.at[e, d])
            c.start()
            copies.append(c)
    for c in copies:
        c.wait()

    def store(lo, value):
        out_ref[lo : lo + value.shape[0]] = value.astype(bf16)

    tap_products(store, taps, lambda lo, hi: x[lo * cells : hi * cells], L)


def wide_kernel(pos_ref, x_ref, *refs):
    blocks, (acc_ref, point_ref, taps, sems) = refs[:BLOCKS], refs[BLOCKS:]
    L = point_ref.shape[0]

    @pl.when(pl.program_id(0) == 0)
    def _():
        for c in fetch_blocks(pos_ref[0], blocks, taps, sems, lanes=True):
            c.wait()

    def store(lo, value):
        if lo < 27 * L:
            acc_ref[lo : lo + value.shape[0]] = value
        else:
            point_ref[...] = value

    w = x_ref.shape[3]
    tap_products(store, taps, lambda lo, hi: x_ref[lo:hi, 0].reshape(-1, w), L)


def widen_kernel(in_ref, pin_ref, keep_ref, pkeep_ref, out_ref, pout_ref):
    w = in_ref.shape[2]
    for s in range(BLOCKS):
        out_ref[:, s * w : (s + 1) * w] = in_ref[s].astype(f32)
        pout_ref[:, s * w : (s + 1) * w] = pin_ref[s].astype(f32)


def input_grad_kernel(pos_ref, lim_ref, col_ref, w_ref, wp_ref, pool_ref, *refs, slabs, cols, rates, images):
    blocks, (out_ref, cg, lhs, rhs, sems) = refs[:BLOCKS], refs[BLOCKS:]
    L = wp_ref.shape[0]
    s = pos_ref[0]

    @pl.when(pl.program_id(0) == 0)
    def _():
        for c in fetch_blocks(s, blocks, cg, sems):
            c.wait()
        pieces = []
        order = [(j, u, v) for j in range(3) for u in range(3) for v in range(3)] + [None]
        for i, tap in enumerate(order):
            if tap is None:
                pieces.append(cg[s, 0:L].astype(f32))
            else:
                j, u, v = tap
                b = s - (u - 1) * (j + 1)
                inside = ((b >= 0) & (b < BLOCKS)).astype(f32)
                f = cg[jnp.clip(b, 0, BLOCKS - 1), (j + 1) * L : (j + 2) * L].astype(f32) * inside
                col = jnp.broadcast_to(col_ref[0:1], f.shape)
                pieces.append(shifted(f, v, rates[j], col, cols))
            if i % 4 == 3:
                lhs[:, (i - 3) * L : (i + 1) * L] = jnp.concatenate(pieces, axis=0).T.astype(bf16)
                pieces = []

    rhs[: 27 * L] = w_ref[...]
    rhs[27 * L :] = wp_ref[...]
    width = out_ref.shape[2]
    per = slabs // images
    cid = lax.broadcasted_iota(jnp.int32, (cols, 256), 0)
    for n in range(0, width, 256):
        part = dot(lhs[...], rhs[:, n : n + 256], NN)
        for i in range(slabs):
            value = part[i * cols : (i + 1) * cols] + pool_ref[i // per : i // per + 1, n : n + 256]
            out_ref[0, i * cols : (i + 1) * cols, n : n + 256] = jnp.where(cid < lim_ref[i], value, 0.0).astype(bf16)


def grouped(pairs, size):
    return [(g * BLOCKS + a, g * BLOCKS + b) for g in range(size // BLOCKS) for a, b in pairs]


def neighbours(first, second, axis, distance):
    size = lax.axis_size(axis)
    rounds = []
    for parity, block in ((0, first), (1, second)):
        lows = [a for a in range(BLOCKS - distance) if (a // distance) % 2 == parity]
        pairs = [(a, a + distance) for a in lows] + [(a + distance, a) for a in lows]
        rounds.append(lax.ppermute(block, axis, grouped(pairs, size)))
    return rounds


def swap(block, axis, bits):
    return lax.ppermute(block, axis, [(i, i ^ bits) for i in range(lax.axis_size(axis))])


def sum_over_sp(x):
    x = x + swap(x, "sp", 1)
    parts = [swap(x, "sp", b) for b in (2, 4, 6)]
    return (x + parts[0]) + (parts[1] + parts[2])


def swaps_over_sp(x):
    blocks = [x, None] + [swap(x, "sp", b) if b % 2 == 0 else None for b in range(2, BLOCKS)]
    for b in range(1, BLOCKS, 2):
        blocks[b] = swap(blocks[b - 1], "sp", 1)
    return blocks


def after(x, *others):
    return lax.optimization_barrier((x,) + others)[0]


def thirds(x):
    hi = lax.reduce_precision(x, 8, 7)
    mid = lax.reduce_precision(x - hi, 8, 7)
    return jnp.stack([hi, mid, x - hi - mid]).astype(bf16)


def sum_over_sp_bf16(x):
    x = x.astype(bf16)
    x = (x.astype(f32) + swap(x, "sp", 1).astype(f32)).astype(bf16)
    parts = [swap(x, "sp", b).astype(f32) for b in (2, 4, 6)]
    return (x.astype(f32) + parts[0]) + (parts[1] + parts[2])


def plain_from_behind(block, axis, distance):
    devices = range(lax.axis_size(axis))
    route = [(i - distance, i) for i in devices if i - distance in devices]
    return lax.ppermute(block, axis, route)


def shift_cols(values, offset):
    margin = abs(offset)
    padded = jnp.pad(values, ((0, 0), (0, 0), (margin, margin), (0, 0)))
    return lax.slice_in_dim(padded, margin + offset, margin + offset + values.shape[2], axis=2)


def silu_slope(pre_act):
    sigmoid_val = jax.nn.sigmoid(pre_act)
    return sigmoid_val * (1.0 + pre_act * (1.0 - sigmoid_val))


def source_inside(block_id, shift_amount):
    source = block_id - shift_amount
    return (source >= 0) & (source < BLOCKS)


def move_features(values, shift_amount):
    return plain_from_behind(values, "sp", shift_amount)


def shifted_gradients(values, shift_amount):
    return plain_from_behind(values, "sp", shift_amount)


def tap_partials(source, weight_taps, dilation_rate):
    count_k, rows_dev, grid_width, channel_total = source.shape
    local_output = weight_taps.shape[1]
    products = jnp.einsum(
        "pc,tc->pt",
        source.reshape(-1, channel_total),
        weight_taps.reshape(3 * local_output, channel_total),
        preferred_element_type=jnp.float32,
    ).reshape(count_k, rows_dev, grid_width, 3, local_output)
    return (
        shift_cols(products[:, :, :, 0, :], -dilation_rate)
        + products[:, :, :, 1, :]
        + shift_cols(products[:, :, :, 2, :], dilation_rate)
    )


def plain_body(
    features, heights, widths, w_point, atrous_weight, w_pool, w_proj, bn_gains, bn_shifts, out_grad
):
    count_k, rows_dev, grid_width, channel_total = features.shape
    local_output = w_point.shape[0]
    full_out = w_proj.shape[2]
    groups = heights.shape[1]
    images = count_k * groups
    pixels = count_k * rows_dev * grid_width
    position = lax.axis_index("sp")
    block_id = position % BLOCKS
    group_id = position // BLOCKS
    channel_start = lax.axis_index("ch") * local_output
    own_out_grad = lax.dynamic_slice_in_dim(out_grad, channel_start, local_output, 3)
    group_pick = jnp.arange(groups, dtype=jnp.int32) == group_id
    group_onehot = group_pick.astype(jnp.float32)
    own_heights = jnp.sum(jnp.where(group_pick[None, :], heights, 0), axis=1)
    own_widths = jnp.sum(jnp.where(group_pick[None, :], widths, 0), axis=1)
    row_ids = block_id * rows_dev + jnp.arange(rows_dev, dtype=jnp.int32)
    col_ids = jnp.arange(grid_width, dtype=jnp.int32)
    inside = (row_ids[None, :, None] < own_heights[:, None, None]) & (
        col_ids[None, None, :] < own_widths[:, None, None]
    )
    pix_mask = inside.astype(jnp.float32)[..., None]
    valid_count = jnp.sum((heights * widths).astype(jnp.float32))
    own_count = (own_heights * own_widths).astype(jnp.float32)
    masked_values = features * pix_mask.astype(jnp.bfloat16)
    flat_pix = masked_values.reshape(pixels, channel_total)
    point_conv = jnp.einsum("pc,fc->pf", flat_pix, w_point, preferred_element_type=jnp.float32)
    conv_list = [point_conv.reshape(count_k, rows_dev, grid_width, local_output)]
    for dilation_index, dilation_factor in enumerate(dilation_factors):
        dilation_rate = rows_dev * dilation_factor
        running_total = tap_partials(masked_values, atrous_weight[dilation_index, 1], dilation_rate)
        for row_offset_tap in (0, 2):
            shift_amount = (1 - row_offset_tap) * dilation_factor
            keep_rows = source_inside(block_id, shift_amount)
            received_part = move_features(masked_values, shift_amount) * keep_rows.astype(
                jnp.bfloat16
            )
            running_total = running_total + tap_partials(
                received_part, atrous_weight[dilation_index, row_offset_tap], dilation_rate
            )
        conv_list.append(running_total)
    conv_out = jnp.stack(conv_list)
    stat_sum, stat_square = lax.psum(
        (
            jnp.sum(conv_out * pix_mask, axis=(1, 2, 3)),
            jnp.sum(conv_out * conv_out * pix_mask, axis=(1, 2, 3)),
        ),
        "sp",
    )
    branch_mean = stat_sum / valid_count
    branch_inv = lax.rsqrt(stat_square / valid_count - branch_mean * branch_mean + epsilon)
    normed = (conv_out - branch_mean[:, None, None, None, :]) * branch_inv[:, None, None, None, :]
    pre_act = bn_gains[:4][:, None, None, None, :] * normed + bn_shifts[:4][:, None, None, None, :]
    branch_act = (pix_mask * jax.nn.silu(pre_act)).astype(jnp.bfloat16)
    own_sums = jnp.sum(masked_values, axis=(1, 2), dtype=jnp.float32)
    own_pooled = own_sums / own_count[:, None]
    pool_weight = w_pool.astype(jnp.float32)
    pooled = lax.psum(own_pooled[:, None, :] * group_onehot[None, :, None], "sp")
    projected = jnp.dot(
        pooled.reshape(images, channel_total), pool_weight.T, precision=highest_precision
    )
    pool_mean = jnp.mean(projected, axis=0)
    pool_inv = lax.rsqrt(jnp.mean(projected * projected, axis=0) - pool_mean * pool_mean + epsilon)
    pool_normed = (projected - pool_mean) * pool_inv
    pool_pre = bn_gains[4] * pool_normed + bn_shifts[4]
    pool_act = jax.nn.silu(pool_pre).astype(jnp.bfloat16)
    own_act = jnp.sum(
        pool_act.astype(jnp.float32).reshape(count_k, groups, local_output)
        * group_onehot[None, :, None],
        axis=1,
    )
    pool_pixels = (own_act[:, None, None, :] * pix_mask).astype(jnp.bfloat16)
    stacked = jnp.concatenate([branch_act, pool_pixels[None]], axis=0).reshape(
        5, pixels, local_output
    )
    partial_value = jnp.einsum("bpf,bfo->po", stacked, w_proj, preferred_element_type=jnp.float32)
    mixed_sum = lax.psum_scatter(
        partial_value.reshape(count_k, rows_dev, grid_width, full_out),
        "ch",
        scatter_dimension=3,
        tiled=True,
    )
    final_sum, final_square = lax.psum(
        (
            jnp.sum(mixed_sum * pix_mask, axis=(0, 1, 2)),
            jnp.sum(mixed_sum * mixed_sum * pix_mask, axis=(0, 1, 2)),
        ),
        "sp",
    )
    final_mean = final_sum / valid_count
    final_inv = lax.rsqrt(final_square / valid_count - final_mean * final_mean + epsilon)
    final_normed = (mixed_sum - final_mean) * final_inv
    final_pre = bn_gains[5] * final_normed + bn_shifts[5]
    output = (pix_mask * jax.nn.silu(final_pre)).astype(jnp.bfloat16)
    final_dt = pix_mask * own_out_grad.astype(jnp.float32) * silu_slope(final_pre)
    final_beta, final_gamma = lax.psum(
        (jnp.sum(final_dt, axis=(0, 1, 2)), jnp.sum(final_dt * final_normed, axis=(0, 1, 2))), "sp"
    )
    mixed_grad = (
        pix_mask
        * final_inv
        * bn_gains[5]
        * (final_dt - final_beta / valid_count - final_normed * final_gamma / valid_count)
    ).astype(jnp.bfloat16)
    full_grad = lax.all_gather(mixed_grad, "ch", axis=3, tiled=True).reshape(pixels, full_out)
    g_proj = jnp.einsum("bpf,po->bfo", stacked, full_grad, preferred_element_type=jnp.float32)
    act_grads = jnp.einsum(
        "po,bfo->bpf", full_grad, w_proj, preferred_element_type=jnp.float32
    ).reshape(5, count_k, rows_dev, grid_width, local_output)
    branch_dt = pix_mask * act_grads[:4] * silu_slope(pre_act)
    pool_own_grad = jnp.sum(act_grads[4] * pix_mask, axis=(1, 2))
    branch_beta, branch_gamma, pool_grad = lax.psum(
        (
            jnp.sum(branch_dt, axis=(1, 2, 3)),
            jnp.sum(branch_dt * normed, axis=(1, 2, 3)),
            pool_own_grad[:, None, :] * group_onehot[None, :, None],
        ),
        "sp",
    )
    convolution_gradients = (
        pix_mask
        * branch_inv[:, None, None, None, :]
        * bn_gains[:4][:, None, None, None, :]
        * (
            branch_dt
            - branch_beta[:, None, None, None, :] / valid_count
            - normed * branch_gamma[:, None, None, None, :] / valid_count
        )
    ).astype(jnp.bfloat16)
    pool_dt = pool_grad.reshape(images, local_output) * silu_slope(pool_pre)
    pool_beta = jnp.sum(pool_dt, axis=0)
    pool_gamma = jnp.sum(pool_dt * pool_normed, axis=0)
    proj_grad = (
        pool_inv * bn_gains[4] * (pool_dt - pool_beta / images - pool_normed * pool_gamma / images)
    )
    own_proj_grad = jnp.sum(
        proj_grad.reshape(count_k, groups, local_output) * group_onehot[None, :, None], axis=1
    )
    g_pool = jnp.einsum("kf,kc->fc", own_proj_grad, own_pooled, precision=highest_precision)
    pooled_grad = (
        jnp.einsum("kf,fc->kc", own_proj_grad, pool_weight, precision=highest_precision)
        / own_count[:, None]
    )
    point_grad = convolution_gradients[0].reshape(pixels, local_output)
    g_point = jnp.einsum("pf,pc->fc", point_grad, flat_pix, preferred_element_type=jnp.float32)
    input_term = jnp.einsum("pf,fc->pc", point_grad, w_point, preferred_element_type=jnp.float32)
    input_term = (
        input_term.reshape(count_k, rows_dev, grid_width, channel_total)
        + pooled_grad[:, None, None, :]
    )
    atrous_list = []
    for dilation_index, dilation_factor in enumerate(dilation_factors):
        dilation_rate = rows_dev * dilation_factor
        tap_list = []
        for row_offset_tap in range(3):
            shift_amount = (row_offset_tap - 1) * dilation_factor
            if shift_amount == 0:
                received_part = convolution_gradients[dilation_index + 1]
            else:
                received_part = shifted_gradients(
                    convolution_gradients[dilation_index + 1], shift_amount
                ) * source_inside(block_id, shift_amount).astype(jnp.bfloat16)
            spread = jnp.stack(
                [
                    shift_cols(received_part, dilation_rate),
                    received_part,
                    shift_cols(received_part, -dilation_rate),
                ],
                axis=3,
            ).reshape(pixels, 3 * local_output)
            tap_list.append(
                jnp.einsum(
                    "pt,pc->tc", spread, flat_pix, preferred_element_type=jnp.float32
                ).reshape(3, local_output, channel_total)
            )
            tap_weight_slice = atrous_weight[dilation_index, row_offset_tap].reshape(
                3 * local_output, channel_total
            )
            input_term = input_term + jnp.einsum(
                "pt,tc->pc", spread, tap_weight_slice, preferred_element_type=jnp.float32
            ).reshape(count_k, rows_dev, grid_width, channel_total)
        atrous_list.append(jnp.stack(tap_list))
    g_atrous = jnp.stack(atrous_list)
    in_grad = lax.psum_scatter(
        (input_term * pix_mask).astype(jnp.bfloat16), "ch", scatter_dimension=3, tiled=True
    )
    g_point, g_atrous, g_proj, g_pool = (
        lax.psum(g_point.astype(jnp.bfloat16), "sp").astype(jnp.float32),
        lax.psum(g_atrous.astype(jnp.bfloat16), "sp").astype(jnp.float32),
        lax.psum(g_proj.astype(jnp.bfloat16), "sp").astype(jnp.float32),
        lax.psum(g_pool.astype(jnp.bfloat16), "sp").astype(jnp.float32),
    )
    g_gains = jnp.concatenate([branch_gamma, pool_gamma[None], final_gamma[None]], axis=0)
    g_shifts = jnp.concatenate([branch_beta, pool_beta[None], final_beta[None]], axis=0)
    return (output, in_grad, g_point, g_atrous, g_pool, g_proj, g_gains, g_shifts)


def body(
    features, heights, widths, w_point, atrous_weight, w_pool, w_proj, bn_gains, bn_shifts, out_grad
):
    images, rows_dev, cols, C = features.shape
    L = w_point.shape[0]
    if lax.axis_size("sp") != BLOCKS or lax.axis_size("ch") != 4 or L != 64:
        return plain_body(
            features, heights, widths, w_point, atrous_weight, w_pool, w_proj, bn_gains, bn_shifts, out_grad
        )
    F = w_proj.shape[2]
    W = BRANCHES * L
    slabs = images * rows_dev
    cells = slabs * cols
    rates = tuple(rows_dev * f for f in dilation_factors)
    block_id = lax.axis_index("sp")
    own = lax.axis_index("ch")
    h, w = heights[:, 0], widths[:, 0]
    row_ids = block_id * rows_dev + jnp.arange(rows_dev, dtype=jnp.int32)
    lim = jnp.where(row_ids[None, :] < h[:, None], w[:, None], 0).reshape(slabs)
    own_count = (h * w).astype(f32)
    n = jnp.sum(own_count)
    x = features.reshape(cells, C)
    og = out_grad.reshape(cells, F)

    norms = jnp.concatenate([bn_gains, bn_shifts, jnp.zeros((4, L), f32)], axis=0)
    wp = w_proj.reshape(5 * L, F)
    packed = jnp.concatenate([wp, thirds(norms).reshape(-1, F)], axis=0)
    packed_y = swap(packed, "ch", 2)
    packed_all = jnp.stack([packed, swap(packed, "ch", 1), packed_y, swap(packed_y, "ch", 1)])
    wp_all = packed_all[:, : 5 * L]
    norms_all = jnp.sum(packed_all[:, 5 * L :].reshape(4, 3, 16, L).astype(f32), axis=1)
    wbranch_all, wpool_all = wp_all[:, :W], wp_all[:, W:]
    natural = (own ^ jnp.arange(4))[:, None] == jnp.arange(4)[None, :]
    final_par = jnp.sum(
        jnp.where(natural[:, :, None, None], norms_all[None, :, (5, 11), :], 0.0), axis=1
    )
    final_gain, final_shift = final_par[:, 0].reshape(F), final_par[:, 1].reshape(F)

    KT = 512
    steps = C // KT
    x_spec = pl.BlockSpec((cells, KT), lambda k: (0, k))
    first = [(1 - (block_id // f) % 2).astype(jnp.int32) for f in dilation_factors]

    def side_taps(which, x):
        out = pl.pallas_call(
            functools.partial(
                side_kernel, steps=steps, slabs=slabs, cols=cols, rates=tuple(rates[j] for j in which)
            ),
            grid=(steps,),
            in_specs=[SMEM, SMEM, x_spec]
            + [
                pl.BlockSpec((1, 1, 3, L, KT), lambda k, j=j, u=u: (j, u, 0, 0, k))
                for j in which
                for u in (0, 2)
            ],
            out_specs=[pl.BlockSpec((cells // 2, 2 * L), lambda k: (0, 0))] * (2 * len(which)),
            out_shape=[jax.ShapeDtypeStruct((cells // 2, 2 * L), bf16)] * (2 * len(which)),
            scratch_shapes=[
                pltpu.VMEM((6 * len(which) * L, KT), bf16),
                pltpu.VMEM((cells, 6 * len(which) * L), f32),
            ],
            compiler_params=params(),
            cost_estimate=cost(2 * cells * C * 6 * len(which) * L, 10e6),
            name="side_taps",
        )(lim, jnp.stack([first[j] for j in which]), x, *[atrous_weight] * (2 * len(which)))
        moved = []
        for i, j in enumerate(which):
            moved += neighbours(out[2 * i], out[2 * i + 1], "sp", dilation_factors[j])
        return moved, out[0]

    narrow = C // 2
    valid = (jnp.arange(cols, dtype=jnp.int32)[None, :] < lim[:, None]).reshape(cells, 1)
    cut = narrow // BLOCKS
    part = cells // images
    image = lax.dynamic_slice(x, (own * part, 0), (part, narrow))
    image = jnp.where(lax.dynamic_slice_in_dim(valid, own * part, part), image, jnp.zeros((), bf16))
    column = block_id // 2
    sent = [lax.dynamic_slice_in_dim(image, (column ^ dz) * 2 * cut, 2 * cut, 1) for dz in range(4)]
    mine = jnp.stack([sent[0]] + [swap(sent[dz], "sp", 2 * dz) for dz in (1, 2, 3)])
    wide_w = (C - narrow) // 4
    own_wide = lax.dynamic_slice_in_dim(x, narrow + own * wide_w, wide_w, 1)
    own_wide = jnp.where(valid, own_wide, jnp.zeros((), bf16))
    halo, made = side_taps((0, 1, 2), x)
    x_wide = lax.all_gather(after(own_wide, made), ("sp", "ch"), axis=0).reshape(BLOCKS, 4, cells, wide_w)
    x_then = after(x, made, mine, own_wide)
    centre, sums = pl.pallas_call(
        functools.partial(centre_kernel, steps=steps, slabs=slabs, cols=cols, rates=rates, images=images),
        grid=(steps,),
        in_specs=[
            SMEM,
            x_spec,
            pl.BlockSpec((3, 1, 3, L, KT), lambda k: (0, 1, 0, 0, k)),
            pl.BlockSpec((L, KT), lambda k: (0, k)),
        ],
        out_specs=[pl.BlockSpec((cells, W), lambda k: (0, 0)), pl.BlockSpec((8, KT), lambda k: (0, k))],
        out_shape=[jax.ShapeDtypeStruct((cells, W), f32), jax.ShapeDtypeStruct((8, C), f32)],
        scratch_shapes=[pltpu.VMEM((10 * L, KT), bf16), pltpu.VMEM((cells, 10 * L), f32)],
        compiler_params=params(),
        cost_estimate=cost(2 * cells * C * 10 * L, 8e6),
        name="centre_taps",
    )(lim, x_then, atrous_weight, w_point)
    own_pooled = sums[:images] / own_count[:, None]
    proj_part = lax.dot_general(own_pooled, w_pool.astype(f32), NT, precision=highest_precision)

    conv, conv_send, stat = pl.pallas_call(
        functools.partial(combine_kernel, slabs=slabs, cols=cols),
        in_specs=[SMEM] + [VMEM] * 7,
        out_specs=[VMEM] * 3,
        out_shape=[
            jax.ShapeDtypeStruct((cells, W), f32),
            jax.ShapeDtypeStruct((cells, W), bf16),
            jax.ShapeDtypeStruct((8, W), f32),
        ],
        compiler_params=params(20),
        cost_estimate=cost(2e6, 4e6),
        name="combine_taps",
    )(lim, centre, *halo)
    conv_y = swap(conv_send, "ch", 2)
    conv_core = swap(conv_send, "ch", 1)
    conv_diag = swap(conv_y, "ch", 1)
    tile = jnp.concatenate([stat[:4], jnp.pad(proj_part, ((0, 0), (0, W - L)))], axis=0)
    tile = sum_over_sp(tile)
    mine = after(mine, tile)
    keep = lax.dynamic_slice_in_dim(mine, (block_id % 2) * cut, cut, 2)
    give = lax.dynamic_slice_in_dim(mine, (1 - block_id % 2) * cut, cut, 2)
    taken = swap(give, "sp", 1)
    tile = jnp.concatenate([tile[:2], stat[2:3], tile[3:]], axis=0)
    tiles = jnp.stack([tile] + [swap(tile, "ch", b) for b in (1, 2, 3)])
    mean = tiles[:, 0] / n
    rstd = lax.rsqrt(tiles[:, 1] / n - mean * mean + epsilon)
    branch_stat = jnp.stack([mean, rstd, tiles[:, 2]], axis=1)
    branch_par = jnp.stack([norms_all[:, :4].reshape(4, W), norms_all[:, 6:10].reshape(4, W)], axis=1)
    projected = tiles[:, 4 : 4 + images, :L]
    pool_mean = jnp.mean(projected, axis=1, keepdims=True)
    pool_rstd = lax.rsqrt(
        jnp.mean(projected * projected, axis=1, keepdims=True) - pool_mean * pool_mean + epsilon
    )
    pool_normed = (projected - pool_mean) * pool_rstd
    pool_pre = norms_all[:, 4:5] * pool_normed + norms_all[:, 10:11]
    pool_act = jax.nn.silu(pool_pre).astype(bf16)
    pool_in = jnp.pad(pool_act, ((0, 0), (0, 8 - images), (0, 0)))

    mixed, act, mixed_stat = pl.pallas_call(
        functools.partial(mix_kernel, slabs=slabs, cols=cols, images=images),
        in_specs=[SMEM] + [VMEM] * 9,
        out_specs=[VMEM] * 3,
        out_shape=[
            jax.ShapeDtypeStruct((cells, F), f32),
            jax.ShapeDtypeStruct((cells, W), bf16),
            jax.ShapeDtypeStruct((8, F), f32),
        ],
        scratch_shapes=[pltpu.VMEM((cells, W), bf16)],
        compiler_params=params(20),
        cost_estimate=cost(2 * cells * 4 * W * F, 6e6),
        name="mix_branches",
    )(lim, conv, conv_core, conv_y, conv_diag, branch_stat, branch_par, wbranch_all, pool_in, wpool_all)
    total = sum_over_sp(mixed_stat)
    fmean = total[0] / n
    frstd = lax.rsqrt(total[1] / n - fmean * fmean + epsilon)
    final_stat = jnp.stack([fmean, frstd, final_gain, final_shift])
    out_all, fdt, fsums = pl.pallas_call(
        functools.partial(final_kernel, slabs=slabs, cols=cols),
        in_specs=[SMEM] + [VMEM] * 3,
        out_specs=[VMEM] * 3,
        out_shape=[
            jax.ShapeDtypeStruct((cells, F), bf16),
            jax.ShapeDtypeStruct((cells, F), f32),
            jax.ShapeDtypeStruct((8, F), f32),
        ],
        compiler_params=params(20),
        cost_estimate=cost(2e6, 4e6),
        name="final_norm",
    )(lim, mixed, og, final_stat)
    ftotal = sum_over_sp(fsums)
    final_beta, final_gamma = ftotal[0], ftotal[1]
    fgrad_stat = jnp.stack([fmean, frstd, frstd * final_gain, final_beta / n, final_gamma / n])
    own_gain, own_shift = branch_par[0, 0], branch_par[0, 1]
    own_mean, own_rstd = branch_stat[0, 0], branch_stat[0, 1]
    dt, gproj, image_sums, bsums = pl.pallas_call(
        functools.partial(branch_kernel, slabs=slabs, cols=cols, images=images),
        in_specs=[SMEM] + [VMEM] * 7,
        out_specs=[VMEM] * 4,
        out_shape=[
            jax.ShapeDtypeStruct((cells, W), f32),
            jax.ShapeDtypeStruct((W, F), f32),
            jax.ShapeDtypeStruct((8, F), f32),
            jax.ShapeDtypeStruct((8, W), f32),
        ],
        scratch_shapes=[pltpu.VMEM((cells, F), bf16)],
        compiler_params=params(20),
        cost_estimate=cost(4 * cells * W * F, 8e6),
        name="branch_grads",
    )(
        lim, mixed, fdt, fgrad_stat, conv, act,
        jnp.stack([own_mean, own_rstd, own_gain, own_shift]), wp[:W],
    )
    image_sums = image_sums[:images]
    pool_part = lax.dot_general(image_sums, w_proj[4].astype(f32), NT, precision=highest_precision)
    gproj_pool = lax.dot_general(pool_act[0].astype(f32), image_sums, TN, precision=highest_precision)
    btile = sum_over_sp(
        jnp.concatenate([bsums[:4], jnp.pad(pool_part, ((0, 0), (0, W - L)))], axis=0)
    )
    branch_beta, branch_gamma = btile[0], btile[1]
    cgt = pl.pallas_call(
        functools.partial(grad_kernel, slabs=slabs, cols=cols),
        in_specs=[SMEM] + [VMEM] * 3,
        out_specs=VMEM,
        out_shape=jax.ShapeDtypeStruct((W, cells), bf16),
        scratch_shapes=[pltpu.VMEM((cells, W), f32)],
        compiler_params=params(20),
        cost_estimate=cost(2e6, 4e6),
        name="conv_grads",
    )(lim, dt, conv, jnp.stack([own_mean, own_rstd, own_rstd * own_gain, branch_beta / n, branch_gamma / n]))
    pool_dt = btile[4 : 4 + images, :L] * silu_slope(pool_pre[0])
    pool_beta = jnp.sum(pool_dt, axis=0)
    pool_gamma = jnp.sum(pool_dt * pool_normed[0], axis=0)
    proj_grad = (
        pool_rstd[0] * bn_gains[4] * (pool_dt - pool_beta / images - pool_normed[0] * pool_gamma / images)
    )
    g_gains = jnp.concatenate([branch_gamma.reshape(4, L), pool_gamma[None],
        lax.dynamic_slice_in_dim(final_gamma, own * L, L)[None]], axis=0)
    g_shifts = jnp.concatenate([branch_beta.reshape(4, L), pool_beta[None],
        lax.dynamic_slice_in_dim(final_beta, own * L, L)[None]], axis=0)
    output = lax.dynamic_slice_in_dim(out_all, own * L, L, 1).reshape(images, rows_dev, cols, L)
    pooled_grad = (
        jnp.einsum("kf,fc->kc", proj_grad, w_pool.astype(f32), precision=highest_precision)
        / own_count[:, None]
    )
    ANY = pl.BlockSpec(memory_space=pl.ANY)
    col_row = jnp.broadcast_to((jnp.arange(cells, dtype=jnp.int32) % cols)[None, :], (8, cells))
    pos = jnp.stack([block_id, own % 2, own]).astype(jnp.int32)
    def column_taps(block):
        return pl.pallas_call(
            functools.partial(expand_kernel, cols=cols, rates=rates),
            grid=(1,),
            in_specs=[pl.BlockSpec((8, cells), lambda i: (0, 0)), pl.BlockSpec((W, cells), lambda i: (0, 0))],
            out_specs=pl.BlockSpec((10 * L, cells), lambda i: (0, 0)),
            out_shape=jax.ShapeDtypeStruct((10 * L, cells), bf16),
            compiler_params=params(),
            cost_estimate=cost(1e9, 6e6),
            name="column_taps",
        )(col_row, block)

    near = [swap(cgt, "sp", b) for b in (2, 4, 6)]
    pair = swap(cgt, "sp", 1)
    taps = [column_taps(cgt), column_taps(pair), column_taps(near[0])]
    near_pair = swap(near[0], "sp", 1)
    taps.append(column_taps(near_pair))
    x_slices = after(jnp.stack([keep, taken], axis=1).reshape(1, BLOCKS, part, cut), near[0])
    x_slices = jnp.concatenate([x_slices, swap(x_slices, "ch", 2)], axis=0)
    x_core = swap(x_slices, "ch", 1)
    x_slices = jnp.stack([x_slices[0], x_core[0], x_slices[1], x_core[1]])
    pooled = sum_over_sp(after(own_pooled, near[0]))
    far = [after(near[1], *taps[:3]), after(near[2], *taps, x_slices, pooled)]
    far_pairs = [swap(t, "sp", 1) for t in far]
    blocks = [cgt, pair, near[0], near_pair, far[0], far_pairs[0], far[1], far_pairs[1]]
    taps += [column_taps(t) for t in blocks[4:]]
    eighth = narrow // BLOCKS
    tap_scratch = pltpu.VMEM((10 * L, BLOCKS * cells), bf16)
    gw = pl.pallas_call(
        functools.partial(narrow_kernel, parts=images),
        in_specs=[SMEM] + [ANY] * (BLOCKS + 1),
        out_specs=pl.BlockSpec((28 * L, eighth), lambda i: (0, 0)),
        grid=(1,),
        out_shape=jax.ShapeDtypeStruct((28 * L, eighth), bf16),
        scratch_shapes=[
            tap_scratch,
            pltpu.VMEM((BLOCKS * cells, eighth), bf16),
            pltpu.SemaphoreType.DMA((BLOCKS,)),
            pltpu.SemaphoreType.DMA((images, BLOCKS)),
        ],
        compiler_params=params(),
        cost_estimate=cost(2 * cells * BLOCKS * 28 * L * eighth, 12e6),
        name="narrow_weight_grads",
    )(pos, *taps, x_slices)
    gw_all = lax.all_gather(gw, "sp", axis=0)
    pos, gw = lax.optimization_barrier((pos, gw))
    group = C // 4
    ig = pl.pallas_call(
        functools.partial(input_grad_kernel, slabs=slabs, cols=cols, rates=rates, images=images),
        grid_spec=pltpu.PrefetchScalarGridSpec(
            num_scalar_prefetch=2,
            grid=(4,),
            in_specs=[
                pl.BlockSpec((8, cells), lambda i, p, l: (0, 0)),
                pl.BlockSpec((27 * L, group), lambda i, p, l: (0, p[2] ^ i)),
                pl.BlockSpec((L, group), lambda i, p, l: (0, p[2] ^ i)),
                pl.BlockSpec((8, group), lambda i, p, l: (0, p[2] ^ i)),
            ]
            + [ANY] * BLOCKS,
            out_specs=pl.BlockSpec((1, cells, group), lambda i, p, l: (i, 0, 0)),
            scratch_shapes=[
                pltpu.VMEM((BLOCKS, W, cells), bf16),
                pltpu.VMEM((cells, 28 * L), bf16),
                pltpu.VMEM((28 * L, group), bf16),
                pltpu.SemaphoreType.DMA((BLOCKS,)),
            ],
        ),
        out_shape=jax.ShapeDtypeStruct((4, cells, group), bf16),
        compiler_params=params(),
        cost_estimate=cost(1e6, 1e6),
        name="input_grads",
    )(pos, lim, col_row, atrous_weight.reshape(27 * L, C), w_point,
      jnp.pad(pooled_grad, ((0, 8 - images), (0, 0))), *blocks)
    gp = after(jnp.concatenate([gproj, gproj_pool], axis=0).astype(bf16), gw)
    gp = (gp.astype(f32) + swap(gp, "sp", 1).astype(f32)).astype(bf16)
    gp_parts = [swap(gp, "sp", b) for b in (2, 4, 6)]
    g_pool = jnp.einsum("kf,kc->fc", proj_grad, pooled, precision=highest_precision)
    from_core = swap(jnp.concatenate([ig[1], ig[3]], axis=1), "ch", 1)
    from_core = from_core.astype(f32)
    keep = ig[0].astype(f32) + from_core[:, :group]
    give = (ig[2].astype(f32) + from_core[:, group:]).astype(bf16)
    given = swap(give, "ch", 2)
    pos = after(pos, give)
    if wide_w:
        g_wide, p_wide = pl.pallas_call(
            wide_kernel,
            grid=(4,),
            in_specs=[SMEM, pl.BlockSpec((BLOCKS, 1, cells, wide_w), lambda i: (0, i, 0, 0))] + [ANY] * BLOCKS,
            out_specs=[
                pl.BlockSpec((27 * L, wide_w), lambda i: (0, narrow // wide_w + i)),
                pl.BlockSpec((L, wide_w), lambda i: (0, narrow // wide_w + i)),
            ],
            out_shape=[jax.ShapeDtypeStruct((27 * L, C), f32), jax.ShapeDtypeStruct((L, C), f32)],
            scratch_shapes=[tap_scratch, pltpu.SemaphoreType.DMA((BLOCKS,))],
            compiler_params=params(),
            cost_estimate=cost(1e6, 1e6),
            name="wide_weight_grads",
        )(pos, x_wide, *taps)
    else:
        g_wide, p_wide = jnp.zeros((27 * L, C), f32), jnp.zeros((L, C), f32)
    gp, *gp_parts = (t.astype(f32) for t in lax.optimization_barrier((gp, *gp_parts, p_wide))[:4])
    g_proj = ((gp + gp_parts[0]) + (gp_parts[1] + gp_parts[2])).reshape(5, L, F)
    in_grad = (keep + after(given, p_wide).astype(f32)).astype(bf16)
    in_grad = in_grad.reshape(images, rows_dev, cols, group)

    step = 3 * L
    g_atrous, g_point = pl.pallas_call(
        widen_kernel,
        grid=(9,),
        in_specs=[
            pl.BlockSpec((BLOCKS, step, eighth), lambda i: (0, i, 0)),
            pl.BlockSpec((BLOCKS, L, eighth), lambda i: (0, 27, 0)),
            ANY,
            ANY,
        ],
        out_specs=[
            pl.BlockSpec((step, narrow), lambda i: (i, 0)),
            pl.BlockSpec((L, narrow), lambda i: (0, 0)),
        ],
        out_shape=[jax.ShapeDtypeStruct((27 * L, C), f32), jax.ShapeDtypeStruct((L, C), f32)],
        input_output_aliases={2: 0, 3: 1},
        compiler_params=params(),
        cost_estimate=cost(1e6, 20e6),
        name="widen",
    )(gw_all, gw_all, g_wide, p_wide)
    g_atrous = g_atrous.reshape(3, 3, 3, L, C)
    return (output, in_grad, g_point, g_atrous, g_pool, g_proj, g_gains, g_shifts)


def solution(mesh):
    placed = (
        P(None, "sp", None, None),
        P(),
        P(),
        P("ch", None),
        P(None, None, None, "ch", None),
        P("ch", None),
        P(None, "ch", None),
        P(None, "ch"),
        P(None, "ch"),
        P(None, "sp", None, None),
    )
    return jax.shard_map(
        body,
        mesh=mesh,
        in_specs=placed,
        out_specs=(
            P(None, "sp", None, "ch"),
            P(None, "sp", None, "ch"),
            P("ch", None),
            P(None, None, None, "ch", None),
            P("ch", None),
            P(None, "ch", None),
            P(None, "ch"),
            P(None, "ch"),
        ),
        check_vma=False,
    )
```

```python
import functools

import jax
import jax.numpy as jnp
from jax import lax
from jax.experimental import pallas as pl
from jax.experimental.pallas import tpu as pltpu
from jax.sharding import PartitionSpec as P

BLOCKS = 8
BRANCHES = 4
epsilon = 1e-05
dilation_factors = (1, 2, 3)
highest_precision = lax.Precision.HIGHEST
f32 = jnp.float32
bf16 = jnp.bfloat16
MIB = 1 << 20
VMEM = pl.BlockSpec(memory_space=pltpu.VMEM)
SMEM = pl.BlockSpec(memory_space=pltpu.SMEM)
NT = (((1,), (1,)), ((), ()))
NN = (((1,), (0,)), ((), ()))
TN = (((0,), (0,)), ((), ()))


def dot(a, b, dims):
    return lax.dot_general(a, b, dims, preferred_element_type=f32)


def params(mib=60, **kw):
    return pltpu.CompilerParams(vmem_limit_bytes=mib * MIB, **kw)


def cost(flops, nbytes):
    return pl.CostEstimate(flops=int(flops), bytes_accessed=int(nbytes), transcendentals=0)


def cell_mask(lim_ref, slabs, cols, width):
    col = lax.broadcasted_iota(jnp.int32, (cols, width), 0)
    return jnp.concatenate([(col < lim_ref[i]).astype(f32) for i in range(slabs)], axis=0)


def column_ids(slabs, cols, width):
    return lax.broadcasted_iota(jnp.int32, (slabs, cols, width), 1).reshape(slabs * cols, width)


def from_left(a, d, col):
    return jnp.where(col >= d, pltpu.roll(a, d, 0), 0.0)


def from_right(a, d, col, cols):
    return jnp.where(col < cols - d, pltpu.roll(a, a.shape[0] - d, 0), 0.0)


def silu_parts(t):
    s = 1.0 / (1.0 + jnp.exp(-t))
    return s, t * s


def slope(t, s):
    return s * (1.0 + t * (1.0 - s))


def column_sums(*rows):
    sums = [jnp.sum(r, axis=0, keepdims=True) for r in rows]
    width = sums[0].shape[1]
    return jnp.concatenate(sums + [jnp.zeros((8 - len(sums), width), f32)], axis=0)


def side_kernel(lim_ref, low_ref, x_ref, *refs, steps, slabs, cols, rates):
    n_rates = len(rates)
    weights, outs, (wcat, acc) = refs[: 2 * n_rates], refs[2 * n_rates : 4 * n_rates], refs[4 * n_rates :]
    k = pl.program_id(0)
    L = weights[0].shape[3]
    for j in range(n_rates):
        for v in range(3):
            t = (j * 3 + v) * 2 * L
            wcat[t : t + L] = weights[2 * j][0, 0, v]
            wcat[t + L : t + 2 * L] = weights[2 * j + 1][0, 0, v]

    @pl.when(k == 0)
    def _():
        acc[...] = jnp.zeros_like(acc)

    x = x_ref[...]
    total = 6 * n_rates * L
    for n in range(0, total, 256):
        e = min(n + 256, total)
        acc[:, n:e] += dot(x, wcat[n:e], NT)

    @pl.when(k == steps - 1)
    def _():
        cells = slabs * cols
        half = cells // 2
        mask = cell_mask(lim_ref, slabs, cols, 2 * L)
        col = column_ids(slabs, cols, 2 * L)
        low = lax.broadcasted_iota(jnp.int32, (half, 2 * L), 1) < L
        for j in range(n_rates):
            a = [acc[:, (j * 3 + v) * 2 * L : (j * 3 + v + 1) * 2 * L] * mask for v in range(3)]
            s = a[1] + from_left(a[0], rates[j], col) + from_right(a[2], rates[j], col, cols)
            top, bottom = s[:half], s[half:]
            up = jnp.where(low, top, pltpu.roll(bottom, L, 1))
            down = jnp.where(low, pltpu.roll(top, L, 1), bottom)
            first = low_ref[j] == 1
            outs[2 * j][...] = jnp.where(first, up, down).astype(bf16)
            outs[2 * j + 1][...] = jnp.where(first, down, up).astype(bf16)


def centre_kernel(
    lim_ref, x_ref, wc_ref, wpoint_ref, out_ref, sums_ref, wcat, acc, *, steps, slabs, cols, rates, images
):
    k = pl.program_id(0)
    L = wpoint_ref.shape[0]
    order = [None, (0, 1), (1, 1), (2, 1), (1, 0), (2, 0), (1, 2), (2, 2), (0, 0), (0, 2)]
    for i, tap in enumerate(order):
        wcat[i * L : (i + 1) * L] = wpoint_ref[...] if tap is None else wc_ref[tap[0], 0, tap[1]]

    @pl.when(k == 0)
    def _():
        acc[...] = jnp.zeros_like(acc)

    x = x_ref[...]
    total = 10 * L
    for n in range(0, total, 256):
        e = min(n + 256, total)
        acc[:, n:e] += dot(x, wcat[n:e], NT)

    width = x_ref.shape[1]
    cid = lax.broadcasted_iota(jnp.int32, (cols, width), 0)
    per = slabs // images
    sums = []
    for image in range(images):
        part = jnp.zeros((cols, width), f32)
        for i in range(image * per, (image + 1) * per):
            part += jnp.where(cid < lim_ref[i], x_ref[i * cols : (i + 1) * cols].astype(f32), 0.0)
        sums.append(jnp.sum(part, axis=0, keepdims=True))
    sums_ref[...] = jnp.concatenate(sums + [jnp.zeros((8 - images, width), f32)], axis=0)

    @pl.when(k == steps - 1)
    def _():
        cells = slabs * cols
        mask = cell_mask(lim_ref, slabs, cols, 2 * L)
        col = column_ids(slabs, cols, 2 * L)
        low = lax.broadcasted_iota(jnp.int32, (cells, 2 * L), 1) < L
        b = [acc[:, i * 2 * L : (i + 1) * 2 * L] * mask for i in range(5)]
        d0, d1, d2 = rates
        t = jnp.where(low, from_left(b[4], d0, col), from_right(b[4], d0, col, cols))
        out_ref[:, : 2 * L] = b[0] + jnp.where(low, 0.0, t + pltpu.roll(t, L, 1))
        out_ref[:, 2 * L :] = (
            b[1]
            + jnp.where(low, from_left(b[2], d1, col), from_left(b[2], d2, col))
            + jnp.where(low, from_right(b[3], d1, col, cols), from_right(b[3], d2, col, cols))
        )


def combine_kernel(lim_ref, centre_ref, *refs, slabs, cols):
    halo, (extra_ref, conv_ref, send_ref, message_ref, local_ref) = refs[:6], refs[6:]
    cells = slabs * cols
    half = cells // 2
    W = centre_ref.shape[1]
    L = W // 4
    h = [halo[2 * j][...].astype(f32) + halo[2 * j + 1][...].astype(f32) for j in range(3)]
    turned = [pltpu.roll(a, L, 1) for a in h]
    low = lax.broadcasted_iota(jnp.int32, (cells, 2 * L), 1) < L
    h0 = jnp.concatenate([turned[0], h[0]], axis=0)
    h1 = jnp.concatenate([h[1], turned[1]], axis=0)
    h2 = jnp.concatenate([turned[2], h[2]], axis=0)
    left = centre_ref[:, : 2 * L] + jnp.where(low, 0.0, h0)
    right = centre_ref[:, 2 * L :] + jnp.where(low, h1, h2)
    conv_ref[:, : 2 * L] = left
    conv_ref[:, 2 * L :] = right
    mask = cell_mask(lim_ref, slabs, cols, 2 * L)
    own = lim_ref[0]
    for i in range(1, slabs):
        own = own + lim_ref[i]
    own = jnp.maximum(own, 1).astype(f32)
    for lo, part in ((0, left), (2 * L, right)):
        s = jnp.sum(part * mask, axis=0, keepdims=True)
        q = jnp.sum(part * part * mask, axis=0, keepdims=True)
        local = s / own
        send_ref[:, lo : lo + 2 * L] = (part - local).astype(bf16)
        message_ref[:8, lo : lo + 2 * L] = extra_ref[:8, lo : lo + 2 * L] + jnp.concatenate(
            [s, q, jnp.zeros((6, 2 * L), f32)], axis=0
        )
        local_ref[:, lo : lo + 2 * L] = jnp.concatenate(
            [jnp.zeros((2, 2 * L), f32), local, jnp.zeros((5, 2 * L), f32)], axis=0
        )
    message_ref[8:] = extra_ref[8:]


def norm_of(total, square, n):
    mean = total / n
    return mean, lax.rsqrt(square / n - mean * mean + epsilon)


def added(parts):
    a, b, c, d = (r[...] for r in parts)
    return (a + b) + (c + d)


def mix_kernel(
    lim_ref, n_ref, conv_ref, c1_ref, c2_ref, c3_ref, t0, t1, t2, t3, p0, p1, p2, p3,
    mixed_ref, act_ref, sums_ref, stat_ref, scratch, *, slabs, cols, images
):
    per = slabs // images
    n = n_ref[0]
    width = conv_ref.shape[1]
    L = width // 4
    cid = lax.broadcasted_iota(jnp.int32, (cols, width), 0)
    pooled = None
    for d, (ref, tile_ref, par_ref) in enumerate(
        ((conv_ref, t0, p0), (c1_ref, t1, p1), (c2_ref, t2, p2), (c3_ref, t3, p3))
    ):
        tile = tile_ref[...]
        par = par_ref[5 * L :].astype(f32)
        par = par[0:4] + par[4:8] + par[8:12]
        gain = par[0:1]
        shift = jnp.concatenate([par[1:2, 2 * L :], par[2:3, : 2 * L]], axis=1)
        mean, rstd = norm_of(tile[0:1], tile[1:2], n)
        offset = mean if d == 0 else mean - tile[2:3]
        scale = rstd * gain
        if d == 0:
            stat_ref[...] = jnp.concatenate([mean, rstd, gain, shift, jnp.zeros((4, width), f32)], axis=0)
        dest = act_ref if d == 0 else scratch
        for i in range(slabs):
            rows = slice(i * cols, (i + 1) * cols)
            pre = (ref[rows].astype(f32) - offset) * scale + shift
            _, act = silu_parts(pre)
            dest[rows] = jnp.where(cid < lim_ref[i], act, 0.0).astype(bf16)
        part = dot(dest[...], par_ref[:width], NN)
        if d == 0:
            mixed_ref[...] = part
        else:
            mixed_ref[...] += part
        projected = tile[4 : 4 + images, :L]
        pmean, prstd = norm_of(
            jnp.sum(projected, axis=0, keepdims=True), jnp.sum(projected * projected, axis=0, keepdims=True), images
        )
        _, pact = silu_parts(par[1:2, :L] * ((projected - pmean) * prstd) + par[2:3, 2 * L : 3 * L])
        pact = jnp.concatenate([pact, jnp.zeros((16 - images, L), f32)], axis=0).astype(bf16)
        part = dot(pact, par_ref[width : width + L], NN)
        pooled = part if d == 0 else pooled + part
    F = mixed_ref.shape[1]
    cid = lax.broadcasted_iota(jnp.int32, (cols, F), 0)
    s = jnp.zeros((cols, F), f32)
    q = jnp.zeros((cols, F), f32)
    for i in range(slabs):
        rows = slice(i * cols, (i + 1) * cols)
        image = i // per
        value = mixed_ref[rows] + jnp.where(cid < lim_ref[i], pooled[image : image + 1], 0.0)
        mixed_ref[rows] = value
        s += value
        q += value * value
    sums_ref[...] = column_sums(s, q)


def final_kernel(
    lim_ref, n_ref, own_ref, mixed_ref, grad_ref, p0, p1, p2, p3, s0, s1, s2, s3, out_ref, dt_ref, sums_ref, stat_ref,
    *, slabs, cols
):
    F = mixed_ref.shape[1]
    total = added((s0, s1, s2, s3))
    mean, rstd = norm_of(total[0:1], total[1:2], n_ref[0])
    L = F // 4
    group = lax.broadcasted_iota(jnp.int32, (8, F), 1) // L
    gain, shift = jnp.zeros((8, F), f32), jnp.zeros((8, F), f32)
    for d, ref in enumerate((p0, p1, p2, p3)):
        par = ref[5 * L :].astype(f32)
        par = par[0:4] + par[4:8] + par[8:12]
        here = group == (own_ref[0] ^ d)
        g = jnp.where(group == 1, jnp.broadcast_to(par[1:2], (8, F)), 0.0)
        h = jnp.where(group == 3, jnp.broadcast_to(par[2:3], (8, F)), 0.0)
        gain += jnp.where(here, g + pltpu.roll(g, L, 1) + pltpu.roll(g, 2 * L, 1) + pltpu.roll(g, 3 * L, 1), 0.0)
        shift += jnp.where(here, h + pltpu.roll(h, L, 1) + pltpu.roll(h, 2 * L, 1) + pltpu.roll(h, 3 * L, 1), 0.0)
    gain, shift = gain[0:1], shift[0:1]
    stat_ref[...] = jnp.concatenate([mean, rstd, gain, shift, jnp.zeros((4, F), f32)], axis=0)
    cid = lax.broadcasted_iota(jnp.int32, (cols, F), 0)
    s = jnp.zeros((cols, F), f32)
    q = jnp.zeros((cols, F), f32)
    for i in range(slabs):
        rows = slice(i * cols, (i + 1) * cols)
        valid = cid < lim_ref[i]
        normed = (mixed_ref[rows] - mean) * rstd
        pre = gain * normed + shift
        sig, act = silu_parts(pre)
        out_ref[rows] = jnp.where(valid, act, 0.0).astype(bf16)
        dt = jnp.where(valid, grad_ref[rows].astype(f32) * slope(pre, sig), 0.0)
        dt_ref[rows] = dt
        s += dt
        q += dt * normed
    sums_ref[...] = column_sums(s, q)


def branch_kernel(
    lim_ref, n_ref, mixed_ref, fdt_ref, fstat_ref, conv_ref, act_ref, stat_ref, wbranch_ref, s0, s1, s2, s3,
    dt_ref, gproj_ref, image_ref, sums_ref, grad, *, slabs, cols, images
):
    F = mixed_ref.shape[1]
    W = conv_ref.shape[1]
    per = slabs // images
    mean, rstd, scale = fstat_ref[0:1], fstat_ref[1:2], fstat_ref[1:2] * fstat_ref[2:3]
    total = added((s0, s1, s2, s3)) / n_ref[0]
    beta, gamma = total[0:1], total[1:2]
    cid = lax.broadcasted_iota(jnp.int32, (cols, F), 0)
    image_sums = []
    for image in range(images):
        total = jnp.zeros((cols, F), f32)
        for i in range(image * per, (image + 1) * per):
            rows = slice(i * cols, (i + 1) * cols)
            normed = (mixed_ref[rows] - mean) * rstd
            g = jnp.where(cid < lim_ref[i], scale * (fdt_ref[rows] - beta - normed * gamma), 0.0)
            g = g.astype(bf16)
            grad[rows] = g
            total += g.astype(f32)
        image_sums.append(jnp.sum(total, axis=0, keepdims=True))
    image_ref[...] = jnp.concatenate(image_sums + [jnp.zeros((8 - images, F), f32)], axis=0)
    dt_ref[...] = dot(grad[...], wbranch_ref[...], NT)
    gproj_ref[...] = dot(act_ref[...], grad[...], TN)
    bmean, brstd, bgain, bshift = (stat_ref[i : i + 1] for i in range(4))
    cid = lax.broadcasted_iota(jnp.int32, (cols, W), 0)
    s = jnp.zeros((cols, W), f32)
    q = jnp.zeros((cols, W), f32)
    for i in range(slabs):
        rows = slice(i * cols, (i + 1) * cols)
        normed = (conv_ref[rows] - bmean) * brstd
        pre = bgain * normed + bshift
        sig, _ = silu_parts(pre)
        dt = jnp.where(cid < lim_ref[i], dt_ref[rows] * slope(pre, sig), 0.0)
        dt_ref[rows] = dt
        s += dt
        q += dt * normed
    sums_ref[...] = column_sums(s, q)


def grad_kernel(lim_ref, n_ref, dt_ref, conv_ref, stat_ref, sums_ref, piece_ref, cg_ref, scratch, *, slabs, cols):
    W = conv_ref.shape[1]
    mean, rstd, scale = stat_ref[0:1], stat_ref[1:2], stat_ref[1:2] * stat_ref[2:3]
    beta, gamma = sums_ref[0:1] / n_ref[0], sums_ref[1:2] / n_ref[0]
    cid = lax.broadcasted_iota(jnp.int32, (cols, W), 0)
    for i in range(slabs):
        rows = slice(i * cols, (i + 1) * cols)
        normed = (conv_ref[rows] - mean) * rstd
        g = scale * (dt_ref[rows] - beta - normed * gamma)
        scratch[rows] = jnp.where(cid < lim_ref[i], g, 0.0)
    cg_ref[:W] = scratch[...].T.astype(bf16)
    F = piece_ref.shape[1]
    for k in range(piece_ref.shape[0] // 16):
        cg_ref[W:, k * F : (k + 1) * F] = piece_ref[k * 16 : (k + 1) * 16].astype(bf16)


def shifted(f, v, d, col, cols):
    if v == 1:
        return f
    if v == 2:
        return jnp.where(col >= d, pltpu.roll(f, d, 1), 0.0)
    return jnp.where(col < cols - d, pltpu.roll(f, f.shape[1] - d, 1), 0.0)


def expand_kernel(col_ref, cg_ref, out_ref, *, cols, rates):
    L = cg_ref.shape[0] // 4
    for j in range(3):
        raw = cg_ref[(j + 1) * L : (j + 2) * L]
        f = raw.astype(f32)
        col = jnp.broadcast_to(col_ref[0:1], f.shape)
        base = 3 * j * L
        out_ref[base : base + L] = shifted(f, 0, rates[j], col, cols).astype(bf16)
        out_ref[base + L : base + 2 * L] = raw
        out_ref[base + 2 * L : base + 3 * L] = shifted(f, 2, rates[j], col, cols).astype(bf16)
    out_ref[9 * L :] = cg_ref[:L]


def fetch_blocks(pos, blocks, dest, sems, lanes=False):
    copies = []
    for d, ref in enumerate(blocks):
        place = pos ^ d
        if lanes:
            cells = ref.shape[1]
            spot = dest.at[:, pl.ds(pl.multiple_of(place * cells, 128), cells)]
        else:
            spot = dest.at[place]
        source = ref if lanes else ref.at[pl.ds(0, dest.shape[1])]
        copies.append(pltpu.make_async_copy(source, spot, sems.at[d]))
    for c in copies:
        c.start()
    return copies


def tap_products(store, taps, x_rows, L):
    cells = taps.shape[1] // BLOCKS
    own_row = dot(taps[...], x_rows(0, BLOCKS), NN)
    for j in range(3):
        lo = (j * 3 + 1) * 3 * L
        store(lo, own_row[3 * j * L : 3 * (j + 1) * L])
    store(27 * L, own_row[9 * L :])
    for j in range(3):
        rows = slice(3 * j * L, 3 * (j + 1) * L)
        span = (BLOCKS - 1 - j) * cells
        far = (j + 1) * cells
        store(j * 9 * L, dot(taps[rows, far:], x_rows(0, BLOCKS - 1 - j), NN))
        store((j * 3 + 2) * 3 * L, dot(taps[rows, :span], x_rows(j + 1, BLOCKS), NN))


def narrow_kernel(pos_ref, *refs, parts):
    blocks, (x_ref, out_ref, taps, x, sems, xsems) = refs[:BLOCKS], refs[BLOCKS:]
    pos, ch = pos_ref[0], pos_ref[2]
    L = taps.shape[0] // 10
    cells = taps.shape[1] // BLOCKS
    rows = x_ref.shape[2]
    copies = fetch_blocks(pos, blocks, taps, sems, lanes=True)
    for e in range(parts):
        for d in range(BLOCKS):
            place = pl.ds(pl.multiple_of((pos ^ d) * cells + (ch ^ e) * rows, 16), rows)
            c = pltpu.make_async_copy(x_ref.at[e, d], x.at[place], xsems.at[e, d])
            c.start()
            copies.append(c)
    for c in copies:
        c.wait()

    def store(lo, value):
        out_ref[lo : lo + value.shape[0]] = value.astype(bf16)

    tap_products(store, taps, lambda lo, hi: x[lo * cells : hi * cells], L)


def wide_kernel(pos_ref, x_ref, *refs):
    blocks, pieces, (acc_ref, point_ref, proj_ref, taps, sems) = (
        refs[:BLOCKS],
        refs[BLOCKS : 2 * BLOCKS],
        refs[2 * BLOCKS :],
    )
    L = point_ref.shape[0]
    F = proj_ref.shape[1]
    rows = proj_ref.shape[0] // BLOCKS

    @pl.when(pl.program_id(0) == 0)
    def _():
        copies = fetch_blocks(pos_ref[0], blocks, taps, sems, lanes=True)
        for d in range(BLOCKS):
            p = pos_ref[0] ^ d
            base = (p % 2 * (BLOCKS // 2) + p // 2) * rows
            for k in range(0, rows, 16):
                n = min(16, rows - k)
                value = pieces[d][:, k // 16 * F : (k // 16 + 1) * F].astype(f32)
                proj_ref[pl.ds(pl.multiple_of(base + k, 8), n)] = value[:n]
        for c in copies:
            c.wait()

    def store(lo, value):
        if lo < 27 * L:
            acc_ref[lo : lo + value.shape[0]] = value
        else:
            point_ref[...] = value

    w = x_ref.shape[3]
    tap_products(store, taps, lambda lo, hi: x_ref[lo:hi, 0].reshape(-1, w), L)


def widen_kernel(in_ref, pin_ref, keep_ref, pkeep_ref, out_ref, pout_ref):
    w = in_ref.shape[2]
    for s in range(BLOCKS):
        out_ref[:, s * w : (s + 1) * w] = in_ref[s].astype(f32)
        pout_ref[:, s * w : (s + 1) * w] = pin_ref[s].astype(f32)


def input_grad_kernel(pos_ref, lim_ref, col_ref, w_ref, wp_ref, pool_ref, *refs, slabs, cols, rates, images):
    blocks, (keep_ref, give_ref, cg, lhs, rhs, sems) = refs[:BLOCKS], refs[BLOCKS:]
    L = wp_ref.shape[0]
    s = pos_ref[0]

    @pl.when(pl.program_id(0) == 0)
    def _():
        for c in fetch_blocks(s, blocks, cg, sems):
            c.wait()
        pieces = []
        order = [(j, u, v) for j in range(3) for u in range(3) for v in range(3)] + [None]
        for i, tap in enumerate(order):
            if tap is None:
                pieces.append(cg[s, 0:L].astype(f32))
            else:
                j, u, v = tap
                b = s - (u - 1) * (j + 1)
                inside = ((b >= 0) & (b < BLOCKS)).astype(f32)
                f = cg[jnp.clip(b, 0, BLOCKS - 1), (j + 1) * L : (j + 2) * L].astype(f32) * inside
                col = jnp.broadcast_to(col_ref[0:1], f.shape)
                pieces.append(shifted(f, v, rates[j], col, cols))
            if i % 4 == 3:
                lhs[:, (i - 3) * L : (i + 1) * L] = jnp.concatenate(pieces, axis=0).T.astype(bf16)
                pieces = []

    rhs[: 27 * L] = w_ref[...]
    rhs[27 * L :] = wp_ref[...]
    width = keep_ref.shape[2]
    per = slabs // images
    cid = lax.broadcasted_iota(jnp.int32, (cols, 256), 0)

    def fill(out_ref):
        for n in range(0, width, 256):
            part = dot(lhs[...], rhs[:, n : n + 256], NN)
            for i in range(slabs):
                value = part[i * cols : (i + 1) * cols] + pool_ref[i // per : i // per + 1, n : n + 256]
                out_ref[0, i * cols : (i + 1) * cols, n : n + 256] = jnp.where(
                    cid < lim_ref[i], value, 0.0
                ).astype(bf16)

    @pl.when(pl.program_id(0) % 2 == 0)
    def _():
        fill(keep_ref)

    @pl.when(pl.program_id(0) % 2 == 1)
    def _():
        fill(give_ref)


def grouped(pairs, size):
    return [(g * BLOCKS + a, g * BLOCKS + b) for g in range(size // BLOCKS) for a, b in pairs]


def neighbours(first, second, axis, distance):
    size = lax.axis_size(axis)
    rounds = []
    for parity, block in ((0, first), (1, second)):
        lows = [a for a in range(BLOCKS - distance) if (a // distance) % 2 == parity]
        pairs = [(a, a + distance) for a in lows] + [(a + distance, a) for a in lows]
        rounds.append(lax.ppermute(block, axis, grouped(pairs, size)))
    return rounds


def swap(block, axis, bits):
    return lax.ppermute(block, axis, [(i, i ^ bits) for i in range(lax.axis_size(axis))])


def parts_over_sp(x):
    x = x + swap(x, "sp", 1)
    return [x] + [swap(x, "sp", b) for b in (2, 4, 6)]


def swaps_over_sp(x):
    blocks = [x, None] + [swap(x, "sp", b) if b % 2 == 0 else None for b in range(2, BLOCKS)]
    for b in range(1, BLOCKS, 2):
        blocks[b] = swap(blocks[b - 1], "sp", 1)
    return blocks


def after(x, *others):
    return lax.optimization_barrier((x, others))[0]


def thirds(x):
    hi = lax.reduce_precision(x, 8, 7)
    mid = lax.reduce_precision(x - hi, 8, 7)
    return jnp.concatenate([hi, mid, x - hi - mid], axis=0).astype(bf16)


def whole(parts):
    hi, mid, low = jnp.split(parts.astype(f32), 3, axis=0)
    return hi + mid + low


def plain_from_behind(block, axis, distance):
    devices = range(lax.axis_size(axis))
    route = [(i - distance, i) for i in devices if i - distance in devices]
    return lax.ppermute(block, axis, route)


def shift_cols(values, offset):
    margin = abs(offset)
    padded = jnp.pad(values, ((0, 0), (0, 0), (margin, margin), (0, 0)))
    return lax.slice_in_dim(padded, margin + offset, margin + offset + values.shape[2], axis=2)


def silu_slope(pre_act):
    sigmoid_val = jax.nn.sigmoid(pre_act)
    return sigmoid_val * (1.0 + pre_act * (1.0 - sigmoid_val))


def source_inside(block_id, shift_amount):
    source = block_id - shift_amount
    return (source >= 0) & (source < BLOCKS)


def move_features(values, shift_amount):
    return plain_from_behind(values, "sp", shift_amount)


def shifted_gradients(values, shift_amount):
    return plain_from_behind(values, "sp", shift_amount)


def tap_partials(source, weight_taps, dilation_rate):
    count_k, rows_dev, grid_width, channel_total = source.shape
    local_output = weight_taps.shape[1]
    products = jnp.einsum(
        "pc,tc->pt",
        source.reshape(-1, channel_total),
        weight_taps.reshape(3 * local_output, channel_total),
        preferred_element_type=jnp.float32,
    ).reshape(count_k, rows_dev, grid_width, 3, local_output)
    return (
        shift_cols(products[:, :, :, 0, :], -dilation_rate)
        + products[:, :, :, 1, :]
        + shift_cols(products[:, :, :, 2, :], dilation_rate)
    )


def plain_body(
    features, heights, widths, w_point, atrous_weight, w_pool, w_proj, bn_gains, bn_shifts, out_grad
):
    count_k, rows_dev, grid_width, channel_total = features.shape
    local_output = w_point.shape[0]
    full_out = w_proj.shape[2]
    groups = heights.shape[1]
    images = count_k * groups
    pixels = count_k * rows_dev * grid_width
    position = lax.axis_index("sp")
    block_id = position % BLOCKS
    group_id = position // BLOCKS
    channel_start = lax.axis_index("ch") * local_output
    own_out_grad = lax.dynamic_slice_in_dim(out_grad, channel_start, local_output, 3)
    group_pick = jnp.arange(groups, dtype=jnp.int32) == group_id
    group_onehot = group_pick.astype(jnp.float32)
    own_heights = jnp.sum(jnp.where(group_pick[None, :], heights, 0), axis=1)
    own_widths = jnp.sum(jnp.where(group_pick[None, :], widths, 0), axis=1)
    row_ids = block_id * rows_dev + jnp.arange(rows_dev, dtype=jnp.int32)
    col_ids = jnp.arange(grid_width, dtype=jnp.int32)
    inside = (row_ids[None, :, None] < own_heights[:, None, None]) & (
        col_ids[None, None, :] < own_widths[:, None, None]
    )
    pix_mask = inside.astype(jnp.float32)[..., None]
    valid_count = jnp.sum((heights * widths).astype(jnp.float32))
    own_count = (own_heights * own_widths).astype(jnp.float32)
    masked_values = features * pix_mask.astype(jnp.bfloat16)
    flat_pix = masked_values.reshape(pixels, channel_total)
    point_conv = jnp.einsum("pc,fc->pf", flat_pix, w_point, preferred_element_type=jnp.float32)
    conv_list = [point_conv.reshape(count_k, rows_dev, grid_width, local_output)]
    for dilation_index, dilation_factor in enumerate(dilation_factors):
        dilation_rate = rows_dev * dilation_factor
        running_total = tap_partials(masked_values, atrous_weight[dilation_index, 1], dilation_rate)
        for row_offset_tap in (0, 2):
            shift_amount = (1 - row_offset_tap) * dilation_factor
            keep_rows = source_inside(block_id, shift_amount)
            received_part = move_features(masked_values, shift_amount) * keep_rows.astype(
                jnp.bfloat16
            )
            running_total = running_total + tap_partials(
                received_part, atrous_weight[dilation_index, row_offset_tap], dilation_rate
            )
        conv_list.append(running_total)
    conv_out = jnp.stack(conv_list)
    stat_sum, stat_square = lax.psum(
        (
            jnp.sum(conv_out * pix_mask, axis=(1, 2, 3)),
            jnp.sum(conv_out * conv_out * pix_mask, axis=(1, 2, 3)),
        ),
        "sp",
    )
    branch_mean = stat_sum / valid_count
    branch_inv = lax.rsqrt(stat_square / valid_count - branch_mean * branch_mean + epsilon)
    normed = (conv_out - branch_mean[:, None, None, None, :]) * branch_inv[:, None, None, None, :]
    pre_act = bn_gains[:4][:, None, None, None, :] * normed + bn_shifts[:4][:, None, None, None, :]
    branch_act = (pix_mask * jax.nn.silu(pre_act)).astype(jnp.bfloat16)
    own_sums = jnp.sum(masked_values, axis=(1, 2), dtype=jnp.float32)
    own_pooled = own_sums / own_count[:, None]
    pool_weight = w_pool.astype(jnp.float32)
    pooled = lax.psum(own_pooled[:, None, :] * group_onehot[None, :, None], "sp")
    projected = jnp.dot(
        pooled.reshape(images, channel_total), pool_weight.T, precision=highest_precision
    )
    pool_mean = jnp.mean(projected, axis=0)
    pool_inv = lax.rsqrt(jnp.mean(projected * projected, axis=0) - pool_mean * pool_mean + epsilon)
    pool_normed = (projected - pool_mean) * pool_inv
    pool_pre = bn_gains[4] * pool_normed + bn_shifts[4]
    pool_act = jax.nn.silu(pool_pre).astype(jnp.bfloat16)
    own_act = jnp.sum(
        pool_act.astype(jnp.float32).reshape(count_k, groups, local_output)
        * group_onehot[None, :, None],
        axis=1,
    )
    pool_pixels = (own_act[:, None, None, :] * pix_mask).astype(jnp.bfloat16)
    stacked = jnp.concatenate([branch_act, pool_pixels[None]], axis=0).reshape(
        5, pixels, local_output
    )
    partial_value = jnp.einsum("bpf,bfo->po", stacked, w_proj, preferred_element_type=jnp.float32)
    mixed_sum = lax.psum_scatter(
        partial_value.reshape(count_k, rows_dev, grid_width, full_out),
        "ch",
        scatter_dimension=3,
        tiled=True,
    )
    final_sum, final_square = lax.psum(
        (
            jnp.sum(mixed_sum * pix_mask, axis=(0, 1, 2)),
            jnp.sum(mixed_sum * mixed_sum * pix_mask, axis=(0, 1, 2)),
        ),
        "sp",
    )
    final_mean = final_sum / valid_count
    final_inv = lax.rsqrt(final_square / valid_count - final_mean * final_mean + epsilon)
    final_normed = (mixed_sum - final_mean) * final_inv
    final_pre = bn_gains[5] * final_normed + bn_shifts[5]
    output = (pix_mask * jax.nn.silu(final_pre)).astype(jnp.bfloat16)
    final_dt = pix_mask * own_out_grad.astype(jnp.float32) * silu_slope(final_pre)
    final_beta, final_gamma = lax.psum(
        (jnp.sum(final_dt, axis=(0, 1, 2)), jnp.sum(final_dt * final_normed, axis=(0, 1, 2))), "sp"
    )
    mixed_grad = (
        pix_mask
        * final_inv
        * bn_gains[5]
        * (final_dt - final_beta / valid_count - final_normed * final_gamma / valid_count)
    ).astype(jnp.bfloat16)
    full_grad = lax.all_gather(mixed_grad, "ch", axis=3, tiled=True).reshape(pixels, full_out)
    g_proj = jnp.einsum("bpf,po->bfo", stacked, full_grad, preferred_element_type=jnp.float32)
    act_grads = jnp.einsum(
        "po,bfo->bpf", full_grad, w_proj, preferred_element_type=jnp.float32
    ).reshape(5, count_k, rows_dev, grid_width, local_output)
    branch_dt = pix_mask * act_grads[:4] * silu_slope(pre_act)
    pool_own_grad = jnp.sum(act_grads[4] * pix_mask, axis=(1, 2))
    branch_beta, branch_gamma, pool_grad = lax.psum(
        (
            jnp.sum(branch_dt, axis=(1, 2, 3)),
            jnp.sum(branch_dt * normed, axis=(1, 2, 3)),
            pool_own_grad[:, None, :] * group_onehot[None, :, None],
        ),
        "sp",
    )
    convolution_gradients = (
        pix_mask
        * branch_inv[:, None, None, None, :]
        * bn_gains[:4][:, None, None, None, :]
        * (
            branch_dt
            - branch_beta[:, None, None, None, :] / valid_count
            - normed * branch_gamma[:, None, None, None, :] / valid_count
        )
    ).astype(jnp.bfloat16)
    pool_dt = pool_grad.reshape(images, local_output) * silu_slope(pool_pre)
    pool_beta = jnp.sum(pool_dt, axis=0)
    pool_gamma = jnp.sum(pool_dt * pool_normed, axis=0)
    proj_grad = (
        pool_inv * bn_gains[4] * (pool_dt - pool_beta / images - pool_normed * pool_gamma / images)
    )
    own_proj_grad = jnp.sum(
        proj_grad.reshape(count_k, groups, local_output) * group_onehot[None, :, None], axis=1
    )
    g_pool = jnp.einsum("kf,kc->fc", own_proj_grad, own_pooled, precision=highest_precision)
    pooled_grad = (
        jnp.einsum("kf,fc->kc", own_proj_grad, pool_weight, precision=highest_precision)
        / own_count[:, None]
    )
    point_grad = convolution_gradients[0].reshape(pixels, local_output)
    g_point = jnp.einsum("pf,pc->fc", point_grad, flat_pix, preferred_element_type=jnp.float32)
    input_term = jnp.einsum("pf,fc->pc", point_grad, w_point, preferred_element_type=jnp.float32)
    input_term = (
        input_term.reshape(count_k, rows_dev, grid_width, channel_total)
        + pooled_grad[:, None, None, :]
    )
    atrous_list = []
    for dilation_index, dilation_factor in enumerate(dilation_factors):
        dilation_rate = rows_dev * dilation_factor
        tap_list = []
        for row_offset_tap in range(3):
            shift_amount = (row_offset_tap - 1) * dilation_factor
            if shift_amount == 0:
                received_part = convolution_gradients[dilation_index + 1]
            else:
                received_part = shifted_gradients(
                    convolution_gradients[dilation_index + 1], shift_amount
                ) * source_inside(block_id, shift_amount).astype(jnp.bfloat16)
            spread = jnp.stack(
                [
                    shift_cols(received_part, dilation_rate),
                    received_part,
                    shift_cols(received_part, -dilation_rate),
                ],
                axis=3,
            ).reshape(pixels, 3 * local_output)
            tap_list.append(
                jnp.einsum(
                    "pt,pc->tc", spread, flat_pix, preferred_element_type=jnp.float32
                ).reshape(3, local_output, channel_total)
            )
            tap_weight_slice = atrous_weight[dilation_index, row_offset_tap].reshape(
                3 * local_output, channel_total
            )
            input_term = input_term + jnp.einsum(
                "pt,tc->pc", spread, tap_weight_slice, preferred_element_type=jnp.float32
            ).reshape(count_k, rows_dev, grid_width, channel_total)
        atrous_list.append(jnp.stack(tap_list))
    g_atrous = jnp.stack(atrous_list)
    in_grad = lax.psum_scatter(
        (input_term * pix_mask).astype(jnp.bfloat16), "ch", scatter_dimension=3, tiled=True
    )
    g_point, g_atrous, g_proj, g_pool = (
        lax.psum(g_point.astype(jnp.bfloat16), "sp").astype(jnp.float32),
        lax.psum(g_atrous.astype(jnp.bfloat16), "sp").astype(jnp.float32),
        lax.psum(g_proj.astype(jnp.bfloat16), "sp").astype(jnp.float32),
        lax.psum(g_pool.astype(jnp.bfloat16), "sp").astype(jnp.float32),
    )
    g_gains = jnp.concatenate([branch_gamma, pool_gamma[None], final_gamma[None]], axis=0)
    g_shifts = jnp.concatenate([branch_beta, pool_beta[None], final_beta[None]], axis=0)
    return (output, in_grad, g_point, g_atrous, g_pool, g_proj, g_gains, g_shifts)


def body(
    features, heights, widths, w_point, atrous_weight, w_pool, w_proj, bn_gains, bn_shifts, out_grad
):
    images, rows_dev, cols, C = features.shape
    L = w_point.shape[0]
    if lax.axis_size("sp") != BLOCKS or lax.axis_size("ch") != 4 or L != 64:
        return plain_body(
            features, heights, widths, w_point, atrous_weight, w_pool, w_proj, bn_gains, bn_shifts, out_grad
        )
    F = w_proj.shape[2]
    W = BRANCHES * L
    slabs = images * rows_dev
    cells = slabs * cols
    rates = tuple(rows_dev * f for f in dilation_factors)
    block_id = lax.axis_index("sp")
    own = lax.axis_index("ch")
    h, w = heights[:, 0], widths[:, 0]
    row_ids = block_id * rows_dev + jnp.arange(rows_dev, dtype=jnp.int32)
    lim = jnp.where(row_ids[None, :] < h[:, None], w[:, None], 0).reshape(slabs)
    own_count = (h * w).astype(f32)
    n = jnp.sum(own_count)
    x = features.reshape(cells, C)
    og = out_grad.reshape(cells, F)

    norms = jnp.concatenate([bn_gains, bn_shifts, jnp.zeros((4, L), f32)], axis=0).reshape(4, W)
    wp = w_proj.reshape(5 * L, F)
    packed = jnp.concatenate([wp, thirds(norms), jnp.zeros((4, F), bf16)], axis=0)
    packed_y = swap(packed, "ch", 2)
    packed_core = swap(packed, "ch", 1)
    packed_all = [packed, packed_core, packed_y, swap(packed_y, "ch", 1)]
    count = n.reshape(1)
    own_id = own.astype(jnp.int32).reshape(1)

    KT = 512
    steps = C // KT
    x_spec = pl.BlockSpec((cells, KT), lambda k: (0, k))
    first = [(1 - (block_id // f) % 2).astype(jnp.int32) for f in dilation_factors]

    def side_taps(which, x):
        out = pl.pallas_call(
            functools.partial(
                side_kernel, steps=steps, slabs=slabs, cols=cols, rates=tuple(rates[j] for j in which)
            ),
            grid=(steps,),
            in_specs=[SMEM, SMEM, x_spec]
            + [
                pl.BlockSpec((1, 1, 3, L, KT), lambda k, j=j, u=u: (j, u, 0, 0, k))
                for j in which
                for u in (0, 2)
            ],
            out_specs=[pl.BlockSpec((cells // 2, 2 * L), lambda k: (0, 0))] * (2 * len(which)),
            out_shape=[jax.ShapeDtypeStruct((cells // 2, 2 * L), bf16)] * (2 * len(which)),
            scratch_shapes=[
                pltpu.VMEM((6 * len(which) * L, KT), bf16),
                pltpu.VMEM((cells, 6 * len(which) * L), f32),
            ],
            compiler_params=params(),
            cost_estimate=cost(2 * cells * C * 6 * len(which) * L, 10e6),
            name="side_taps",
        )(lim, jnp.stack([first[j] for j in which]), x, *[atrous_weight] * (2 * len(which)))
        out = after(tuple(out), packed_y, packed_core)
        moved = []
        for i, j in enumerate(which):
            moved += neighbours(out[2 * i], out[2 * i + 1], "sp", dilation_factors[j])
        return moved, out[0]

    narrow = C // 2
    valid = (jnp.arange(cols, dtype=jnp.int32)[None, :] < lim[:, None]).reshape(cells, 1)
    cut = narrow // BLOCKS
    part = cells // images
    image = lax.dynamic_slice(x, (own * part, 0), (part, narrow))
    image = jnp.where(lax.dynamic_slice_in_dim(valid, own * part, part), image, jnp.zeros((), bf16))
    column = block_id // 2
    sent = [lax.dynamic_slice_in_dim(image, (column ^ dz) * 2 * cut, 2 * cut, 1) for dz in range(4)]
    mine = jnp.stack([sent[0]] + [swap(sent[dz], "sp", 2 * dz) for dz in (1, 2, 3)])
    wide_w = (C - narrow) // 4
    own_wide = lax.dynamic_slice_in_dim(x, narrow + own * wide_w, wide_w, 1)
    own_wide = jnp.where(valid, own_wide, jnp.zeros((), bf16))
    halo, made = side_taps((0, 1, 2), after(x, packed, own_wide, *sent))
    x_wide = lax.all_gather(own_wide, ("sp", "ch"), axis=0).reshape(BLOCKS, 4, cells, wide_w)
    x_then = after(x, made, halo[0], halo[1], mine)
    centre, sums = pl.pallas_call(
        functools.partial(centre_kernel, steps=steps, slabs=slabs, cols=cols, rates=rates, images=images),
        grid=(steps,),
        in_specs=[
            SMEM,
            x_spec,
            pl.BlockSpec((3, 1, 3, L, KT), lambda k: (0, 1, 0, 0, k)),
            pl.BlockSpec((L, KT), lambda k: (0, k)),
        ],
        out_specs=[pl.BlockSpec((cells, W), lambda k: (0, 0)), pl.BlockSpec((8, KT), lambda k: (0, k))],
        out_shape=[jax.ShapeDtypeStruct((cells, W), f32), jax.ShapeDtypeStruct((8, C), f32)],
        scratch_shapes=[pltpu.VMEM((10 * L, KT), bf16), pltpu.VMEM((cells, 10 * L), f32)],
        compiler_params=params(),
        cost_estimate=cost(2 * cells * C * 10 * L, 8e6),
        name="centre_taps",
    )(lim, x_then, atrous_weight, w_point)
    own_pooled = sums[:images] / own_count[:, None]
    proj_part = lax.dot_general(own_pooled, w_pool.astype(f32), NT, precision=highest_precision)

    extra = jnp.concatenate(
        [jnp.pad(proj_part, ((4, 4 - images), (0, W - L))), own_pooled.reshape(-1, W)], axis=0
    )
    conv, conv_send, message, local = pl.pallas_call(
        functools.partial(combine_kernel, slabs=slabs, cols=cols),
        in_specs=[SMEM] + [VMEM] * 8,
        out_specs=[VMEM] * 4,
        out_shape=[
            jax.ShapeDtypeStruct((cells, W), f32),
            jax.ShapeDtypeStruct((cells, W), bf16),
            jax.ShapeDtypeStruct(extra.shape, f32),
            jax.ShapeDtypeStruct((8, W), f32),
        ],
        compiler_params=params(20),
        cost_estimate=cost(2e6, 4e6),
        name="combine_taps",
    )(lim, centre, *halo, extra)
    conv_y = swap(conv_send, "ch", 2)
    conv_core = swap(conv_send, "ch", 1)
    message = parts_over_sp(message)
    conv_diag = swap(after(conv_y, *message), "ch", 1)
    tile = ((message[0][:8] + message[1][:8]) + (message[2][:8] + message[3][:8])) + local
    mine = after(mine, tile)
    keep = lax.dynamic_slice_in_dim(mine, (block_id % 2) * cut, cut, 2)
    give = lax.dynamic_slice_in_dim(mine, (1 - block_id % 2) * cut, cut, 2)
    taken = swap(give, "sp", 1)
    tiles = [tile] + [swap(tile, "ch", b) for b in (1, 2, 3)]
    projected = tile[4 : 4 + images, :L]
    pool_mean = jnp.mean(projected, axis=0)
    pool_rstd = lax.rsqrt(jnp.mean(projected * projected, axis=0) - pool_mean * pool_mean + epsilon)
    pool_normed = (projected - pool_mean) * pool_rstd
    pool_pre = bn_gains[4] * pool_normed + bn_shifts[4]
    pool_act = jax.nn.silu(pool_pre).astype(bf16)

    mixed, act, mixed_stat, own_stat = pl.pallas_call(
        functools.partial(mix_kernel, slabs=slabs, cols=cols, images=images),
        in_specs=[SMEM] * 2 + [VMEM] * 12,
        out_specs=[VMEM] * 4,
        out_shape=[
            jax.ShapeDtypeStruct((cells, F), f32),
            jax.ShapeDtypeStruct((cells, W), bf16),
            jax.ShapeDtypeStruct((8, F), f32),
            jax.ShapeDtypeStruct((8, W), f32),
        ],
        scratch_shapes=[pltpu.VMEM((cells, W), bf16)],
        compiler_params=params(20),
        cost_estimate=cost(2 * cells * 4 * W * F, 6e6),
        name="mix_branches",
    )(lim, count, conv, conv_core, conv_y, conv_diag, *tiles, *packed_all)
    total = parts_over_sp(mixed_stat)
    out_all, fdt, fsums, fstat = pl.pallas_call(
        functools.partial(final_kernel, slabs=slabs, cols=cols),
        in_specs=[SMEM] * 3 + [VMEM] * 10,
        out_specs=[VMEM] * 4,
        out_shape=[
            jax.ShapeDtypeStruct((cells, F), bf16),
            jax.ShapeDtypeStruct((cells, F), f32),
            jax.ShapeDtypeStruct((8, F), f32),
            jax.ShapeDtypeStruct((8, F), f32),
        ],
        compiler_params=params(20),
        cost_estimate=cost(2e6, 4e6),
        name="final_norm",
    )(lim, count, own_id, mixed, og, *packed_all, *total)
    ftotal = parts_over_sp(fsums)
    final_sums = (ftotal[0] + ftotal[1]) + (ftotal[2] + ftotal[3])
    final_beta, final_gamma = final_sums[0], final_sums[1]
    dt, gproj, image_sums, bsums = pl.pallas_call(
        functools.partial(branch_kernel, slabs=slabs, cols=cols, images=images),
        in_specs=[SMEM] * 2 + [VMEM] * 11,
        out_specs=[VMEM] * 4,
        out_shape=[
            jax.ShapeDtypeStruct((cells, W), f32),
            jax.ShapeDtypeStruct((W, F), f32),
            jax.ShapeDtypeStruct((8, F), f32),
            jax.ShapeDtypeStruct((8, W), f32),
        ],
        scratch_shapes=[pltpu.VMEM((cells, F), bf16)],
        compiler_params=params(20),
        cost_estimate=cost(4 * cells * W * F, 8e6),
        name="branch_grads",
    )(
        lim, count, mixed, fdt, fstat, conv, act, own_stat, wp[:W], *ftotal
    )
    image_sums = image_sums[:images]
    pool_part = lax.dot_general(image_sums, w_proj[4].astype(f32), NT, precision=highest_precision)
    gproj_pool = lax.dot_general(pool_act.astype(f32), image_sums, TN, precision=highest_precision)
    gp = jnp.concatenate([gproj, gproj_pool], axis=0)
    across, along = block_id % 2, block_id // 2
    gp_half, gp_piece = gp.shape[0] // 2, gp.shape[0] // BLOCKS
    bown = jnp.concatenate([bsums[:4], jnp.pad(pool_part, ((0, 0), (0, W - L)))], axis=0)
    got = swap(
        jnp.concatenate(
            [thirds(bown), lax.dynamic_slice_in_dim(gp, (1 - across) * gp_half, gp_half).astype(bf16)], axis=0
        ),
        "sp",
        1,
    )
    bown = bown + whole(got[:24])
    gp = lax.dynamic_slice_in_dim(gp, across * gp_half, gp_half) + got[24:].astype(f32)
    mine_thirds = thirds(bown)
    got = [
        swap(
            jnp.concatenate(
                [mine_thirds, lax.dynamic_slice_in_dim(gp, (along ^ dz) * gp_piece, gp_piece).astype(bf16)],
                axis=0,
            ),
            "sp",
            2 * dz,
        )
        for dz in (1, 2, 3)
    ]
    btile = (bown + whole(got[0][:24])) + (whole(got[1][:24]) + whole(got[2][:24]))
    gp = lax.dynamic_slice_in_dim(gp, along * gp_piece, gp_piece)
    gp = (gp + got[0][24:].astype(f32)) + (got[1][24:].astype(f32) + got[2][24:].astype(f32))
    gp = jnp.pad(gp, ((0, -gp_piece % 16), (0, 0)))
    branch_beta, branch_gamma = btile[0], btile[1]
    cgt = pl.pallas_call(
        functools.partial(grad_kernel, slabs=slabs, cols=cols),
        in_specs=[SMEM] * 2 + [VMEM] * 5,
        out_specs=VMEM,
        out_shape=jax.ShapeDtypeStruct((W + 16, cells), bf16),
        scratch_shapes=[pltpu.VMEM((cells, W), f32)],
        compiler_params=params(20),
        cost_estimate=cost(2e6, 4e6),
        name="conv_grads",
    )(lim, count, dt, conv, own_stat, btile, gp)
    pool_dt = btile[4 : 4 + images, :L] * silu_slope(pool_pre)
    pool_beta = jnp.sum(pool_dt, axis=0)
    pool_gamma = jnp.sum(pool_dt * pool_normed, axis=0)
    proj_grad = (
        pool_rstd * bn_gains[4] * (pool_dt - pool_beta / images - pool_normed * pool_gamma / images)
    )
    g_gains = jnp.concatenate([branch_gamma.reshape(4, L), pool_gamma[None],
        lax.dynamic_slice_in_dim(final_gamma, own * L, L)[None]], axis=0)
    g_shifts = jnp.concatenate([branch_beta.reshape(4, L), pool_beta[None],
        lax.dynamic_slice_in_dim(final_beta, own * L, L)[None]], axis=0)
    output = lax.dynamic_slice_in_dim(out_all, own * L, L, 1).reshape(images, rows_dev, cols, L)
    pooled_grad = (
        jnp.einsum("kf,fc->kc", proj_grad, w_pool.astype(f32), precision=highest_precision)
        / own_count[:, None]
    )
    ANY = pl.BlockSpec(memory_space=pl.ANY)
    col_row = jnp.broadcast_to((jnp.arange(cells, dtype=jnp.int32) % cols)[None, :], (8, cells))
    pos = jnp.stack([block_id, own % 2, own]).astype(jnp.int32)
    def column_taps(block):
        return pl.pallas_call(
            functools.partial(expand_kernel, cols=cols, rates=rates),
            grid=(1,),
            in_specs=[pl.BlockSpec((8, cells), lambda i: (0, 0)), pl.BlockSpec((W, cells), lambda i: (0, 0))],
            out_specs=pl.BlockSpec((10 * L, cells), lambda i: (0, 0)),
            out_shape=jax.ShapeDtypeStruct((10 * L, cells), bf16),
            compiler_params=params(),
            cost_estimate=cost(1e9, 6e6),
            name="column_taps",
        )(col_row, block)

    near = [swap(cgt, "sp", b) for b in (2, 4)]
    near.append(swap(after(cgt, near[1]), "sp", 6))
    pair = swap(cgt, "sp", 1)
    taps = [column_taps(cgt), column_taps(pair), column_taps(near[0])]
    near_pair = swap(near[0], "sp", 1)
    taps.append(column_taps(near_pair))
    message = after(tuple(message), pair)
    pooled = ((message[0][8:] + message[1][8:]) + (message[2][8:] + message[3][8:])).reshape(images, C)
    x_slices = after(jnp.stack([keep, taken], axis=1).reshape(1, BLOCKS, part, cut), pair)
    x_slices = jnp.concatenate([x_slices, swap(x_slices, "ch", 2)], axis=0)
    x_core = swap(x_slices, "ch", 1)
    x_slices = jnp.stack([x_slices[0], x_core[0], x_slices[1], x_core[1]])
    g_pool = jnp.einsum("kf,kc->fc", proj_grad, pooled, precision=highest_precision)
    far = [after(near[1], *taps[:2], output, g_pool, g_gains, g_shifts, pooled_grad), after(near[2], *taps)]
    far_pairs = [swap(t, "sp", 1) for t in far]
    blocks = [cgt, pair, near[0], near_pair, far[0], far_pairs[0], far[1], far_pairs[1]]
    taps += [column_taps(t) for t in blocks[4:]]
    eighth = narrow // BLOCKS
    tap_scratch = pltpu.VMEM((10 * L, BLOCKS * cells), bf16)
    gw = pl.pallas_call(
        functools.partial(narrow_kernel, parts=images),
        in_specs=[SMEM] + [ANY] * (BLOCKS + 1),
        out_specs=pl.BlockSpec((28 * L, eighth), lambda i: (0, 0)),
        grid=(1,),
        out_shape=jax.ShapeDtypeStruct((28 * L, eighth), bf16),
        scratch_shapes=[
            tap_scratch,
            pltpu.VMEM((BLOCKS * cells, eighth), bf16),
            pltpu.SemaphoreType.DMA((BLOCKS,)),
            pltpu.SemaphoreType.DMA((images, BLOCKS)),
        ],
        compiler_params=params(),
        cost_estimate=cost(2 * cells * BLOCKS * 28 * L * eighth, 12e6),
        name="narrow_weight_grads",
    )(pos, *taps, x_slices)
    gw_all = lax.all_gather(gw, "sp", axis=0)
    pos, gw = lax.optimization_barrier((pos, gw))
    group = C // 4
    ig_keep, ig_give = pl.pallas_call(
        functools.partial(input_grad_kernel, slabs=slabs, cols=cols, rates=rates, images=images),
        grid_spec=pltpu.PrefetchScalarGridSpec(
            num_scalar_prefetch=2,
            grid=(4,),
            in_specs=[
                pl.BlockSpec((8, cells), lambda i, p, l: (0, 0)),
                pl.BlockSpec((27 * L, group), lambda i, p, l: (0, p[2] ^ i)),
                pl.BlockSpec((L, group), lambda i, p, l: (0, p[2] ^ i)),
                pl.BlockSpec((8, group), lambda i, p, l: (0, p[2] ^ i)),
            ]
            + [ANY] * BLOCKS,
            out_specs=[pl.BlockSpec((1, cells, group), lambda i, p, l: (i // 2, 0, 0))] * 2,
            scratch_shapes=[
                pltpu.VMEM((BLOCKS, W, cells), bf16),
                pltpu.VMEM((cells, 28 * L), bf16),
                pltpu.VMEM((28 * L, group), bf16),
                pltpu.SemaphoreType.DMA((BLOCKS,)),
            ],
        ),
        out_shape=[jax.ShapeDtypeStruct((2, cells, group), bf16)] * 2,
        compiler_params=params(),
        cost_estimate=cost(1e6, 1e6),
        name="input_grads",
    )(pos, lim, col_row, atrous_weight.reshape(27 * L, C), w_point,
      jnp.pad(pooled_grad, ((0, 8 - images), (0, 0))), *blocks)
    from_core = swap(ig_give, "ch", 1)

    from_core = from_core.astype(f32)
    keep = ig_keep[0].astype(f32) + from_core[0]
    give = (ig_keep[1].astype(f32) + from_core[1]).astype(bf16)
    given = swap(give, "ch", 2)
    pos = after(pos, give)
    g_wide, p_wide, g_proj = pl.pallas_call(
        wide_kernel,
        grid=(4,),
        in_specs=[SMEM, pl.BlockSpec((BLOCKS, 1, cells, wide_w), lambda i: (0, i, 0, 0))]
        + [ANY] * BLOCKS
        + [pl.BlockSpec((16, cells), lambda i: (W // 16, 0))] * BLOCKS,
        out_specs=[
            pl.BlockSpec((27 * L, wide_w), lambda i: (0, narrow // wide_w + i)),
            pl.BlockSpec((L, wide_w), lambda i: (0, narrow // wide_w + i)),
            pl.BlockSpec((5 * L, F), lambda i: (0, 0)),
        ],
        out_shape=[
            jax.ShapeDtypeStruct((27 * L, C), f32),
            jax.ShapeDtypeStruct((L, C), f32),
            jax.ShapeDtypeStruct((5 * L, F), f32),
        ],
        scratch_shapes=[tap_scratch, pltpu.SemaphoreType.DMA((BLOCKS,))],
        compiler_params=params(),
        cost_estimate=cost(1e6, 1e6),
        name="wide_weight_grads",
    )(pos, x_wide, *taps, *blocks)
    g_proj = g_proj.reshape(5, L, F)
    in_grad = (keep + after(given, p_wide).astype(f32)).astype(bf16)
    in_grad = in_grad.reshape(images, rows_dev, cols, group)

    step = 9 * L
    g_atrous, g_point = pl.pallas_call(
        widen_kernel,
        grid=(3,),
        in_specs=[
            pl.BlockSpec((BLOCKS, step, eighth), lambda i: (0, i, 0)),
            pl.BlockSpec((BLOCKS, L, eighth), lambda i: (0, 27, 0)),
            ANY,
            ANY,
        ],
        out_specs=[
            pl.BlockSpec((step, narrow), lambda i: (i, 0)),
            pl.BlockSpec((L, narrow), lambda i: (0, 0)),
        ],
        out_shape=[jax.ShapeDtypeStruct((27 * L, C), f32), jax.ShapeDtypeStruct((L, C), f32)],
        input_output_aliases={2: 0, 3: 1},
        compiler_params=params(),
        cost_estimate=cost(1e6, 20e6),
        name="widen",
    )(gw_all, gw_all, g_wide, p_wide)
    g_atrous = g_atrous.reshape(3, 3, 3, L, C)
    return (output, in_grad, g_point, g_atrous, g_pool, g_proj, g_gains, g_shifts)


def solution(mesh):
    placed = (
        P(None, "sp", None, None),
        P(),
        P(),
        P("ch", None),
        P(None, None, None, "ch", None),
        P("ch", None),
        P(None, "ch", None),
        P(None, "ch"),
        P(None, "ch"),
        P(None, "sp", None, None),
    )
    return jax.shard_map(
        body,
        mesh=mesh,
        in_specs=placed,
        out_specs=(
            P(None, "sp", None, "ch"),
            P(None, "sp", None, "ch"),
            P("ch", None),
            P(None, None, None, "ch", None),
            P("ch", None),
            P(None, "ch", None),
            P(None, "ch"),
            P(None, "ch"),
        ),
        check_vma=False,
    )
```

```python
import functools

import jax
import jax.numpy as jnp
from jax import lax
from jax.experimental import pallas as pl
from jax.experimental.pallas import tpu as pltpu
from jax.sharding import PartitionSpec as P

BLOCKS = 8
BRANCHES = 4
epsilon = 1e-05
dilation_factors = (1, 2, 3)
highest_precision = lax.Precision.HIGHEST
f32 = jnp.float32
bf16 = jnp.bfloat16
MIB = 1 << 20
VMEM = pl.BlockSpec(memory_space=pltpu.VMEM)
SMEM = pl.BlockSpec(memory_space=pltpu.SMEM)
NT = (((1,), (1,)), ((), ()))
NN = (((1,), (0,)), ((), ()))
TN = (((0,), (0,)), ((), ()))


def dot(a, b, dims):
    return lax.dot_general(a, b, dims, preferred_element_type=f32)


def params(mib=60, **kw):
    return pltpu.CompilerParams(vmem_limit_bytes=mib * MIB, **kw)


def cost(flops, nbytes):
    return pl.CostEstimate(flops=int(flops), bytes_accessed=int(nbytes), transcendentals=0)


def cell_mask(lim_ref, slabs, cols, width):
    col = lax.broadcasted_iota(jnp.int32, (cols, width), 0)
    return jnp.concatenate([(col < lim_ref[i]).astype(f32) for i in range(slabs)], axis=0)


def column_ids(slabs, cols, width):
    return lax.broadcasted_iota(jnp.int32, (slabs, cols, width), 1).reshape(slabs * cols, width)


def from_left(a, d, col):
    return jnp.where(col >= d, pltpu.roll(a, d, 0), 0.0)


def from_right(a, d, col, cols):
    return jnp.where(col < cols - d, pltpu.roll(a, a.shape[0] - d, 0), 0.0)


def silu_parts(t):
    s = 1.0 / (1.0 + jnp.exp(-t))
    return s, t * s


def slope(t, s):
    return s * (1.0 + t * (1.0 - s))


def column_sums(*rows):
    sums = [jnp.sum(r, axis=0, keepdims=True) for r in rows]
    width = sums[0].shape[1]
    return jnp.concatenate(sums + [jnp.zeros((8 - len(sums), width), f32)], axis=0)


def side_kernel(lim_ref, low_ref, x_ref, *refs, steps, slabs, cols, rates):
    n_rates = len(rates)
    weights, outs, (wcat, acc) = refs[: 2 * n_rates], refs[2 * n_rates : 4 * n_rates], refs[4 * n_rates :]
    k = pl.program_id(0)
    L = weights[0].shape[3]
    for j in range(n_rates):
        for v in range(3):
            t = (j * 3 + v) * 2 * L
            wcat[t : t + L] = weights[2 * j][0, 0, v]
            wcat[t + L : t + 2 * L] = weights[2 * j + 1][0, 0, v]

    @pl.when(k == 0)
    def _():
        acc[...] = jnp.zeros_like(acc)

    x = x_ref[...]
    total = 6 * n_rates * L
    for n in range(0, total, 256):
        e = min(n + 256, total)
        acc[:, n:e] += dot(x, wcat[n:e], NT)

    @pl.when(k == steps - 1)
    def _():
        cells = slabs * cols
        half = cells // 2
        mask = cell_mask(lim_ref, slabs, cols, 2 * L)
        col = column_ids(slabs, cols, 2 * L)
        low = lax.broadcasted_iota(jnp.int32, (half, 2 * L), 1) < L
        for j in range(n_rates):
            a = [acc[:, (j * 3 + v) * 2 * L : (j * 3 + v + 1) * 2 * L] * mask for v in range(3)]
            s = a[1] + from_left(a[0], rates[j], col) + from_right(a[2], rates[j], col, cols)
            top, bottom = s[:half], s[half:]
            up = jnp.where(low, top, pltpu.roll(bottom, L, 1))
            down = jnp.where(low, pltpu.roll(top, L, 1), bottom)
            first = low_ref[j] == 1
            outs[2 * j][...] = jnp.where(first, up, down).astype(bf16)
            outs[2 * j + 1][...] = jnp.where(first, down, up).astype(bf16)


def centre_kernel(
    lim_ref, x_ref, wc_ref, wpoint_ref, out_ref, sums_ref, wcat, acc, *, steps, slabs, cols, rates, images
):
    k = pl.program_id(0)
    L = wpoint_ref.shape[0]
    order = [None, (0, 1), (1, 1), (2, 1), (1, 0), (2, 0), (1, 2), (2, 2), (0, 0), (0, 2)]
    for i, tap in enumerate(order):
        wcat[i * L : (i + 1) * L] = wpoint_ref[...] if tap is None else wc_ref[tap[0], 0, tap[1]]

    @pl.when(k == 0)
    def _():
        acc[...] = jnp.zeros_like(acc)

    x = x_ref[...]
    total = 10 * L
    for n in range(0, total, 256):
        e = min(n + 256, total)
        acc[:, n:e] += dot(x, wcat[n:e], NT)

    width = x_ref.shape[1]
    cid = lax.broadcasted_iota(jnp.int32, (cols, width), 0)
    per = slabs // images
    sums = []
    for image in range(images):
        part = jnp.zeros((cols, width), f32)
        for i in range(image * per, (image + 1) * per):
            part += jnp.where(cid < lim_ref[i], x_ref[i * cols : (i + 1) * cols].astype(f32), 0.0)
        sums.append(jnp.sum(part, axis=0, keepdims=True))
    sums_ref[...] = jnp.concatenate(sums + [jnp.zeros((8 - images, width), f32)], axis=0)

    @pl.when(k == steps - 1)
    def _():
        cells = slabs * cols
        mask = cell_mask(lim_ref, slabs, cols, 2 * L)
        col = column_ids(slabs, cols, 2 * L)
        low = lax.broadcasted_iota(jnp.int32, (cells, 2 * L), 1) < L
        b = [acc[:, i * 2 * L : (i + 1) * 2 * L] * mask for i in range(5)]
        d0, d1, d2 = rates
        t = jnp.where(low, from_left(b[4], d0, col), from_right(b[4], d0, col, cols))
        out_ref[:, : 2 * L] = b[0] + jnp.where(low, 0.0, t + pltpu.roll(t, L, 1))
        out_ref[:, 2 * L :] = (
            b[1]
            + jnp.where(low, from_left(b[2], d1, col), from_left(b[2], d2, col))
            + jnp.where(low, from_right(b[3], d1, col, cols), from_right(b[3], d2, col, cols))
        )


def combine_kernel(lim_ref, centre_ref, *refs, slabs, cols):
    halo, (extra_ref, conv_ref, send_ref, message_ref, local_ref) = refs[:6], refs[6:]
    cells = slabs * cols
    half = cells // 2
    W = centre_ref.shape[1]
    L = W // 4
    h = [halo[2 * j][...].astype(f32) + halo[2 * j + 1][...].astype(f32) for j in range(3)]
    turned = [pltpu.roll(a, L, 1) for a in h]
    low = lax.broadcasted_iota(jnp.int32, (cells, 2 * L), 1) < L
    h0 = jnp.concatenate([turned[0], h[0]], axis=0)
    h1 = jnp.concatenate([h[1], turned[1]], axis=0)
    h2 = jnp.concatenate([turned[2], h[2]], axis=0)
    left = centre_ref[:, : 2 * L] + jnp.where(low, 0.0, h0)
    right = centre_ref[:, 2 * L :] + jnp.where(low, h1, h2)
    conv_ref[:, : 2 * L] = left
    conv_ref[:, 2 * L :] = right
    mask = cell_mask(lim_ref, slabs, cols, 2 * L)
    own = lim_ref[0]
    for i in range(1, slabs):
        own = own + lim_ref[i]
    own = jnp.maximum(own, 1).astype(f32)
    for lo, part in ((0, left), (2 * L, right)):
        s = jnp.sum(part * mask, axis=0, keepdims=True)
        q = jnp.sum(part * part * mask, axis=0, keepdims=True)
        local = s / own
        send_ref[:, lo : lo + 2 * L] = (part - local).astype(bf16)
        message_ref[:8, lo : lo + 2 * L] = extra_ref[:8, lo : lo + 2 * L] + jnp.concatenate(
            [s, q, jnp.zeros((6, 2 * L), f32)], axis=0
        )
        local_ref[:, lo : lo + 2 * L] = jnp.concatenate(
            [jnp.zeros((2, 2 * L), f32), local, jnp.zeros((5, 2 * L), f32)], axis=0
        )
    message_ref[8:] = extra_ref[8:]


def norm_of(total, square, n):
    mean = total / n
    return mean, lax.rsqrt(square / n - mean * mean + epsilon)


def added(parts):
    a, b, c, d = (r[...] for r in parts)
    return (a + b) + (c + d)


def mix_kernel(
    lim_ref, n_ref, conv_ref, c1_ref, c2_ref, c3_ref, t0, t1, t2, t3, p0, p1, p2, p3,
    mixed_ref, act_ref, sums_ref, stat_ref, scratch, *, slabs, cols, images
):
    per = slabs // images
    n = n_ref[0]
    width = conv_ref.shape[1]
    L = width // 4
    cid = lax.broadcasted_iota(jnp.int32, (cols, width), 0)
    pooled = None
    for d, (ref, tile_ref, par_ref) in enumerate(
        ((conv_ref, t0, p0), (c1_ref, t1, p1), (c2_ref, t2, p2), (c3_ref, t3, p3))
    ):
        tile = tile_ref[...]
        par = par_ref[5 * L :].astype(f32)
        par = par[0:4] + par[4:8] + par[8:12]
        gain = par[0:1]
        shift = jnp.concatenate([par[1:2, 2 * L :], par[2:3, : 2 * L]], axis=1)
        mean, rstd = norm_of(tile[0:1], tile[1:2], n)
        offset = mean if d == 0 else mean - tile[2:3]
        scale = rstd * gain
        if d == 0:
            stat_ref[...] = jnp.concatenate([mean, rstd, gain, shift, jnp.zeros((4, width), f32)], axis=0)
        dest = act_ref if d == 0 else scratch
        for i in range(slabs):
            rows = slice(i * cols, (i + 1) * cols)
            pre = (ref[rows].astype(f32) - offset) * scale + shift
            _, act = silu_parts(pre)
            dest[rows] = jnp.where(cid < lim_ref[i], act, 0.0).astype(bf16)
        part = dot(dest[...], par_ref[:width], NN)
        if d == 0:
            mixed_ref[...] = part
        else:
            mixed_ref[...] += part
        projected = tile[4 : 4 + images, :L]
        pmean, prstd = norm_of(
            jnp.sum(projected, axis=0, keepdims=True), jnp.sum(projected * projected, axis=0, keepdims=True), images
        )
        _, pact = silu_parts(par[1:2, :L] * ((projected - pmean) * prstd) + par[2:3, 2 * L : 3 * L])
        pact = jnp.concatenate([pact, jnp.zeros((16 - images, L), f32)], axis=0).astype(bf16)
        part = dot(pact, par_ref[width : width + L], NN)
        pooled = part if d == 0 else pooled + part
    F = mixed_ref.shape[1]
    cid = lax.broadcasted_iota(jnp.int32, (cols, F), 0)
    s = jnp.zeros((cols, F), f32)
    q = jnp.zeros((cols, F), f32)
    for i in range(slabs):
        rows = slice(i * cols, (i + 1) * cols)
        image = i // per
        value = mixed_ref[rows] + jnp.where(cid < lim_ref[i], pooled[image : image + 1], 0.0)
        mixed_ref[rows] = value
        s += value
        q += value * value
    sums_ref[...] = column_sums(s, q)


def final_kernel(
    lim_ref, n_ref, own_ref, mixed_ref, grad_ref, p0, p1, p2, p3, s0, s1, s2, s3, out_ref, dt_ref, sums_ref, stat_ref,
    *, slabs, cols
):
    F = mixed_ref.shape[1]
    total = added((s0, s1, s2, s3))
    mean, rstd = norm_of(total[0:1], total[1:2], n_ref[0])
    L = F // 4
    group = lax.broadcasted_iota(jnp.int32, (8, F), 1) // L
    gain, shift = jnp.zeros((8, F), f32), jnp.zeros((8, F), f32)
    for d, ref in enumerate((p0, p1, p2, p3)):
        par = ref[5 * L :].astype(f32)
        par = par[0:4] + par[4:8] + par[8:12]
        here = group == (own_ref[0] ^ d)
        g = jnp.where(group == 1, jnp.broadcast_to(par[1:2], (8, F)), 0.0)
        h = jnp.where(group == 3, jnp.broadcast_to(par[2:3], (8, F)), 0.0)
        gain += jnp.where(here, g + pltpu.roll(g, L, 1) + pltpu.roll(g, 2 * L, 1) + pltpu.roll(g, 3 * L, 1), 0.0)
        shift += jnp.where(here, h + pltpu.roll(h, L, 1) + pltpu.roll(h, 2 * L, 1) + pltpu.roll(h, 3 * L, 1), 0.0)
    gain, shift = gain[0:1], shift[0:1]
    stat_ref[...] = jnp.concatenate([mean, rstd, gain, shift, jnp.zeros((4, F), f32)], axis=0)
    cid = lax.broadcasted_iota(jnp.int32, (cols, F), 0)
    s = jnp.zeros((cols, F), f32)
    q = jnp.zeros((cols, F), f32)
    for i in range(slabs):
        rows = slice(i * cols, (i + 1) * cols)
        valid = cid < lim_ref[i]
        normed = (mixed_ref[rows] - mean) * rstd
        pre = gain * normed + shift
        sig, act = silu_parts(pre)
        out_ref[rows] = jnp.where(valid, act, 0.0).astype(bf16)
        dt = jnp.where(valid, grad_ref[rows].astype(f32) * slope(pre, sig), 0.0)
        dt_ref[rows] = dt
        s += dt
        q += dt * normed
    sums_ref[...] = column_sums(s, q)


def branch_kernel(
    lim_ref, n_ref, mixed_ref, fdt_ref, fstat_ref, conv_ref, act_ref, stat_ref, wbranch_ref, s0, s1, s2, s3,
    dt_ref, gproj_ref, image_ref, sums_ref, grad, *, slabs, cols, images
):
    F = mixed_ref.shape[1]
    W = conv_ref.shape[1]
    per = slabs // images
    mean, rstd, scale = fstat_ref[0:1], fstat_ref[1:2], fstat_ref[1:2] * fstat_ref[2:3]
    total = added((s0, s1, s2, s3)) / n_ref[0]
    beta, gamma = total[0:1], total[1:2]
    cid = lax.broadcasted_iota(jnp.int32, (cols, F), 0)
    image_sums = []
    for image in range(images):
        total = jnp.zeros((cols, F), f32)
        for i in range(image * per, (image + 1) * per):
            rows = slice(i * cols, (i + 1) * cols)
            normed = (mixed_ref[rows] - mean) * rstd
            g = jnp.where(cid < lim_ref[i], scale * (fdt_ref[rows] - beta - normed * gamma), 0.0)
            g = g.astype(bf16)
            grad[rows] = g
            total += g.astype(f32)
        image_sums.append(jnp.sum(total, axis=0, keepdims=True))
    image_ref[...] = jnp.concatenate(image_sums + [jnp.zeros((8 - images, F), f32)], axis=0)
    dt_ref[...] = dot(grad[...], wbranch_ref[...], NT)
    gproj_ref[...] = dot(act_ref[...], grad[...], TN)
    bmean, brstd, bgain, bshift = (stat_ref[i : i + 1] for i in range(4))
    cid = lax.broadcasted_iota(jnp.int32, (cols, W), 0)
    s = jnp.zeros((cols, W), f32)
    q = jnp.zeros((cols, W), f32)
    for i in range(slabs):
        rows = slice(i * cols, (i + 1) * cols)
        normed = (conv_ref[rows] - bmean) * brstd
        pre = bgain * normed + bshift
        sig, _ = silu_parts(pre)
        dt = jnp.where(cid < lim_ref[i], dt_ref[rows] * slope(pre, sig), 0.0)
        dt_ref[rows] = dt
        s += dt
        q += dt * normed
    sums_ref[...] = column_sums(s, q)


def grad_kernel(lim_ref, n_ref, dt_ref, conv_ref, stat_ref, sums_ref, piece_ref, cg_ref, scratch, *, slabs, cols):
    W = conv_ref.shape[1]
    mean, rstd, scale = stat_ref[0:1], stat_ref[1:2], stat_ref[1:2] * stat_ref[2:3]
    beta, gamma = sums_ref[0:1] / n_ref[0], sums_ref[1:2] / n_ref[0]
    cid = lax.broadcasted_iota(jnp.int32, (cols, W), 0)
    for i in range(slabs):
        rows = slice(i * cols, (i + 1) * cols)
        normed = (conv_ref[rows] - mean) * rstd
        g = scale * (dt_ref[rows] - beta - normed * gamma)
        scratch[rows] = jnp.where(cid < lim_ref[i], g, 0.0)
    cg_ref[:W] = scratch[...].T.astype(bf16)
    F = piece_ref.shape[1]
    for k in range(piece_ref.shape[0] // 16):
        cg_ref[W:, k * F : (k + 1) * F] = piece_ref[k * 16 : (k + 1) * 16].astype(bf16)


def shifted(f, v, d, col, cols):
    if v == 1:
        return f
    if v == 2:
        return jnp.where(col >= d, pltpu.roll(f, d, 1), 0.0)
    return jnp.where(col < cols - d, pltpu.roll(f, f.shape[1] - d, 1), 0.0)


def expand_kernel(col_ref, cg_ref, out_ref, *, cols, rates):
    L = cg_ref.shape[0] // 4
    for j in range(3):
        raw = cg_ref[(j + 1) * L : (j + 2) * L]
        f = raw.astype(f32)
        col = jnp.broadcast_to(col_ref[0:1], f.shape)
        base = 3 * j * L
        out_ref[base : base + L] = shifted(f, 0, rates[j], col, cols).astype(bf16)
        out_ref[base + L : base + 2 * L] = raw
        out_ref[base + 2 * L : base + 3 * L] = shifted(f, 2, rates[j], col, cols).astype(bf16)
    out_ref[9 * L :] = cg_ref[:L]


def fetch_blocks(pos, blocks, dest, sems, lanes=False):
    copies = []
    for d, ref in enumerate(blocks):
        place = pos ^ d
        if lanes:
            cells = ref.shape[1]
            spot = dest.at[:, pl.ds(pl.multiple_of(place * cells, 128), cells)]
        else:
            spot = dest.at[place]
        source = ref if lanes else ref.at[pl.ds(0, dest.shape[1])]
        copies.append(pltpu.make_async_copy(source, spot, sems.at[d]))
    for c in copies:
        c.start()
    return copies


def tap_products(store, taps, x_rows, L):
    cells = taps.shape[1] // BLOCKS
    own_row = dot(taps[...], x_rows(0, BLOCKS), NN)
    for j in range(3):
        lo = (j * 3 + 1) * 3 * L
        store(lo, own_row[3 * j * L : 3 * (j + 1) * L])
    store(27 * L, own_row[9 * L :])
    for j in range(3):
        rows = slice(3 * j * L, 3 * (j + 1) * L)
        span = (BLOCKS - 1 - j) * cells
        far = (j + 1) * cells
        store(j * 9 * L, dot(taps[rows, far:], x_rows(0, BLOCKS - 1 - j), NN))
        store((j * 3 + 2) * 3 * L, dot(taps[rows, :span], x_rows(j + 1, BLOCKS), NN))


def narrow_kernel(pos_ref, *refs, parts):
    blocks, (xown_ref, xcore_ref, out_ref, taps, x, sems, xsems) = refs[:BLOCKS], refs[BLOCKS:]
    pos, ch = pos_ref[0], pos_ref[2]
    L = taps.shape[0] // 10
    cells = taps.shape[1] // BLOCKS
    rows = xown_ref.shape[2]
    copies = fetch_blocks(pos, blocks, taps, sems, lanes=True)
    for e in range(parts):
        for d in range(BLOCKS):
            place = pl.ds(pl.multiple_of((pos ^ d) * cells + (ch ^ e) * rows, 16), rows)
            source = (xown_ref, xcore_ref)[e % 2].at[e // 2, d]
            c = pltpu.make_async_copy(source, x.at[place], xsems.at[e, d])
            c.start()
            copies.append(c)
    for c in copies:
        c.wait()

    def store(lo, value):
        out_ref[lo : lo + value.shape[0]] = value.astype(bf16)

    tap_products(store, taps, lambda lo, hi: x[lo * cells : hi * cells], L)


def wide_kernel(pos_ref, x_ref, *refs):
    blocks, pieces, (acc_ref, point_ref, proj_ref, taps, sems) = (
        refs[:BLOCKS],
        refs[BLOCKS : 2 * BLOCKS],
        refs[2 * BLOCKS :],
    )
    L = point_ref.shape[0]
    F = proj_ref.shape[1]
    rows = proj_ref.shape[0] // BLOCKS

    @pl.when(pl.program_id(0) == 0)
    def _():
        copies = fetch_blocks(pos_ref[0], blocks, taps, sems, lanes=True)
        for d in range(BLOCKS):
            p = pos_ref[0] ^ d
            base = (p % 2 * (BLOCKS // 2) + p // 2) * rows
            for k in range(0, rows, 16):
                n = min(16, rows - k)
                value = pieces[d][:, k // 16 * F : (k // 16 + 1) * F].astype(f32)
                proj_ref[pl.ds(pl.multiple_of(base + k, 8), n)] = value[:n]
        for c in copies:
            c.wait()

    def store(lo, value):
        if lo < 27 * L:
            acc_ref[lo : lo + value.shape[0]] = value
        else:
            point_ref[...] = value

    w = x_ref.shape[3]
    tap_products(store, taps, lambda lo, hi: x_ref[lo:hi, 0].reshape(-1, w), L)


def widen_kernel(in_ref, pin_ref, keep_ref, pkeep_ref, out_ref, pout_ref):
    w = in_ref.shape[2]
    for s in range(BLOCKS):
        out_ref[:, s * w : (s + 1) * w] = in_ref[s].astype(f32)
        pout_ref[:, s * w : (s + 1) * w] = pin_ref[s].astype(f32)


def input_grad_kernel(pos_ref, lim_ref, col_ref, w_ref, wp_ref, pool_ref, *refs, slabs, cols, rates, images):
    blocks, (keep_ref, give_ref, cg, lhs, rhs, sems) = refs[:BLOCKS], refs[BLOCKS:]
    L = wp_ref.shape[0]
    s = pos_ref[0]

    @pl.when(pl.program_id(0) == 0)
    def _():
        for c in fetch_blocks(s, blocks, cg, sems):
            c.wait()
        pieces = []
        order = [(j, u, v) for j in range(3) for u in range(3) for v in range(3)] + [None]
        for i, tap in enumerate(order):
            if tap is None:
                pieces.append(cg[s, 0:L].astype(f32))
            else:
                j, u, v = tap
                b = s - (u - 1) * (j + 1)
                inside = ((b >= 0) & (b < BLOCKS)).astype(f32)
                f = cg[jnp.clip(b, 0, BLOCKS - 1), (j + 1) * L : (j + 2) * L].astype(f32) * inside
                col = jnp.broadcast_to(col_ref[0:1], f.shape)
                pieces.append(shifted(f, v, rates[j], col, cols))
            if i % 4 == 3:
                lhs[:, (i - 3) * L : (i + 1) * L] = jnp.concatenate(pieces, axis=0).T.astype(bf16)
                pieces = []

    rhs[: 27 * L] = w_ref[...]
    rhs[27 * L :] = wp_ref[...]
    width = keep_ref.shape[2]
    per = slabs // images
    cid = lax.broadcasted_iota(jnp.int32, (cols, 256), 0)

    def fill(out_ref):
        for n in range(0, width, 256):
            part = dot(lhs[...], rhs[:, n : n + 256], NN)
            for i in range(slabs):
                value = part[i * cols : (i + 1) * cols] + pool_ref[i // per : i // per + 1, n : n + 256]
                out_ref[0, i * cols : (i + 1) * cols, n : n + 256] = jnp.where(
                    cid < lim_ref[i], value, 0.0
                ).astype(bf16)

    @pl.when(pl.program_id(0) % 2 == 0)
    def _():
        fill(keep_ref)

    @pl.when(pl.program_id(0) % 2 == 1)
    def _():
        fill(give_ref)


def grouped(pairs, size):
    return [(g * BLOCKS + a, g * BLOCKS + b) for g in range(size // BLOCKS) for a, b in pairs]


def neighbours(first, second, axis, distance):
    size = lax.axis_size(axis)
    rounds = []
    for parity, block in ((0, first), (1, second)):
        lows = [a for a in range(BLOCKS - distance) if (a // distance) % 2 == parity]
        pairs = [(a, a + distance) for a in lows] + [(a + distance, a) for a in lows]
        rounds.append(lax.ppermute(block, axis, grouped(pairs, size)))
    return rounds


def swap(block, axis, bits):
    return lax.ppermute(block, axis, [(i, i ^ bits) for i in range(lax.axis_size(axis))])


def parts_over_sp(x):
    x = x + swap(x, "sp", 1)
    return [x] + [swap(x, "sp", b) for b in (2, 4, 6)]


def swaps_over_sp(x):
    blocks = [x, None] + [swap(x, "sp", b) if b % 2 == 0 else None for b in range(2, BLOCKS)]
    for b in range(1, BLOCKS, 2):
        blocks[b] = swap(blocks[b - 1], "sp", 1)
    return blocks


def after(x, *others):
    return lax.optimization_barrier((x, others))[0]


def thirds(x):
    hi = lax.reduce_precision(x, 8, 7)
    mid = lax.reduce_precision(x - hi, 8, 7)
    return jnp.concatenate([hi, mid, x - hi - mid], axis=0).astype(bf16)


def whole(parts):
    hi, mid, low = jnp.split(parts.astype(f32), 3, axis=0)
    return hi + mid + low


def plain_from_behind(block, axis, distance):
    devices = range(lax.axis_size(axis))
    route = [(i - distance, i) for i in devices if i - distance in devices]
    return lax.ppermute(block, axis, route)


def shift_cols(values, offset):
    margin = abs(offset)
    padded = jnp.pad(values, ((0, 0), (0, 0), (margin, margin), (0, 0)))
    return lax.slice_in_dim(padded, margin + offset, margin + offset + values.shape[2], axis=2)


def silu_slope(pre_act):
    sigmoid_val = jax.nn.sigmoid(pre_act)
    return sigmoid_val * (1.0 + pre_act * (1.0 - sigmoid_val))


def source_inside(block_id, shift_amount):
    source = block_id - shift_amount
    return (source >= 0) & (source < BLOCKS)


def move_features(values, shift_amount):
    return plain_from_behind(values, "sp", shift_amount)


def shifted_gradients(values, shift_amount):
    return plain_from_behind(values, "sp", shift_amount)


def tap_partials(source, weight_taps, dilation_rate):
    count_k, rows_dev, grid_width, channel_total = source.shape
    local_output = weight_taps.shape[1]
    products = jnp.einsum(
        "pc,tc->pt",
        source.reshape(-1, channel_total),
        weight_taps.reshape(3 * local_output, channel_total),
        preferred_element_type=jnp.float32,
    ).reshape(count_k, rows_dev, grid_width, 3, local_output)
    return (
        shift_cols(products[:, :, :, 0, :], -dilation_rate)
        + products[:, :, :, 1, :]
        + shift_cols(products[:, :, :, 2, :], dilation_rate)
    )


def plain_body(
    features, heights, widths, w_point, atrous_weight, w_pool, w_proj, bn_gains, bn_shifts, out_grad
):
    count_k, rows_dev, grid_width, channel_total = features.shape
    local_output = w_point.shape[0]
    full_out = w_proj.shape[2]
    groups = heights.shape[1]
    images = count_k * groups
    pixels = count_k * rows_dev * grid_width
    position = lax.axis_index("sp")
    block_id = position % BLOCKS
    group_id = position // BLOCKS
    channel_start = lax.axis_index("ch") * local_output
    own_out_grad = lax.dynamic_slice_in_dim(out_grad, channel_start, local_output, 3)
    group_pick = jnp.arange(groups, dtype=jnp.int32) == group_id
    group_onehot = group_pick.astype(jnp.float32)
    own_heights = jnp.sum(jnp.where(group_pick[None, :], heights, 0), axis=1)
    own_widths = jnp.sum(jnp.where(group_pick[None, :], widths, 0), axis=1)
    row_ids = block_id * rows_dev + jnp.arange(rows_dev, dtype=jnp.int32)
    col_ids = jnp.arange(grid_width, dtype=jnp.int32)
    inside = (row_ids[None, :, None] < own_heights[:, None, None]) & (
        col_ids[None, None, :] < own_widths[:, None, None]
    )
    pix_mask = inside.astype(jnp.float32)[..., None]
    valid_count = jnp.sum((heights * widths).astype(jnp.float32))
    own_count = (own_heights * own_widths).astype(jnp.float32)
    masked_values = features * pix_mask.astype(jnp.bfloat16)
    flat_pix = masked_values.reshape(pixels, channel_total)
    point_conv = jnp.einsum("pc,fc->pf", flat_pix, w_point, preferred_element_type=jnp.float32)
    conv_list = [point_conv.reshape(count_k, rows_dev, grid_width, local_output)]
    for dilation_index, dilation_factor in enumerate(dilation_factors):
        dilation_rate = rows_dev * dilation_factor
        running_total = tap_partials(masked_values, atrous_weight[dilation_index, 1], dilation_rate)
        for row_offset_tap in (0, 2):
            shift_amount = (1 - row_offset_tap) * dilation_factor
            keep_rows = source_inside(block_id, shift_amount)
            received_part = move_features(masked_values, shift_amount) * keep_rows.astype(
                jnp.bfloat16
            )
            running_total = running_total + tap_partials(
                received_part, atrous_weight[dilation_index, row_offset_tap], dilation_rate
            )
        conv_list.append(running_total)
    conv_out = jnp.stack(conv_list)
    stat_sum, stat_square = lax.psum(
        (
            jnp.sum(conv_out * pix_mask, axis=(1, 2, 3)),
            jnp.sum(conv_out * conv_out * pix_mask, axis=(1, 2, 3)),
        ),
        "sp",
    )
    branch_mean = stat_sum / valid_count
    branch_inv = lax.rsqrt(stat_square / valid_count - branch_mean * branch_mean + epsilon)
    normed = (conv_out - branch_mean[:, None, None, None, :]) * branch_inv[:, None, None, None, :]
    pre_act = bn_gains[:4][:, None, None, None, :] * normed + bn_shifts[:4][:, None, None, None, :]
    branch_act = (pix_mask * jax.nn.silu(pre_act)).astype(jnp.bfloat16)
    own_sums = jnp.sum(masked_values, axis=(1, 2), dtype=jnp.float32)
    own_pooled = own_sums / own_count[:, None]
    pool_weight = w_pool.astype(jnp.float32)
    pooled = lax.psum(own_pooled[:, None, :] * group_onehot[None, :, None], "sp")
    projected = jnp.dot(
        pooled.reshape(images, channel_total), pool_weight.T, precision=highest_precision
    )
    pool_mean = jnp.mean(projected, axis=0)
    pool_inv = lax.rsqrt(jnp.mean(projected * projected, axis=0) - pool_mean * pool_mean + epsilon)
    pool_normed = (projected - pool_mean) * pool_inv
    pool_pre = bn_gains[4] * pool_normed + bn_shifts[4]
    pool_act = jax.nn.silu(pool_pre).astype(jnp.bfloat16)
    own_act = jnp.sum(
        pool_act.astype(jnp.float32).reshape(count_k, groups, local_output)
        * group_onehot[None, :, None],
        axis=1,
    )
    pool_pixels = (own_act[:, None, None, :] * pix_mask).astype(jnp.bfloat16)
    stacked = jnp.concatenate([branch_act, pool_pixels[None]], axis=0).reshape(
        5, pixels, local_output
    )
    partial_value = jnp.einsum("bpf,bfo->po", stacked, w_proj, preferred_element_type=jnp.float32)
    mixed_sum = lax.psum_scatter(
        partial_value.reshape(count_k, rows_dev, grid_width, full_out),
        "ch",
        scatter_dimension=3,
        tiled=True,
    )
    final_sum, final_square = lax.psum(
        (
            jnp.sum(mixed_sum * pix_mask, axis=(0, 1, 2)),
            jnp.sum(mixed_sum * mixed_sum * pix_mask, axis=(0, 1, 2)),
        ),
        "sp",
    )
    final_mean = final_sum / valid_count
    final_inv = lax.rsqrt(final_square / valid_count - final_mean * final_mean + epsilon)
    final_normed = (mixed_sum - final_mean) * final_inv
    final_pre = bn_gains[5] * final_normed + bn_shifts[5]
    output = (pix_mask * jax.nn.silu(final_pre)).astype(jnp.bfloat16)
    final_dt = pix_mask * own_out_grad.astype(jnp.float32) * silu_slope(final_pre)
    final_beta, final_gamma = lax.psum(
        (jnp.sum(final_dt, axis=(0, 1, 2)), jnp.sum(final_dt * final_normed, axis=(0, 1, 2))), "sp"
    )
    mixed_grad = (
        pix_mask
        * final_inv
        * bn_gains[5]
        * (final_dt - final_beta / valid_count - final_normed * final_gamma / valid_count)
    ).astype(jnp.bfloat16)
    full_grad = lax.all_gather(mixed_grad, "ch", axis=3, tiled=True).reshape(pixels, full_out)
    g_proj = jnp.einsum("bpf,po->bfo", stacked, full_grad, preferred_element_type=jnp.float32)
    act_grads = jnp.einsum(
        "po,bfo->bpf", full_grad, w_proj, preferred_element_type=jnp.float32
    ).reshape(5, count_k, rows_dev, grid_width, local_output)
    branch_dt = pix_mask * act_grads[:4] * silu_slope(pre_act)
    pool_own_grad = jnp.sum(act_grads[4] * pix_mask, axis=(1, 2))
    branch_beta, branch_gamma, pool_grad = lax.psum(
        (
            jnp.sum(branch_dt, axis=(1, 2, 3)),
            jnp.sum(branch_dt * normed, axis=(1, 2, 3)),
            pool_own_grad[:, None, :] * group_onehot[None, :, None],
        ),
        "sp",
    )
    convolution_gradients = (
        pix_mask
        * branch_inv[:, None, None, None, :]
        * bn_gains[:4][:, None, None, None, :]
        * (
            branch_dt
            - branch_beta[:, None, None, None, :] / valid_count
            - normed * branch_gamma[:, None, None, None, :] / valid_count
        )
    ).astype(jnp.bfloat16)
    pool_dt = pool_grad.reshape(images, local_output) * silu_slope(pool_pre)
    pool_beta = jnp.sum(pool_dt, axis=0)
    pool_gamma = jnp.sum(pool_dt * pool_normed, axis=0)
    proj_grad = (
        pool_inv * bn_gains[4] * (pool_dt - pool_beta / images - pool_normed * pool_gamma / images)
    )
    own_proj_grad = jnp.sum(
        proj_grad.reshape(count_k, groups, local_output) * group_onehot[None, :, None], axis=1
    )
    g_pool = jnp.einsum("kf,kc->fc", own_proj_grad, own_pooled, precision=highest_precision)
    pooled_grad = (
        jnp.einsum("kf,fc->kc", own_proj_grad, pool_weight, precision=highest_precision)
        / own_count[:, None]
    )
    point_grad = convolution_gradients[0].reshape(pixels, local_output)
    g_point = jnp.einsum("pf,pc->fc", point_grad, flat_pix, preferred_element_type=jnp.float32)
    input_term = jnp.einsum("pf,fc->pc", point_grad, w_point, preferred_element_type=jnp.float32)
    input_term = (
        input_term.reshape(count_k, rows_dev, grid_width, channel_total)
        + pooled_grad[:, None, None, :]
    )
    atrous_list = []
    for dilation_index, dilation_factor in enumerate(dilation_factors):
        dilation_rate = rows_dev * dilation_factor
        tap_list = []
        for row_offset_tap in range(3):
            shift_amount = (row_offset_tap - 1) * dilation_factor
            if shift_amount == 0:
                received_part = convolution_gradients[dilation_index + 1]
            else:
                received_part = shifted_gradients(
                    convolution_gradients[dilation_index + 1], shift_amount
                ) * source_inside(block_id, shift_amount).astype(jnp.bfloat16)
            spread = jnp.stack(
                [
                    shift_cols(received_part, dilation_rate),
                    received_part,
                    shift_cols(received_part, -dilation_rate),
                ],
                axis=3,
            ).reshape(pixels, 3 * local_output)
            tap_list.append(
                jnp.einsum(
                    "pt,pc->tc", spread, flat_pix, preferred_element_type=jnp.float32
                ).reshape(3, local_output, channel_total)
            )
            tap_weight_slice = atrous_weight[dilation_index, row_offset_tap].reshape(
                3 * local_output, channel_total
            )
            input_term = input_term + jnp.einsum(
                "pt,tc->pc", spread, tap_weight_slice, preferred_element_type=jnp.float32
            ).reshape(count_k, rows_dev, grid_width, channel_total)
        atrous_list.append(jnp.stack(tap_list))
    g_atrous = jnp.stack(atrous_list)
    in_grad = lax.psum_scatter(
        (input_term * pix_mask).astype(jnp.bfloat16), "ch", scatter_dimension=3, tiled=True
    )
    g_point, g_atrous, g_proj, g_pool = (
        lax.psum(g_point.astype(jnp.bfloat16), "sp").astype(jnp.float32),
        lax.psum(g_atrous.astype(jnp.bfloat16), "sp").astype(jnp.float32),
        lax.psum(g_proj.astype(jnp.bfloat16), "sp").astype(jnp.float32),
        lax.psum(g_pool.astype(jnp.bfloat16), "sp").astype(jnp.float32),
    )
    g_gains = jnp.concatenate([branch_gamma, pool_gamma[None], final_gamma[None]], axis=0)
    g_shifts = jnp.concatenate([branch_beta, pool_beta[None], final_beta[None]], axis=0)
    return (output, in_grad, g_point, g_atrous, g_pool, g_proj, g_gains, g_shifts)


def body(
    features, heights, widths, w_point, atrous_weight, w_pool, w_proj, bn_gains, bn_shifts, out_grad
):
    images, rows_dev, cols, C = features.shape
    L = w_point.shape[0]
    if lax.axis_size("sp") != BLOCKS or lax.axis_size("ch") != 4 or L != 64:
        return plain_body(
            features, heights, widths, w_point, atrous_weight, w_pool, w_proj, bn_gains, bn_shifts, out_grad
        )
    F = w_proj.shape[2]
    W = BRANCHES * L
    slabs = images * rows_dev
    cells = slabs * cols
    rates = tuple(rows_dev * f for f in dilation_factors)
    block_id = lax.axis_index("sp")
    own = lax.axis_index("ch")
    h, w = heights[:, 0], widths[:, 0]
    row_ids = block_id * rows_dev + jnp.arange(rows_dev, dtype=jnp.int32)
    lim = jnp.where(row_ids[None, :] < h[:, None], w[:, None], 0).reshape(slabs)
    own_count = (h * w).astype(f32)
    n = jnp.sum(own_count)
    x = features.reshape(cells, C)
    og = out_grad.reshape(cells, F)

    norms = jnp.concatenate([bn_gains, bn_shifts, jnp.zeros((4, L), f32)], axis=0).reshape(4, W)
    wp = w_proj.reshape(5 * L, F)
    packed = jnp.concatenate([wp, thirds(norms), jnp.zeros((4, F), bf16)], axis=0)
    packed_y = swap(packed, "ch", 2)
    packed_core = swap(packed, "ch", 1)
    packed_all = [packed, packed_core, packed_y, swap(packed_y, "ch", 1)]
    count = n.reshape(1)
    own_id = own.astype(jnp.int32).reshape(1)

    KT = 512
    steps = C // KT
    x_spec = pl.BlockSpec((cells, KT), lambda k: (0, k))
    first = [(1 - (block_id // f) % 2).astype(jnp.int32) for f in dilation_factors]

    def side_taps(which, x):
        out = pl.pallas_call(
            functools.partial(
                side_kernel, steps=steps, slabs=slabs, cols=cols, rates=tuple(rates[j] for j in which)
            ),
            grid=(steps,),
            in_specs=[SMEM, SMEM, x_spec]
            + [
                pl.BlockSpec((1, 1, 3, L, KT), lambda k, j=j, u=u: (j, u, 0, 0, k))
                for j in which
                for u in (0, 2)
            ],
            out_specs=[pl.BlockSpec((cells // 2, 2 * L), lambda k: (0, 0))] * (2 * len(which)),
            out_shape=[jax.ShapeDtypeStruct((cells // 2, 2 * L), bf16)] * (2 * len(which)),
            scratch_shapes=[
                pltpu.VMEM((6 * len(which) * L, KT), bf16),
                pltpu.VMEM((cells, 6 * len(which) * L), f32),
            ],
            compiler_params=params(),
            cost_estimate=cost(2 * cells * C * 6 * len(which) * L, 10e6),
            name="side_taps",
        )(lim, jnp.stack([first[j] for j in which]), x, *[atrous_weight] * (2 * len(which)))
        out = after(tuple(out), packed_y, packed_core)
        moved = []
        for i, j in enumerate(which):
            moved += neighbours(out[2 * i], out[2 * i + 1], "sp", dilation_factors[j])
        return moved, out[0]

    narrow = C // 2
    valid = (jnp.arange(cols, dtype=jnp.int32)[None, :] < lim[:, None]).reshape(cells, 1)
    cut = narrow // BLOCKS
    part = cells // images
    image = lax.dynamic_slice(x, (own * part, 0), (part, narrow))
    image = jnp.where(lax.dynamic_slice_in_dim(valid, own * part, part), image, jnp.zeros((), bf16))
    column = block_id // 2
    sent = [lax.dynamic_slice_in_dim(image, (column ^ dz) * 2 * cut, 2 * cut, 1) for dz in range(4)]
    mine = jnp.stack([sent[0]] + [swap(sent[dz], "sp", 2 * dz) for dz in (1, 2, 3)])
    wide_w = (C - narrow) // 4
    own_wide = lax.dynamic_slice_in_dim(x, narrow + own * wide_w, wide_w, 1)
    own_wide = jnp.where(valid, own_wide, jnp.zeros((), bf16))
    halo, made = side_taps((0, 1, 2), after(x, packed, own_wide, *sent))
    x_wide = lax.all_gather(own_wide, ("sp", "ch"), axis=0).reshape(BLOCKS, 4, cells, wide_w)
    x_then = after(x, made, halo[0], halo[1], mine)
    centre, sums = pl.pallas_call(
        functools.partial(centre_kernel, steps=steps, slabs=slabs, cols=cols, rates=rates, images=images),
        grid=(steps,),
        in_specs=[
            SMEM,
            x_spec,
            pl.BlockSpec((3, 1, 3, L, KT), lambda k: (0, 1, 0, 0, k)),
            pl.BlockSpec((L, KT), lambda k: (0, k)),
        ],
        out_specs=[pl.BlockSpec((cells, W), lambda k: (0, 0)), pl.BlockSpec((8, KT), lambda k: (0, k))],
        out_shape=[jax.ShapeDtypeStruct((cells, W), f32), jax.ShapeDtypeStruct((8, C), f32)],
        scratch_shapes=[pltpu.VMEM((10 * L, KT), bf16), pltpu.VMEM((cells, 10 * L), f32)],
        compiler_params=params(),
        cost_estimate=cost(2 * cells * C * 10 * L, 8e6),
        name="centre_taps",
    )(lim, x_then, atrous_weight, w_point)
    own_pooled = sums[:images] / own_count[:, None]
    proj_part = lax.dot_general(own_pooled, w_pool.astype(f32), NT, precision=highest_precision)

    extra = jnp.concatenate(
        [jnp.pad(proj_part, ((4, 4 - images), (0, W - L))), own_pooled.reshape(-1, W)], axis=0
    )
    conv, conv_send, message, local = pl.pallas_call(
        functools.partial(combine_kernel, slabs=slabs, cols=cols),
        in_specs=[SMEM] + [VMEM] * 8,
        out_specs=[VMEM] * 4,
        out_shape=[
            jax.ShapeDtypeStruct((cells, W), f32),
            jax.ShapeDtypeStruct((cells, W), bf16),
            jax.ShapeDtypeStruct(extra.shape, f32),
            jax.ShapeDtypeStruct((8, W), f32),
        ],
        compiler_params=params(20),
        cost_estimate=cost(2e6, 4e6),
        name="combine_taps",
    )(lim, centre, *halo, extra)
    conv_y = swap(conv_send, "ch", 2)
    conv_core = swap(conv_send, "ch", 1)
    message = parts_over_sp(message)
    conv_diag = swap(after(conv_y, *message), "ch", 1)
    tile = ((message[0][:8] + message[1][:8]) + (message[2][:8] + message[3][:8])) + local
    mine = after(mine, tile)
    keep = lax.dynamic_slice_in_dim(mine, (block_id % 2) * cut, cut, 2)
    give = lax.dynamic_slice_in_dim(mine, (1 - block_id % 2) * cut, cut, 2)
    taken = swap(give, "sp", 1)
    tiles = [tile] + [swap(tile, "ch", b) for b in (1, 2, 3)]
    projected = tile[4 : 4 + images, :L]
    pool_mean = jnp.mean(projected, axis=0)
    pool_rstd = lax.rsqrt(jnp.mean(projected * projected, axis=0) - pool_mean * pool_mean + epsilon)
    pool_normed = (projected - pool_mean) * pool_rstd
    pool_pre = bn_gains[4] * pool_normed + bn_shifts[4]
    pool_act = jax.nn.silu(pool_pre).astype(bf16)

    mixed, act, mixed_stat, own_stat = pl.pallas_call(
        functools.partial(mix_kernel, slabs=slabs, cols=cols, images=images),
        in_specs=[SMEM] * 2 + [VMEM] * 12,
        out_specs=[VMEM] * 4,
        out_shape=[
            jax.ShapeDtypeStruct((cells, F), f32),
            jax.ShapeDtypeStruct((cells, W), bf16),
            jax.ShapeDtypeStruct((8, F), f32),
            jax.ShapeDtypeStruct((8, W), f32),
        ],
        scratch_shapes=[pltpu.VMEM((cells, W), bf16)],
        compiler_params=params(20),
        cost_estimate=cost(2 * cells * 4 * W * F, 6e6),
        name="mix_branches",
    )(lim, count, conv, conv_core, conv_y, conv_diag, *tiles, *packed_all)
    total = parts_over_sp(mixed_stat)
    out_all, fdt, fsums, fstat = pl.pallas_call(
        functools.partial(final_kernel, slabs=slabs, cols=cols),
        in_specs=[SMEM] * 3 + [VMEM] * 10,
        out_specs=[VMEM] * 4,
        out_shape=[
            jax.ShapeDtypeStruct((cells, F), bf16),
            jax.ShapeDtypeStruct((cells, F), f32),
            jax.ShapeDtypeStruct((8, F), f32),
            jax.ShapeDtypeStruct((8, F), f32),
        ],
        compiler_params=params(20),
        cost_estimate=cost(2e6, 4e6),
        name="final_norm",
    )(lim, count, own_id, mixed, og, *packed_all, *total)
    ftotal = parts_over_sp(fsums)
    final_sums = (ftotal[0] + ftotal[1]) + (ftotal[2] + ftotal[3])
    final_beta, final_gamma = final_sums[0], final_sums[1]
    dt, gproj, image_sums, bsums = pl.pallas_call(
        functools.partial(branch_kernel, slabs=slabs, cols=cols, images=images),
        in_specs=[SMEM] * 2 + [VMEM] * 11,
        out_specs=[VMEM] * 4,
        out_shape=[
            jax.ShapeDtypeStruct((cells, W), f32),
            jax.ShapeDtypeStruct((W, F), f32),
            jax.ShapeDtypeStruct((8, F), f32),
            jax.ShapeDtypeStruct((8, W), f32),
        ],
        scratch_shapes=[pltpu.VMEM((cells, F), bf16)],
        compiler_params=params(20),
        cost_estimate=cost(4 * cells * W * F, 8e6),
        name="branch_grads",
    )(
        lim, count, mixed, fdt, fstat, conv, act, own_stat, wp[:W], *ftotal
    )
    image_sums = image_sums[:images]
    pool_part = lax.dot_general(image_sums, w_proj[4].astype(f32), NT, precision=highest_precision)
    gproj_pool = lax.dot_general(pool_act.astype(f32), image_sums, TN, precision=highest_precision)
    gp = jnp.concatenate([gproj, gproj_pool], axis=0)
    across, along = block_id % 2, block_id // 2
    gp_half, gp_piece = gp.shape[0] // 2, gp.shape[0] // BLOCKS
    bown = jnp.concatenate([bsums[:4], jnp.pad(pool_part, ((0, 0), (0, W - L)))], axis=0)
    got = swap(
        jnp.concatenate(
            [thirds(bown), lax.dynamic_slice_in_dim(gp, (1 - across) * gp_half, gp_half).astype(bf16)], axis=0
        ),
        "sp",
        1,
    )
    bown = bown + whole(got[:24])
    gp = lax.dynamic_slice_in_dim(gp, across * gp_half, gp_half) + got[24:].astype(f32)
    mine_thirds = thirds(bown)
    got = [
        swap(
            jnp.concatenate(
                [mine_thirds, lax.dynamic_slice_in_dim(gp, (along ^ dz) * gp_piece, gp_piece).astype(bf16)],
                axis=0,
            ),
            "sp",
            2 * dz,
        )
        for dz in (1, 2, 3)
    ]
    btile = (bown + whole(got[0][:24])) + (whole(got[1][:24]) + whole(got[2][:24]))
    gp = lax.dynamic_slice_in_dim(gp, along * gp_piece, gp_piece)
    gp = (gp + got[0][24:].astype(f32)) + (got[1][24:].astype(f32) + got[2][24:].astype(f32))
    gp = jnp.pad(gp, ((0, -gp_piece % 16), (0, 0)))
    branch_beta, branch_gamma = btile[0], btile[1]
    cgt = pl.pallas_call(
        functools.partial(grad_kernel, slabs=slabs, cols=cols),
        in_specs=[SMEM] * 2 + [VMEM] * 5,
        out_specs=VMEM,
        out_shape=jax.ShapeDtypeStruct((W + 16, cells), bf16),
        scratch_shapes=[pltpu.VMEM((cells, W), f32)],
        compiler_params=params(20),
        cost_estimate=cost(2e6, 4e6),
        name="conv_grads",
    )(lim, count, dt, conv, own_stat, btile, gp)
    pool_dt = btile[4 : 4 + images, :L] * silu_slope(pool_pre)
    pool_beta = jnp.sum(pool_dt, axis=0)
    pool_gamma = jnp.sum(pool_dt * pool_normed, axis=0)
    proj_grad = (
        pool_rstd * bn_gains[4] * (pool_dt - pool_beta / images - pool_normed * pool_gamma / images)
    )
    g_gains = jnp.concatenate([branch_gamma.reshape(4, L), pool_gamma[None],
        lax.dynamic_slice_in_dim(final_gamma, own * L, L)[None]], axis=0)
    g_shifts = jnp.concatenate([branch_beta.reshape(4, L), pool_beta[None],
        lax.dynamic_slice_in_dim(final_beta, own * L, L)[None]], axis=0)
    output = lax.dynamic_slice_in_dim(out_all, own * L, L, 1).reshape(images, rows_dev, cols, L)
    pooled_grad = (
        jnp.einsum("kf,fc->kc", proj_grad, w_pool.astype(f32), precision=highest_precision)
        / own_count[:, None]
    )
    ANY = pl.BlockSpec(memory_space=pl.ANY)
    col_row = jnp.broadcast_to((jnp.arange(cells, dtype=jnp.int32) % cols)[None, :], (8, cells))
    pos = jnp.stack([block_id, own % 2, own]).astype(jnp.int32)
    def column_taps(block):
        return pl.pallas_call(
            functools.partial(expand_kernel, cols=cols, rates=rates),
            grid=(1,),
            in_specs=[pl.BlockSpec((8, cells), lambda i: (0, 0)), pl.BlockSpec((W, cells), lambda i: (0, 0))],
            out_specs=pl.BlockSpec((10 * L, cells), lambda i: (0, 0)),
            out_shape=jax.ShapeDtypeStruct((10 * L, cells), bf16),
            compiler_params=params(),
            cost_estimate=cost(1e9, 6e6),
            name="column_taps",
        )(col_row, block)

    near = [swap(cgt, "sp", b) for b in (2, 4)]
    near.append(swap(after(cgt, near[0]), "sp", 6))
    pair = swap(cgt, "sp", 1)
    taps = [column_taps(cgt), column_taps(pair), column_taps(near[0])]
    near_pair = swap(near[0], "sp", 1)
    taps.append(column_taps(near_pair))
    message = after(tuple(message), pair)
    pooled = ((message[0][8:] + message[1][8:]) + (message[2][8:] + message[3][8:])).reshape(images, C)
    x_slices = after(jnp.stack([keep, taken], axis=1).reshape(1, BLOCKS, part, cut), pair)
    x_slices = jnp.concatenate([x_slices, swap(x_slices, "ch", 2)], axis=0)
    x_core = swap(x_slices, "ch", 1)
    g_pool = jnp.einsum("kf,kc->fc", proj_grad, pooled, precision=highest_precision)
    far = [after(near[1], *taps[:2], output, g_pool, g_gains, g_shifts, pooled_grad), after(near[2], *taps)]
    far_pairs = [swap(t, "sp", 1) for t in far]
    blocks = [cgt, pair, near[0], near_pair, far[0], far_pairs[0], far[1], far_pairs[1]]
    taps += [column_taps(t) for t in blocks[4:]]
    eighth = narrow // BLOCKS
    tap_scratch = pltpu.VMEM((10 * L, BLOCKS * cells), bf16)
    gw = pl.pallas_call(
        functools.partial(narrow_kernel, parts=images),
        in_specs=[SMEM] + [ANY] * (BLOCKS + 2),
        out_specs=pl.BlockSpec((28 * L, eighth), lambda i: (0, 0)),
        grid=(1,),
        out_shape=jax.ShapeDtypeStruct((28 * L, eighth), bf16),
        scratch_shapes=[
            tap_scratch,
            pltpu.VMEM((BLOCKS * cells, eighth), bf16),
            pltpu.SemaphoreType.DMA((BLOCKS,)),
            pltpu.SemaphoreType.DMA((images, BLOCKS)),
        ],
        compiler_params=params(),
        cost_estimate=cost(2 * cells * BLOCKS * 28 * L * eighth, 12e6),
        name="narrow_weight_grads",
    )(pos, *taps, x_slices, x_core)
    gw_all = lax.all_gather(gw, "sp", axis=0)
    pos, gw = lax.optimization_barrier((pos, gw))
    group = C // 4
    ig_keep, ig_give = pl.pallas_call(
        functools.partial(input_grad_kernel, slabs=slabs, cols=cols, rates=rates, images=images),
        grid_spec=pltpu.PrefetchScalarGridSpec(
            num_scalar_prefetch=2,
            grid=(4,),
            in_specs=[
                pl.BlockSpec((8, cells), lambda i, p, l: (0, 0)),
                pl.BlockSpec((27 * L, group), lambda i, p, l: (0, p[2] ^ i)),
                pl.BlockSpec((L, group), lambda i, p, l: (0, p[2] ^ i)),
                pl.BlockSpec((8, group), lambda i, p, l: (0, p[2] ^ i)),
            ]
            + [ANY] * BLOCKS,
            out_specs=[pl.BlockSpec((1, cells, group), lambda i, p, l: (i // 2, 0, 0))] * 2,
            scratch_shapes=[
                pltpu.VMEM((BLOCKS, W, cells), bf16),
                pltpu.VMEM((cells, 28 * L), bf16),
                pltpu.VMEM((28 * L, group), bf16),
                pltpu.SemaphoreType.DMA((BLOCKS,)),
            ],
        ),
        out_shape=[jax.ShapeDtypeStruct((2, cells, group), bf16)] * 2,
        compiler_params=params(),
        cost_estimate=cost(1e6, 1e6),
        name="input_grads",
    )(pos, lim, col_row, atrous_weight.reshape(27 * L, C), w_point,
      jnp.pad(pooled_grad, ((0, 8 - images), (0, 0))), *blocks)
    from_core = swap(ig_give, "ch", 1)

    from_core = from_core.astype(f32)
    keep = ig_keep[0].astype(f32) + from_core[0]
    give = (ig_keep[1].astype(f32) + from_core[1]).astype(bf16)
    given = swap(give, "ch", 2)
    pos = after(pos, give)
    g_wide, p_wide, g_proj = pl.pallas_call(
        wide_kernel,
        grid=(4,),
        in_specs=[SMEM, pl.BlockSpec((BLOCKS, 1, cells, wide_w), lambda i: (0, i, 0, 0))]
        + [ANY] * BLOCKS
        + [pl.BlockSpec((16, cells), lambda i: (W // 16, 0))] * BLOCKS,
        out_specs=[
            pl.BlockSpec((27 * L, wide_w), lambda i: (0, narrow // wide_w + i)),
            pl.BlockSpec((L, wide_w), lambda i: (0, narrow // wide_w + i)),
            pl.BlockSpec((5 * L, F), lambda i: (0, 0)),
        ],
        out_shape=[
            jax.ShapeDtypeStruct((27 * L, C), f32),
            jax.ShapeDtypeStruct((L, C), f32),
            jax.ShapeDtypeStruct((5 * L, F), f32),
        ],
        scratch_shapes=[tap_scratch, pltpu.SemaphoreType.DMA((BLOCKS,))],
        compiler_params=params(),
        cost_estimate=cost(1e6, 1e6),
        name="wide_weight_grads",
    )(pos, x_wide, *taps, *blocks)
    g_proj = g_proj.reshape(5, L, F)
    in_grad = (keep + after(given, p_wide).astype(f32)).astype(bf16)
    in_grad = in_grad.reshape(images, rows_dev, cols, group)

    step = 9 * L
    g_atrous, g_point = pl.pallas_call(
        widen_kernel,
        grid=(3,),
        in_specs=[
            pl.BlockSpec((BLOCKS, step, eighth), lambda i: (0, i, 0)),
            pl.BlockSpec((BLOCKS, L, eighth), lambda i: (0, 27, 0)),
            ANY,
            ANY,
        ],
        out_specs=[
            pl.BlockSpec((step, narrow), lambda i: (i, 0)),
            pl.BlockSpec((L, narrow), lambda i: (0, 0)),
        ],
        out_shape=[jax.ShapeDtypeStruct((27 * L, C), f32), jax.ShapeDtypeStruct((L, C), f32)],
        input_output_aliases={2: 0, 3: 1},
        compiler_params=params(),
        cost_estimate=cost(1e6, 20e6),
        name="widen",
    )(gw_all, gw_all, g_wide, p_wide)
    g_atrous = g_atrous.reshape(3, 3, 3, L, C)
    return (output, in_grad, g_point, g_atrous, g_pool, g_proj, g_gains, g_shifts)


def solution(mesh):
    placed = (
        P(None, "sp", None, None),
        P(),
        P(),
        P("ch", None),
        P(None, None, None, "ch", None),
        P("ch", None),
        P(None, "ch", None),
        P(None, "ch"),
        P(None, "ch"),
        P(None, "sp", None, None),
    )
    return jax.shard_map(
        body,
        mesh=mesh,
        in_specs=placed,
        out_specs=(
            P(None, "sp", None, "ch"),
            P(None, "sp", None, "ch"),
            P("ch", None),
            P(None, None, None, "ch", None),
            P("ch", None),
            P(None, "ch", None),
            P(None, "ch"),
            P(None, "ch"),
        ),
        check_vma=False,
    )
```

```python
import functools

import jax
import jax.numpy as jnp
from jax import lax
from jax.experimental import pallas as pl
from jax.experimental.pallas import tpu as pltpu
from jax.sharding import PartitionSpec as P

BLOCKS = 8
BRANCHES = 4
epsilon = 1e-05
dilation_factors = (1, 2, 3)
highest_precision = lax.Precision.HIGHEST
f32 = jnp.float32
bf16 = jnp.bfloat16
MIB = 1 << 20
VMEM = pl.BlockSpec(memory_space=pltpu.VMEM)
SMEM = pl.BlockSpec(memory_space=pltpu.SMEM)
NT = (((1,), (1,)), ((), ()))
NN = (((1,), (0,)), ((), ()))
TN = (((0,), (0,)), ((), ()))


def dot(a, b, dims):
    return lax.dot_general(a, b, dims, preferred_element_type=f32)


def params(mib=60, **kw):
    return pltpu.CompilerParams(vmem_limit_bytes=mib * MIB, **kw)


def cost(flops, nbytes):
    return pl.CostEstimate(flops=int(flops), bytes_accessed=int(nbytes), transcendentals=0)


def cell_mask(lim_ref, slabs, cols, width):
    col = lax.broadcasted_iota(jnp.int32, (cols, width), 0)
    return jnp.concatenate([(col < lim_ref[i]).astype(f32) for i in range(slabs)], axis=0)


def column_ids(slabs, cols, width):
    return lax.broadcasted_iota(jnp.int32, (slabs, cols, width), 1).reshape(slabs * cols, width)


def from_left(a, d, col):
    return jnp.where(col >= d, pltpu.roll(a, d, 0), 0.0)


def from_right(a, d, col, cols):
    return jnp.where(col < cols - d, pltpu.roll(a, a.shape[0] - d, 0), 0.0)


def silu_parts(t):
    s = 1.0 / (1.0 + jnp.exp(-t))
    return s, t * s


def slope(t, s):
    return s * (1.0 + t * (1.0 - s))


def column_sums(*rows):
    sums = [jnp.sum(r, axis=0, keepdims=True) for r in rows]
    width = sums[0].shape[1]
    return jnp.concatenate(sums + [jnp.zeros((8 - len(sums), width), f32)], axis=0)


def side_kernel(lim_ref, low_ref, x_ref, *refs, steps, slabs, cols, rates):
    n_rates = len(rates)
    weights, outs, (wcat, acc) = refs[: 2 * n_rates], refs[2 * n_rates : 4 * n_rates], refs[4 * n_rates :]
    k = pl.program_id(0)
    L = weights[0].shape[3]
    for j in range(n_rates):
        for v in range(3):
            t = (j * 3 + v) * 2 * L
            wcat[t : t + L] = weights[2 * j][0, 0, v]
            wcat[t + L : t + 2 * L] = weights[2 * j + 1][0, 0, v]

    @pl.when(k == 0)
    def _():
        acc[...] = jnp.zeros_like(acc)

    x = x_ref[...]
    total = 6 * n_rates * L
    for n in range(0, total, 256):
        e = min(n + 256, total)
        acc[:, n:e] += dot(x, wcat[n:e], NT)

    @pl.when(k == steps - 1)
    def _():
        cells = slabs * cols
        half = cells // 2
        mask = cell_mask(lim_ref, slabs, cols, 2 * L)
        col = column_ids(slabs, cols, 2 * L)
        low = lax.broadcasted_iota(jnp.int32, (half, 2 * L), 1) < L
        for j in range(n_rates):
            a = [acc[:, (j * 3 + v) * 2 * L : (j * 3 + v + 1) * 2 * L] * mask for v in range(3)]
            s = a[1] + from_left(a[0], rates[j], col) + from_right(a[2], rates[j], col, cols)
            top, bottom = s[:half], s[half:]
            up = jnp.where(low, top, pltpu.roll(bottom, L, 1))
            down = jnp.where(low, pltpu.roll(top, L, 1), bottom)
            first = low_ref[j] == 1
            outs[2 * j][...] = jnp.where(first, up, down).astype(bf16)
            outs[2 * j + 1][...] = jnp.where(first, down, up).astype(bf16)


def centre_kernel(
    lim_ref, x_ref, wc_ref, wpoint_ref, out_ref, sums_ref, wcat, acc, *, steps, slabs, cols, rates, images
):
    k = pl.program_id(0)
    L = wpoint_ref.shape[0]
    order = [None, (0, 1), (1, 1), (2, 1), (1, 0), (2, 0), (1, 2), (2, 2), (0, 0), (0, 2)]
    for i, tap in enumerate(order):
        wcat[i * L : (i + 1) * L] = wpoint_ref[...] if tap is None else wc_ref[tap[0], 0, tap[1]]

    @pl.when(k == 0)
    def _():
        acc[...] = jnp.zeros_like(acc)

    x = x_ref[...]
    total = 10 * L
    for n in range(0, total, 256):
        e = min(n + 256, total)
        acc[:, n:e] += dot(x, wcat[n:e], NT)

    width = x_ref.shape[1]
    cid = lax.broadcasted_iota(jnp.int32, (cols, width), 0)
    per = slabs // images
    sums = []
    for image in range(images):
        part = jnp.zeros((cols, width), f32)
        for i in range(image * per, (image + 1) * per):
            part += jnp.where(cid < lim_ref[i], x_ref[i * cols : (i + 1) * cols].astype(f32), 0.0)
        sums.append(jnp.sum(part, axis=0, keepdims=True))
    sums_ref[...] = jnp.concatenate(sums + [jnp.zeros((8 - images, width), f32)], axis=0)

    @pl.when(k == steps - 1)
    def _():
        cells = slabs * cols
        mask = cell_mask(lim_ref, slabs, cols, 2 * L)
        col = column_ids(slabs, cols, 2 * L)
        low = lax.broadcasted_iota(jnp.int32, (cells, 2 * L), 1) < L
        b = [acc[:, i * 2 * L : (i + 1) * 2 * L] * mask for i in range(5)]
        d0, d1, d2 = rates
        t = jnp.where(low, from_left(b[4], d0, col), from_right(b[4], d0, col, cols))
        out_ref[:, : 2 * L] = b[0] + jnp.where(low, 0.0, t + pltpu.roll(t, L, 1))
        out_ref[:, 2 * L :] = (
            b[1]
            + jnp.where(low, from_left(b[2], d1, col), from_left(b[2], d2, col))
            + jnp.where(low, from_right(b[3], d1, col, cols), from_right(b[3], d2, col, cols))
        )


def combine_kernel(lim_ref, centre_ref, *refs, slabs, cols):
    halo, (extra_ref, conv_ref, send_ref, message_ref, local_ref) = refs[:6], refs[6:]
    cells = slabs * cols
    half = cells // 2
    W = centre_ref.shape[1]
    L = W // 4
    h = [halo[2 * j][...].astype(f32) + halo[2 * j + 1][...].astype(f32) for j in range(3)]
    turned = [pltpu.roll(a, L, 1) for a in h]
    low = lax.broadcasted_iota(jnp.int32, (cells, 2 * L), 1) < L
    h0 = jnp.concatenate([turned[0], h[0]], axis=0)
    h1 = jnp.concatenate([h[1], turned[1]], axis=0)
    h2 = jnp.concatenate([turned[2], h[2]], axis=0)
    left = centre_ref[:, : 2 * L] + jnp.where(low, 0.0, h0)
    right = centre_ref[:, 2 * L :] + jnp.where(low, h1, h2)
    conv_ref[:, : 2 * L] = left
    conv_ref[:, 2 * L :] = right
    mask = cell_mask(lim_ref, slabs, cols, 2 * L)
    own = lim_ref[0]
    for i in range(1, slabs):
        own = own + lim_ref[i]
    own = jnp.maximum(own, 1).astype(f32)
    for lo, part in ((0, left), (2 * L, right)):
        s = jnp.sum(part * mask, axis=0, keepdims=True)
        q = jnp.sum(part * part * mask, axis=0, keepdims=True)
        local = s / own
        send_ref[:, lo : lo + 2 * L] = (part - local).astype(bf16)
        message_ref[:8, lo : lo + 2 * L] = extra_ref[:8, lo : lo + 2 * L] + jnp.concatenate(
            [s, q, jnp.zeros((6, 2 * L), f32)], axis=0
        )
        local_ref[:, lo : lo + 2 * L] = jnp.concatenate(
            [jnp.zeros((2, 2 * L), f32), local, jnp.zeros((5, 2 * L), f32)], axis=0
        )
    message_ref[8:] = extra_ref[8:]


def norm_of(total, square, n):
    mean = total / n
    return mean, lax.rsqrt(square / n - mean * mean + epsilon)


def added(parts):
    a, b, c, d = (r[...] for r in parts)
    return (a + b) + (c + d)


def mix_kernel(
    lim_ref, n_ref, conv_ref, c1_ref, c2_ref, c3_ref, t0, t1, t2, t3, p0, p1, p2, p3,
    mixed_ref, act_ref, sums_ref, stat_ref, scratch, *, slabs, cols, images
):
    per = slabs // images
    n = n_ref[0]
    width = conv_ref.shape[1]
    L = width // 4
    cid = lax.broadcasted_iota(jnp.int32, (cols, width), 0)
    pooled = None
    for d, (ref, tile_ref, par_ref) in enumerate(
        ((conv_ref, t0, p0), (c1_ref, t1, p1), (c2_ref, t2, p2), (c3_ref, t3, p3))
    ):
        tile = tile_ref[...]
        par = par_ref[5 * L :].astype(f32)
        par = par[0:4] + par[4:8] + par[8:12]
        gain = par[0:1]
        shift = jnp.concatenate([par[1:2, 2 * L :], par[2:3, : 2 * L]], axis=1)
        mean, rstd = norm_of(tile[0:1], tile[1:2], n)
        offset = mean if d == 0 else mean - tile[2:3]
        scale = rstd * gain
        if d == 0:
            stat_ref[...] = jnp.concatenate([mean, rstd, gain, shift, jnp.zeros((4, width), f32)], axis=0)
        dest = act_ref if d == 0 else scratch
        for i in range(slabs):
            rows = slice(i * cols, (i + 1) * cols)
            pre = (ref[rows].astype(f32) - offset) * scale + shift
            _, act = silu_parts(pre)
            dest[rows] = jnp.where(cid < lim_ref[i], act, 0.0).astype(bf16)
        part = dot(dest[...], par_ref[:width], NN)
        if d == 0:
            mixed_ref[...] = part
        else:
            mixed_ref[...] += part
        projected = tile[4 : 4 + images, :L]
        pmean, prstd = norm_of(
            jnp.sum(projected, axis=0, keepdims=True), jnp.sum(projected * projected, axis=0, keepdims=True), images
        )
        _, pact = silu_parts(par[1:2, :L] * ((projected - pmean) * prstd) + par[2:3, 2 * L : 3 * L])
        pact = jnp.concatenate([pact, jnp.zeros((16 - images, L), f32)], axis=0).astype(bf16)
        part = dot(pact, par_ref[width : width + L], NN)
        pooled = part if d == 0 else pooled + part
    F = mixed_ref.shape[1]
    cid = lax.broadcasted_iota(jnp.int32, (cols, F), 0)
    s = jnp.zeros((cols, F), f32)
    q = jnp.zeros((cols, F), f32)
    for i in range(slabs):
        rows = slice(i * cols, (i + 1) * cols)
        image = i // per
        value = mixed_ref[rows] + jnp.where(cid < lim_ref[i], pooled[image : image + 1], 0.0)
        mixed_ref[rows] = value
        s += value
        q += value * value
    sums_ref[...] = column_sums(s, q)


def final_kernel(
    lim_ref, n_ref, own_ref, mixed_ref, grad_ref, p0, p1, p2, p3, s0, s1, s2, s3, out_ref, dt_ref, sums_ref, stat_ref,
    *, slabs, cols
):
    F = mixed_ref.shape[1]
    total = added((s0, s1, s2, s3))
    mean, rstd = norm_of(total[0:1], total[1:2], n_ref[0])
    L = F // 4
    group = lax.broadcasted_iota(jnp.int32, (8, F), 1) // L
    gain, shift = jnp.zeros((8, F), f32), jnp.zeros((8, F), f32)
    for d, ref in enumerate((p0, p1, p2, p3)):
        par = ref[5 * L :].astype(f32)
        par = par[0:4] + par[4:8] + par[8:12]
        here = group == (own_ref[0] ^ d)
        g = jnp.where(group == 1, jnp.broadcast_to(par[1:2], (8, F)), 0.0)
        h = jnp.where(group == 3, jnp.broadcast_to(par[2:3], (8, F)), 0.0)
        gain += jnp.where(here, g + pltpu.roll(g, L, 1) + pltpu.roll(g, 2 * L, 1) + pltpu.roll(g, 3 * L, 1), 0.0)
        shift += jnp.where(here, h + pltpu.roll(h, L, 1) + pltpu.roll(h, 2 * L, 1) + pltpu.roll(h, 3 * L, 1), 0.0)
    gain, shift = gain[0:1], shift[0:1]
    stat_ref[...] = jnp.concatenate([mean, rstd, gain, shift, jnp.zeros((4, F), f32)], axis=0)
    cid = lax.broadcasted_iota(jnp.int32, (cols, F), 0)
    s = jnp.zeros((cols, F), f32)
    q = jnp.zeros((cols, F), f32)
    for i in range(slabs):
        rows = slice(i * cols, (i + 1) * cols)
        valid = cid < lim_ref[i]
        normed = (mixed_ref[rows] - mean) * rstd
        pre = gain * normed + shift
        sig, act = silu_parts(pre)
        out_ref[rows] = jnp.where(valid, act, 0.0).astype(bf16)
        dt = jnp.where(valid, grad_ref[rows].astype(f32) * slope(pre, sig), 0.0)
        dt_ref[rows] = dt
        s += dt
        q += dt * normed
    sums_ref[...] = column_sums(s, q)


def branch_kernel(
    lim_ref, n_ref, mixed_ref, fdt_ref, fstat_ref, conv_ref, act_ref, stat_ref, wbranch_ref, s0, s1, s2, s3,
    dt_ref, gproj_ref, image_ref, sums_ref, grad, *, slabs, cols, images
):
    F = mixed_ref.shape[1]
    W = conv_ref.shape[1]
    per = slabs // images
    mean, rstd, scale = fstat_ref[0:1], fstat_ref[1:2], fstat_ref[1:2] * fstat_ref[2:3]
    total = added((s0, s1, s2, s3)) / n_ref[0]
    beta, gamma = total[0:1], total[1:2]
    cid = lax.broadcasted_iota(jnp.int32, (cols, F), 0)
    image_sums = []
    for image in range(images):
        total = jnp.zeros((cols, F), f32)
        for i in range(image * per, (image + 1) * per):
            rows = slice(i * cols, (i + 1) * cols)
            normed = (mixed_ref[rows] - mean) * rstd
            g = jnp.where(cid < lim_ref[i], scale * (fdt_ref[rows] - beta - normed * gamma), 0.0)
            g = g.astype(bf16)
            grad[rows] = g
            total += g.astype(f32)
        image_sums.append(jnp.sum(total, axis=0, keepdims=True))
    image_ref[...] = jnp.concatenate(image_sums + [jnp.zeros((8 - images, F), f32)], axis=0)
    dt_ref[...] = dot(grad[...], wbranch_ref[...], NT)
    gproj_ref[...] = dot(act_ref[...], grad[...], TN)
    bmean, brstd, bgain, bshift = (stat_ref[i : i + 1] for i in range(4))
    cid = lax.broadcasted_iota(jnp.int32, (cols, W), 0)
    s = jnp.zeros((cols, W), f32)
    q = jnp.zeros((cols, W), f32)
    for i in range(slabs):
        rows = slice(i * cols, (i + 1) * cols)
        normed = (conv_ref[rows] - bmean) * brstd
        pre = bgain * normed + bshift
        sig, _ = silu_parts(pre)
        dt = jnp.where(cid < lim_ref[i], dt_ref[rows] * slope(pre, sig), 0.0)
        dt_ref[rows] = dt
        s += dt
        q += dt * normed
    sums_ref[...] = column_sums(s, q)


def grad_kernel(lim_ref, n_ref, dt_ref, conv_ref, stat_ref, sums_ref, piece_ref, cg_ref, scratch, *, slabs, cols):
    W = conv_ref.shape[1]
    mean, rstd, scale = stat_ref[0:1], stat_ref[1:2], stat_ref[1:2] * stat_ref[2:3]
    beta, gamma = sums_ref[0:1] / n_ref[0], sums_ref[1:2] / n_ref[0]
    cid = lax.broadcasted_iota(jnp.int32, (cols, W), 0)
    for i in range(slabs):
        rows = slice(i * cols, (i + 1) * cols)
        normed = (conv_ref[rows] - mean) * rstd
        g = scale * (dt_ref[rows] - beta - normed * gamma)
        scratch[rows] = jnp.where(cid < lim_ref[i], g, 0.0)
    cg_ref[:W] = scratch[...].T.astype(bf16)
    F = piece_ref.shape[1]
    for k in range(piece_ref.shape[0] // 16):
        cg_ref[W:, k * F : (k + 1) * F] = piece_ref[k * 16 : (k + 1) * 16].astype(bf16)


def shifted(f, v, d, col, cols):
    if v == 1:
        return f
    if v == 2:
        return jnp.where(col >= d, pltpu.roll(f, d, 1), 0.0)
    return jnp.where(col < cols - d, pltpu.roll(f, f.shape[1] - d, 1), 0.0)


def expand_kernel(col_ref, cg_ref, out_ref, *, cols, rates):
    L = cg_ref.shape[0] // 4
    for j in range(3):
        raw = cg_ref[(j + 1) * L : (j + 2) * L]
        f = raw.astype(f32)
        col = jnp.broadcast_to(col_ref[0:1], f.shape)
        base = 3 * j * L
        out_ref[base : base + L] = shifted(f, 0, rates[j], col, cols).astype(bf16)
        out_ref[base + L : base + 2 * L] = raw
        out_ref[base + 2 * L : base + 3 * L] = shifted(f, 2, rates[j], col, cols).astype(bf16)
    out_ref[9 * L :] = cg_ref[:L]


def fetch_blocks(pos, blocks, dest, sems, lanes=False):
    copies = []
    for d, ref in enumerate(blocks):
        place = pos ^ d
        if lanes:
            cells = ref.shape[1]
            spot = dest.at[:, pl.ds(pl.multiple_of(place * cells, 128), cells)]
        else:
            spot = dest.at[place]
        source = ref if lanes else ref.at[pl.ds(0, dest.shape[1])]
        copies.append(pltpu.make_async_copy(source, spot, sems.at[d]))
    for c in copies:
        c.start()
    return copies


def tap_products(store, taps, x_rows, L):
    cells = taps.shape[1] // BLOCKS
    own_row = dot(taps[...], x_rows(0, BLOCKS), NN)
    for j in range(3):
        lo = (j * 3 + 1) * 3 * L
        store(lo, own_row[3 * j * L : 3 * (j + 1) * L])
    store(27 * L, own_row[9 * L :])
    for j in range(3):
        rows = slice(3 * j * L, 3 * (j + 1) * L)
        span = (BLOCKS - 1 - j) * cells
        far = (j + 1) * cells
        store(j * 9 * L, dot(taps[rows, far:], x_rows(0, BLOCKS - 1 - j), NN))
        store((j * 3 + 2) * 3 * L, dot(taps[rows, :span], x_rows(j + 1, BLOCKS), NN))


def narrow_kernel(pos_ref, *refs, parts):
    blocks, (xown_ref, xcore_ref, out_ref, taps, x, sems, xsems) = refs[:BLOCKS], refs[BLOCKS:]
    pos, ch = pos_ref[0], pos_ref[2]
    L = taps.shape[0] // 10
    cells = taps.shape[1] // BLOCKS
    rows = xown_ref.shape[2]
    copies = fetch_blocks(pos, blocks, taps, sems, lanes=True)
    for e in range(parts):
        for d in range(BLOCKS):
            place = pl.ds(pl.multiple_of((pos ^ d) * cells + (ch ^ e) * rows, 16), rows)
            source = (xown_ref, xcore_ref)[e % 2].at[e // 2, d]
            c = pltpu.make_async_copy(source, x.at[place], xsems.at[e, d])
            c.start()
            copies.append(c)
    for c in copies:
        c.wait()

    def store(lo, value):
        out_ref[lo : lo + value.shape[0]] = value.astype(bf16)

    tap_products(store, taps, lambda lo, hi: x[lo * cells : hi * cells], L)


def wide_kernel(pos_ref, x_ref, *refs):
    blocks, pieces, (acc_ref, point_ref, proj_ref, taps, sems) = (
        refs[:BLOCKS],
        refs[BLOCKS : 2 * BLOCKS],
        refs[2 * BLOCKS :],
    )
    L = point_ref.shape[0]
    F = proj_ref.shape[1]
    rows = proj_ref.shape[0] // BLOCKS

    @pl.when(pl.program_id(0) == 0)
    def _():
        copies = fetch_blocks(pos_ref[0], blocks, taps, sems, lanes=True)
        for d in range(BLOCKS):
            p = pos_ref[0] ^ d
            base = (p % 2 * (BLOCKS // 2) + p // 2) * rows
            for k in range(0, rows, 16):
                n = min(16, rows - k)
                value = pieces[d][:, k // 16 * F : (k // 16 + 1) * F].astype(f32)
                proj_ref[pl.ds(pl.multiple_of(base + k, 8), n)] = value[:n]
        for c in copies:
            c.wait()

    def store(lo, value):
        if lo < 27 * L:
            acc_ref[lo : lo + value.shape[0]] = value
        else:
            point_ref[...] = value

    w = x_ref.shape[3]
    tap_products(store, taps, lambda lo, hi: x_ref[lo:hi, 0].reshape(-1, w), L)


def widen_kernel(in_ref, pin_ref, keep_ref, pkeep_ref, out_ref, pout_ref):
    w = in_ref.shape[2]
    for s in range(BLOCKS):
        out_ref[:, s * w : (s + 1) * w] = in_ref[s].astype(f32)
        pout_ref[:, s * w : (s + 1) * w] = pin_ref[s].astype(f32)


def input_grad_kernel(pos_ref, lim_ref, col_ref, w_ref, wp_ref, pool_ref, *refs, slabs, cols, rates, images):
    blocks, (keep_ref, give_ref, cg, lhs, rhs, sems) = refs[:BLOCKS], refs[BLOCKS:]
    L = wp_ref.shape[0]
    s = pos_ref[0]

    @pl.when(pl.program_id(0) == 0)
    def _():
        for c in fetch_blocks(s, blocks, cg, sems):
            c.wait()
        pieces = []
        order = [(j, u, v) for j in range(3) for u in range(3) for v in range(3)] + [None]
        for i, tap in enumerate(order):
            if tap is None:
                pieces.append(cg[s, 0:L].astype(f32))
            else:
                j, u, v = tap
                b = s - (u - 1) * (j + 1)
                inside = ((b >= 0) & (b < BLOCKS)).astype(f32)
                f = cg[jnp.clip(b, 0, BLOCKS - 1), (j + 1) * L : (j + 2) * L].astype(f32) * inside
                col = jnp.broadcast_to(col_ref[0:1], f.shape)
                pieces.append(shifted(f, v, rates[j], col, cols))
            if i % 4 == 3:
                lhs[:, (i - 3) * L : (i + 1) * L] = jnp.concatenate(pieces, axis=0).T.astype(bf16)
                pieces = []

    rhs[: 27 * L] = w_ref[...]
    rhs[27 * L :] = wp_ref[...]
    width = keep_ref.shape[2]
    per = slabs // images
    cid = lax.broadcasted_iota(jnp.int32, (cols, 256), 0)

    def fill(out_ref):
        for n in range(0, width, 256):
            part = dot(lhs[...], rhs[:, n : n + 256], NN)
            for i in range(slabs):
                value = part[i * cols : (i + 1) * cols] + pool_ref[i // per : i // per + 1, n : n + 256]
                out_ref[0, i * cols : (i + 1) * cols, n : n + 256] = jnp.where(
                    cid < lim_ref[i], value, 0.0
                ).astype(bf16)

    @pl.when(pl.program_id(0) % 2 == 0)
    def _():
        fill(keep_ref)

    @pl.when(pl.program_id(0) % 2 == 1)
    def _():
        fill(give_ref)


def grouped(pairs, size):
    return [(g * BLOCKS + a, g * BLOCKS + b) for g in range(size // BLOCKS) for a, b in pairs]


def neighbours(first, second, axis, distance):
    size = lax.axis_size(axis)
    rounds = []
    for parity, block in ((0, first), (1, second)):
        lows = [a for a in range(BLOCKS - distance) if (a // distance) % 2 == parity]
        pairs = [(a, a + distance) for a in lows] + [(a + distance, a) for a in lows]
        rounds.append(lax.ppermute(block, axis, grouped(pairs, size)))
    return rounds


def swap(block, axis, bits):
    return lax.ppermute(block, axis, [(i, i ^ bits) for i in range(lax.axis_size(axis))])


def parts_over_sp(x):
    x = x + swap(x, "sp", 1)
    return [x] + [swap(x, "sp", b) for b in (2, 4, 6)]


def swaps_over_sp(x):
    blocks = [x, None] + [swap(x, "sp", b) if b % 2 == 0 else None for b in range(2, BLOCKS)]
    for b in range(1, BLOCKS, 2):
        blocks[b] = swap(blocks[b - 1], "sp", 1)
    return blocks


def after(x, *others):
    return lax.optimization_barrier((x, others))[0]


def thirds(x):
    hi = lax.reduce_precision(x, 8, 7)
    mid = lax.reduce_precision(x - hi, 8, 7)
    return jnp.concatenate([hi, mid, x - hi - mid], axis=0).astype(bf16)


def whole(parts):
    hi, mid, low = jnp.split(parts.astype(f32), 3, axis=0)
    return hi + mid + low


def plain_from_behind(block, axis, distance):
    devices = range(lax.axis_size(axis))
    route = [(i - distance, i) for i in devices if i - distance in devices]
    return lax.ppermute(block, axis, route)


def shift_cols(values, offset):
    margin = abs(offset)
    padded = jnp.pad(values, ((0, 0), (0, 0), (margin, margin), (0, 0)))
    return lax.slice_in_dim(padded, margin + offset, margin + offset + values.shape[2], axis=2)


def silu_slope(pre_act):
    sigmoid_val = jax.nn.sigmoid(pre_act)
    return sigmoid_val * (1.0 + pre_act * (1.0 - sigmoid_val))


def source_inside(block_id, shift_amount):
    source = block_id - shift_amount
    return (source >= 0) & (source < BLOCKS)


def move_features(values, shift_amount):
    return plain_from_behind(values, "sp", shift_amount)


def shifted_gradients(values, shift_amount):
    return plain_from_behind(values, "sp", shift_amount)


def tap_partials(source, weight_taps, dilation_rate):
    count_k, rows_dev, grid_width, channel_total = source.shape
    local_output = weight_taps.shape[1]
    products = jnp.einsum(
        "pc,tc->pt",
        source.reshape(-1, channel_total),
        weight_taps.reshape(3 * local_output, channel_total),
        preferred_element_type=jnp.float32,
    ).reshape(count_k, rows_dev, grid_width, 3, local_output)
    return (
        shift_cols(products[:, :, :, 0, :], -dilation_rate)
        + products[:, :, :, 1, :]
        + shift_cols(products[:, :, :, 2, :], dilation_rate)
    )


def plain_body(
    features, heights, widths, w_point, atrous_weight, w_pool, w_proj, bn_gains, bn_shifts, out_grad
):
    count_k, rows_dev, grid_width, channel_total = features.shape
    local_output = w_point.shape[0]
    full_out = w_proj.shape[2]
    groups = heights.shape[1]
    images = count_k * groups
    pixels = count_k * rows_dev * grid_width
    position = lax.axis_index("sp")
    block_id = position % BLOCKS
    group_id = position // BLOCKS
    channel_start = lax.axis_index("ch") * local_output
    own_out_grad = lax.dynamic_slice_in_dim(out_grad, channel_start, local_output, 3)
    group_pick = jnp.arange(groups, dtype=jnp.int32) == group_id
    group_onehot = group_pick.astype(jnp.float32)
    own_heights = jnp.sum(jnp.where(group_pick[None, :], heights, 0), axis=1)
    own_widths = jnp.sum(jnp.where(group_pick[None, :], widths, 0), axis=1)
    row_ids = block_id * rows_dev + jnp.arange(rows_dev, dtype=jnp.int32)
    col_ids = jnp.arange(grid_width, dtype=jnp.int32)
    inside = (row_ids[None, :, None] < own_heights[:, None, None]) & (
        col_ids[None, None, :] < own_widths[:, None, None]
    )
    pix_mask = inside.astype(jnp.float32)[..., None]
    valid_count = jnp.sum((heights * widths).astype(jnp.float32))
    own_count = (own_heights * own_widths).astype(jnp.float32)
    masked_values = features * pix_mask.astype(jnp.bfloat16)
    flat_pix = masked_values.reshape(pixels, channel_total)
    point_conv = jnp.einsum("pc,fc->pf", flat_pix, w_point, preferred_element_type=jnp.float32)
    conv_list = [point_conv.reshape(count_k, rows_dev, grid_width, local_output)]
    for dilation_index, dilation_factor in enumerate(dilation_factors):
        dilation_rate = rows_dev * dilation_factor
        running_total = tap_partials(masked_values, atrous_weight[dilation_index, 1], dilation_rate)
        for row_offset_tap in (0, 2):
            shift_amount = (1 - row_offset_tap) * dilation_factor
            keep_rows = source_inside(block_id, shift_amount)
            received_part = move_features(masked_values, shift_amount) * keep_rows.astype(
                jnp.bfloat16
            )
            running_total = running_total + tap_partials(
                received_part, atrous_weight[dilation_index, row_offset_tap], dilation_rate
            )
        conv_list.append(running_total)
    conv_out = jnp.stack(conv_list)
    stat_sum, stat_square = lax.psum(
        (
            jnp.sum(conv_out * pix_mask, axis=(1, 2, 3)),
            jnp.sum(conv_out * conv_out * pix_mask, axis=(1, 2, 3)),
        ),
        "sp",
    )
    branch_mean = stat_sum / valid_count
    branch_inv = lax.rsqrt(stat_square / valid_count - branch_mean * branch_mean + epsilon)
    normed = (conv_out - branch_mean[:, None, None, None, :]) * branch_inv[:, None, None, None, :]
    pre_act = bn_gains[:4][:, None, None, None, :] * normed + bn_shifts[:4][:, None, None, None, :]
    branch_act = (pix_mask * jax.nn.silu(pre_act)).astype(jnp.bfloat16)
    own_sums = jnp.sum(masked_values, axis=(1, 2), dtype=jnp.float32)
    own_pooled = own_sums / own_count[:, None]
    pool_weight = w_pool.astype(jnp.float32)
    pooled = lax.psum(own_pooled[:, None, :] * group_onehot[None, :, None], "sp")
    projected = jnp.dot(
        pooled.reshape(images, channel_total), pool_weight.T, precision=highest_precision
    )
    pool_mean = jnp.mean(projected, axis=0)
    pool_inv = lax.rsqrt(jnp.mean(projected * projected, axis=0) - pool_mean * pool_mean + epsilon)
    pool_normed = (projected - pool_mean) * pool_inv
    pool_pre = bn_gains[4] * pool_normed + bn_shifts[4]
    pool_act = jax.nn.silu(pool_pre).astype(jnp.bfloat16)
    own_act = jnp.sum(
        pool_act.astype(jnp.float32).reshape(count_k, groups, local_output)
        * group_onehot[None, :, None],
        axis=1,
    )
    pool_pixels = (own_act[:, None, None, :] * pix_mask).astype(jnp.bfloat16)
    stacked = jnp.concatenate([branch_act, pool_pixels[None]], axis=0).reshape(
        5, pixels, local_output
    )
    partial_value = jnp.einsum("bpf,bfo->po", stacked, w_proj, preferred_element_type=jnp.float32)
    mixed_sum = lax.psum_scatter(
        partial_value.reshape(count_k, rows_dev, grid_width, full_out),
        "ch",
        scatter_dimension=3,
        tiled=True,
    )
    final_sum, final_square = lax.psum(
        (
            jnp.sum(mixed_sum * pix_mask, axis=(0, 1, 2)),
            jnp.sum(mixed_sum * mixed_sum * pix_mask, axis=(0, 1, 2)),
        ),
        "sp",
    )
    final_mean = final_sum / valid_count
    final_inv = lax.rsqrt(final_square / valid_count - final_mean * final_mean + epsilon)
    final_normed = (mixed_sum - final_mean) * final_inv
    final_pre = bn_gains[5] * final_normed + bn_shifts[5]
    output = (pix_mask * jax.nn.silu(final_pre)).astype(jnp.bfloat16)
    final_dt = pix_mask * own_out_grad.astype(jnp.float32) * silu_slope(final_pre)
    final_beta, final_gamma = lax.psum(
        (jnp.sum(final_dt, axis=(0, 1, 2)), jnp.sum(final_dt * final_normed, axis=(0, 1, 2))), "sp"
    )
    mixed_grad = (
        pix_mask
        * final_inv
        * bn_gains[5]
        * (final_dt - final_beta / valid_count - final_normed * final_gamma / valid_count)
    ).astype(jnp.bfloat16)
    full_grad = lax.all_gather(mixed_grad, "ch", axis=3, tiled=True).reshape(pixels, full_out)
    g_proj = jnp.einsum("bpf,po->bfo", stacked, full_grad, preferred_element_type=jnp.float32)
    act_grads = jnp.einsum(
        "po,bfo->bpf", full_grad, w_proj, preferred_element_type=jnp.float32
    ).reshape(5, count_k, rows_dev, grid_width, local_output)
    branch_dt = pix_mask * act_grads[:4] * silu_slope(pre_act)
    pool_own_grad = jnp.sum(act_grads[4] * pix_mask, axis=(1, 2))
    branch_beta, branch_gamma, pool_grad = lax.psum(
        (
            jnp.sum(branch_dt, axis=(1, 2, 3)),
            jnp.sum(branch_dt * normed, axis=(1, 2, 3)),
            pool_own_grad[:, None, :] * group_onehot[None, :, None],
        ),
        "sp",
    )
    convolution_gradients = (
        pix_mask
        * branch_inv[:, None, None, None, :]
        * bn_gains[:4][:, None, None, None, :]
        * (
            branch_dt
            - branch_beta[:, None, None, None, :] / valid_count
            - normed * branch_gamma[:, None, None, None, :] / valid_count
        )
    ).astype(jnp.bfloat16)
    pool_dt = pool_grad.reshape(images, local_output) * silu_slope(pool_pre)
    pool_beta = jnp.sum(pool_dt, axis=0)
    pool_gamma = jnp.sum(pool_dt * pool_normed, axis=0)
    proj_grad = (
        pool_inv * bn_gains[4] * (pool_dt - pool_beta / images - pool_normed * pool_gamma / images)
    )
    own_proj_grad = jnp.sum(
        proj_grad.reshape(count_k, groups, local_output) * group_onehot[None, :, None], axis=1
    )
    g_pool = jnp.einsum("kf,kc->fc", own_proj_grad, own_pooled, precision=highest_precision)
    pooled_grad = (
        jnp.einsum("kf,fc->kc", own_proj_grad, pool_weight, precision=highest_precision)
        / own_count[:, None]
    )
    point_grad = convolution_gradients[0].reshape(pixels, local_output)
    g_point = jnp.einsum("pf,pc->fc", point_grad, flat_pix, preferred_element_type=jnp.float32)
    input_term = jnp.einsum("pf,fc->pc", point_grad, w_point, preferred_element_type=jnp.float32)
    input_term = (
        input_term.reshape(count_k, rows_dev, grid_width, channel_total)
        + pooled_grad[:, None, None, :]
    )
    atrous_list = []
    for dilation_index, dilation_factor in enumerate(dilation_factors):
        dilation_rate = rows_dev * dilation_factor
        tap_list = []
        for row_offset_tap in range(3):
            shift_amount = (row_offset_tap - 1) * dilation_factor
            if shift_amount == 0:
                received_part = convolution_gradients[dilation_index + 1]
            else:
                received_part = shifted_gradients(
                    convolution_gradients[dilation_index + 1], shift_amount
                ) * source_inside(block_id, shift_amount).astype(jnp.bfloat16)
            spread = jnp.stack(
                [
                    shift_cols(received_part, dilation_rate),
                    received_part,
                    shift_cols(received_part, -dilation_rate),
                ],
                axis=3,
            ).reshape(pixels, 3 * local_output)
            tap_list.append(
                jnp.einsum(
                    "pt,pc->tc", spread, flat_pix, preferred_element_type=jnp.float32
                ).reshape(3, local_output, channel_total)
            )
            tap_weight_slice = atrous_weight[dilation_index, row_offset_tap].reshape(
                3 * local_output, channel_total
            )
            input_term = input_term + jnp.einsum(
                "pt,tc->pc", spread, tap_weight_slice, preferred_element_type=jnp.float32
            ).reshape(count_k, rows_dev, grid_width, channel_total)
        atrous_list.append(jnp.stack(tap_list))
    g_atrous = jnp.stack(atrous_list)
    in_grad = lax.psum_scatter(
        (input_term * pix_mask).astype(jnp.bfloat16), "ch", scatter_dimension=3, tiled=True
    )
    g_point, g_atrous, g_proj, g_pool = (
        lax.psum(g_point.astype(jnp.bfloat16), "sp").astype(jnp.float32),
        lax.psum(g_atrous.astype(jnp.bfloat16), "sp").astype(jnp.float32),
        lax.psum(g_proj.astype(jnp.bfloat16), "sp").astype(jnp.float32),
        lax.psum(g_pool.astype(jnp.bfloat16), "sp").astype(jnp.float32),
    )
    g_gains = jnp.concatenate([branch_gamma, pool_gamma[None], final_gamma[None]], axis=0)
    g_shifts = jnp.concatenate([branch_beta, pool_beta[None], final_beta[None]], axis=0)
    return (output, in_grad, g_point, g_atrous, g_pool, g_proj, g_gains, g_shifts)


def body(
    features, heights, widths, w_point, atrous_weight, w_pool, w_proj, bn_gains, bn_shifts, out_grad
):
    images, rows_dev, cols, C = features.shape
    L = w_point.shape[0]
    if lax.axis_size("sp") != BLOCKS or lax.axis_size("ch") != 4 or L != 64:
        return plain_body(
            features, heights, widths, w_point, atrous_weight, w_pool, w_proj, bn_gains, bn_shifts, out_grad
        )
    F = w_proj.shape[2]
    W = BRANCHES * L
    slabs = images * rows_dev
    cells = slabs * cols
    rates = tuple(rows_dev * f for f in dilation_factors)
    block_id = lax.axis_index("sp")
    own = lax.axis_index("ch")
    h, w = heights[:, 0], widths[:, 0]
    row_ids = block_id * rows_dev + jnp.arange(rows_dev, dtype=jnp.int32)
    lim = jnp.where(row_ids[None, :] < h[:, None], w[:, None], 0).reshape(slabs)
    own_count = (h * w).astype(f32)
    n = jnp.sum(own_count)
    x = features.reshape(cells, C)
    og = out_grad.reshape(cells, F)

    norms = jnp.concatenate([bn_gains, bn_shifts, jnp.zeros((4, L), f32)], axis=0).reshape(4, W)
    wp = w_proj.reshape(5 * L, F)
    packed = jnp.concatenate([wp, thirds(norms), jnp.zeros((4, F), bf16)], axis=0)
    packed_y = swap(packed, "ch", 2)
    packed_core = swap(packed, "ch", 1)
    packed_all = [packed, packed_core, packed_y, swap(packed_y, "ch", 1)]
    count = n.reshape(1)
    own_id = own.astype(jnp.int32).reshape(1)

    KT = 512
    steps = C // KT
    x_spec = pl.BlockSpec((cells, KT), lambda k: (0, k))
    first = [(1 - (block_id // f) % 2).astype(jnp.int32) for f in dilation_factors]

    def side_taps(which, x):
        out = pl.pallas_call(
            functools.partial(
                side_kernel, steps=steps, slabs=slabs, cols=cols, rates=tuple(rates[j] for j in which)
            ),
            grid=(steps,),
            in_specs=[SMEM, SMEM, x_spec]
            + [
                pl.BlockSpec((1, 1, 3, L, KT), lambda k, j=j, u=u: (j, u, 0, 0, k))
                for j in which
                for u in (0, 2)
            ],
            out_specs=[pl.BlockSpec((cells // 2, 2 * L), lambda k: (0, 0))] * (2 * len(which)),
            out_shape=[jax.ShapeDtypeStruct((cells // 2, 2 * L), bf16)] * (2 * len(which)),
            scratch_shapes=[
                pltpu.VMEM((6 * len(which) * L, KT), bf16),
                pltpu.VMEM((cells, 6 * len(which) * L), f32),
            ],
            compiler_params=params(),
            cost_estimate=cost(2 * cells * C * 6 * len(which) * L, 10e6),
            name="side_taps",
        )(lim, jnp.stack([first[j] for j in which]), x, *[atrous_weight] * (2 * len(which)))
        out = after(tuple(out), packed_y, packed_core)
        moved = []
        for i, j in enumerate(which):
            moved += neighbours(out[2 * i], out[2 * i + 1], "sp", dilation_factors[j])
        return moved, out[0]

    narrow = C // 2
    valid = (jnp.arange(cols, dtype=jnp.int32)[None, :] < lim[:, None]).reshape(cells, 1)
    cut = narrow // BLOCKS
    part = cells // images
    image = lax.dynamic_slice(x, (own * part, 0), (part, narrow))
    image = jnp.where(lax.dynamic_slice_in_dim(valid, own * part, part), image, jnp.zeros((), bf16))
    column = block_id // 2
    sent = [lax.dynamic_slice_in_dim(image, (column ^ dz) * 2 * cut, 2 * cut, 1) for dz in range(4)]
    pieces = sent
    sent = [sent[0]] + [swap(sent[dz], "sp", 2 * dz) for dz in (1, 2, 3)]
    mine = jnp.stack(sent)
    wide_w = (C - narrow) // 4
    own_wide = lax.dynamic_slice_in_dim(x, narrow + own * wide_w, wide_w, 1)
    own_wide = jnp.where(valid, own_wide, jnp.zeros((), bf16))
    halo, made = side_taps((0, 1, 2), after(x, packed, own_wide, *pieces))
    x_wide = lax.all_gather(own_wide, ("sp", "ch"), axis=0).reshape(BLOCKS, 4, cells, wide_w)
    x_then = after(x, made, halo[0], halo[1], *sent)
    centre, sums = pl.pallas_call(
        functools.partial(centre_kernel, steps=steps, slabs=slabs, cols=cols, rates=rates, images=images),
        grid=(steps,),
        in_specs=[
            SMEM,
            x_spec,
            pl.BlockSpec((3, 1, 3, L, KT), lambda k: (0, 1, 0, 0, k)),
            pl.BlockSpec((L, KT), lambda k: (0, k)),
        ],
        out_specs=[pl.BlockSpec((cells, W), lambda k: (0, 0)), pl.BlockSpec((8, KT), lambda k: (0, k))],
        out_shape=[jax.ShapeDtypeStruct((cells, W), f32), jax.ShapeDtypeStruct((8, C), f32)],
        scratch_shapes=[pltpu.VMEM((10 * L, KT), bf16), pltpu.VMEM((cells, 10 * L), f32)],
        compiler_params=params(),
        cost_estimate=cost(2 * cells * C * 10 * L, 8e6),
        name="centre_taps",
    )(lim, x_then, atrous_weight, w_point)
    own_pooled = sums[:images] / own_count[:, None]
    proj_part = lax.dot_general(own_pooled, w_pool.astype(f32), NT, precision=highest_precision)

    extra = jnp.concatenate(
        [jnp.pad(proj_part, ((4, 4 - images), (0, W - L))), own_pooled.reshape(-1, W)], axis=0
    )
    conv, conv_send, message, local = pl.pallas_call(
        functools.partial(combine_kernel, slabs=slabs, cols=cols),
        in_specs=[SMEM] + [VMEM] * 8,
        out_specs=[VMEM] * 4,
        out_shape=[
            jax.ShapeDtypeStruct((cells, W), f32),
            jax.ShapeDtypeStruct((cells, W), bf16),
            jax.ShapeDtypeStruct(extra.shape, f32),
            jax.ShapeDtypeStruct((8, W), f32),
        ],
        compiler_params=params(20),
        cost_estimate=cost(2e6, 4e6),
        name="combine_taps",
    )(lim, centre, *halo, extra)
    conv_y = swap(conv_send, "ch", 2)
    conv_core = swap(conv_send, "ch", 1)
    message = parts_over_sp(message)
    conv_diag = swap(after(conv_y, *message), "ch", 1)
    tile = ((message[0][:8] + message[1][:8]) + (message[2][:8] + message[3][:8])) + local
    mine = after(mine, tile)
    keep = lax.dynamic_slice_in_dim(mine, (block_id % 2) * cut, cut, 2)
    give = lax.dynamic_slice_in_dim(mine, (1 - block_id % 2) * cut, cut, 2)
    taken = swap(give, "sp", 1)
    tiles = [tile] + [swap(tile, "ch", b) for b in (1, 2, 3)]
    projected = tile[4 : 4 + images, :L]
    pool_mean = jnp.mean(projected, axis=0)
    pool_rstd = lax.rsqrt(jnp.mean(projected * projected, axis=0) - pool_mean * pool_mean + epsilon)
    pool_normed = (projected - pool_mean) * pool_rstd
    pool_pre = bn_gains[4] * pool_normed + bn_shifts[4]
    pool_act = jax.nn.silu(pool_pre).astype(bf16)

    mixed, act, mixed_stat, own_stat = pl.pallas_call(
        functools.partial(mix_kernel, slabs=slabs, cols=cols, images=images),
        in_specs=[SMEM] * 2 + [VMEM] * 12,
        out_specs=[VMEM] * 4,
        out_shape=[
            jax.ShapeDtypeStruct((cells, F), f32),
            jax.ShapeDtypeStruct((cells, W), bf16),
            jax.ShapeDtypeStruct((8, F), f32),
            jax.ShapeDtypeStruct((8, W), f32),
        ],
        scratch_shapes=[pltpu.VMEM((cells, W), bf16)],
        compiler_params=params(20),
        cost_estimate=cost(2 * cells * 4 * W * F, 6e6),
        name="mix_branches",
    )(lim, count, conv, conv_core, conv_y, conv_diag, *tiles, *packed_all)
    total = parts_over_sp(mixed_stat)
    out_all, fdt, fsums, fstat = pl.pallas_call(
        functools.partial(final_kernel, slabs=slabs, cols=cols),
        in_specs=[SMEM] * 3 + [VMEM] * 10,
        out_specs=[VMEM] * 4,
        out_shape=[
            jax.ShapeDtypeStruct((cells, F), bf16),
            jax.ShapeDtypeStruct((cells, F), f32),
            jax.ShapeDtypeStruct((8, F), f32),
            jax.ShapeDtypeStruct((8, F), f32),
        ],
        compiler_params=params(20),
        cost_estimate=cost(2e6, 4e6),
        name="final_norm",
    )(lim, count, own_id, mixed, og, *packed_all, *total)
    ftotal = parts_over_sp(fsums)
    final_sums = (ftotal[0] + ftotal[1]) + (ftotal[2] + ftotal[3])
    final_beta, final_gamma = final_sums[0], final_sums[1]
    dt, gproj, image_sums, bsums = pl.pallas_call(
        functools.partial(branch_kernel, slabs=slabs, cols=cols, images=images),
        in_specs=[SMEM] * 2 + [VMEM] * 11,
        out_specs=[VMEM] * 4,
        out_shape=[
            jax.ShapeDtypeStruct((cells, W), f32),
            jax.ShapeDtypeStruct((W, F), f32),
            jax.ShapeDtypeStruct((8, F), f32),
            jax.ShapeDtypeStruct((8, W), f32),
        ],
        scratch_shapes=[pltpu.VMEM((cells, F), bf16)],
        compiler_params=params(20),
        cost_estimate=cost(4 * cells * W * F, 8e6),
        name="branch_grads",
    )(
        lim, count, mixed, fdt, fstat, conv, act, own_stat, wp[:W], *ftotal
    )
    image_sums = image_sums[:images]
    pool_part = lax.dot_general(image_sums, w_proj[4].astype(f32), NT, precision=highest_precision)
    gproj_pool = lax.dot_general(pool_act.astype(f32), image_sums, TN, precision=highest_precision)
    gp = jnp.concatenate([gproj, gproj_pool], axis=0)
    across, along = block_id % 2, block_id // 2
    gp_half, gp_piece = gp.shape[0] // 2, gp.shape[0] // BLOCKS
    bown = jnp.concatenate([bsums[:4], jnp.pad(pool_part, ((0, 0), (0, W - L)))], axis=0)
    got = swap(
        jnp.concatenate(
            [thirds(bown), lax.dynamic_slice_in_dim(gp, (1 - across) * gp_half, gp_half).astype(bf16)], axis=0
        ),
        "sp",
        1,
    )
    bown = bown + whole(got[:24])
    gp = lax.dynamic_slice_in_dim(gp, across * gp_half, gp_half) + got[24:].astype(f32)
    mine_thirds = thirds(bown)
    got = [
        swap(
            jnp.concatenate(
                [mine_thirds, lax.dynamic_slice_in_dim(gp, (along ^ dz) * gp_piece, gp_piece).astype(bf16)],
                axis=0,
            ),
            "sp",
            2 * dz,
        )
        for dz in (1, 2, 3)
    ]
    btile = (bown + whole(got[0][:24])) + (whole(got[1][:24]) + whole(got[2][:24]))
    gp = lax.dynamic_slice_in_dim(gp, along * gp_piece, gp_piece)
    gp = (gp + got[0][24:].astype(f32)) + (got[1][24:].astype(f32) + got[2][24:].astype(f32))
    gp = jnp.pad(gp, ((0, -gp_piece % 16), (0, 0)))
    branch_beta, branch_gamma = btile[0], btile[1]
    cgt = pl.pallas_call(
        functools.partial(grad_kernel, slabs=slabs, cols=cols),
        in_specs=[SMEM] * 2 + [VMEM] * 5,
        out_specs=VMEM,
        out_shape=jax.ShapeDtypeStruct((W + 16, cells), bf16),
        scratch_shapes=[pltpu.VMEM((cells, W), f32)],
        compiler_params=params(20),
        cost_estimate=cost(2e6, 4e6),
        name="conv_grads",
    )(lim, count, dt, conv, own_stat, btile, gp)
    pool_dt = btile[4 : 4 + images, :L] * silu_slope(pool_pre)
    pool_beta = jnp.sum(pool_dt, axis=0)
    pool_gamma = jnp.sum(pool_dt * pool_normed, axis=0)
    proj_grad = (
        pool_rstd * bn_gains[4] * (pool_dt - pool_beta / images - pool_normed * pool_gamma / images)
    )
    g_gains = jnp.concatenate([branch_gamma.reshape(4, L), pool_gamma[None],
        lax.dynamic_slice_in_dim(final_gamma, own * L, L)[None]], axis=0)
    g_shifts = jnp.concatenate([branch_beta.reshape(4, L), pool_beta[None],
        lax.dynamic_slice_in_dim(final_beta, own * L, L)[None]], axis=0)
    output = lax.dynamic_slice_in_dim(out_all, own * L, L, 1).reshape(images, rows_dev, cols, L)
    pooled_grad = (
        jnp.einsum("kf,fc->kc", proj_grad, w_pool.astype(f32), precision=highest_precision)
        / own_count[:, None]
    )
    ANY = pl.BlockSpec(memory_space=pl.ANY)
    col_row = jnp.broadcast_to((jnp.arange(cells, dtype=jnp.int32) % cols)[None, :], (8, cells))
    pos = jnp.stack([block_id, own % 2, own]).astype(jnp.int32)
    def column_taps(block):
        return pl.pallas_call(
            functools.partial(expand_kernel, cols=cols, rates=rates),
            grid=(1,),
            in_specs=[pl.BlockSpec((8, cells), lambda i: (0, 0)), pl.BlockSpec((W, cells), lambda i: (0, 0))],
            out_specs=pl.BlockSpec((10 * L, cells), lambda i: (0, 0)),
            out_shape=jax.ShapeDtypeStruct((10 * L, cells), bf16),
            compiler_params=params(),
            cost_estimate=cost(1e9, 6e6),
            name="column_taps",
        )(col_row, block)

    near = [swap(cgt, "sp", b) for b in (2, 4)]
    near.append(swap(after(cgt, near[0]), "sp", 6))
    pair = swap(cgt, "sp", 1)
    taps = [column_taps(cgt), column_taps(pair), column_taps(near[0])]
    near_pair = swap(near[0], "sp", 1)
    taps.append(column_taps(near_pair))
    message = after(tuple(message), pair)
    pooled = ((message[0][8:] + message[1][8:]) + (message[2][8:] + message[3][8:])).reshape(images, C)
    x_slices = after(jnp.stack([keep, taken], axis=1).reshape(1, BLOCKS, part, cut), pair)
    x_slices = jnp.concatenate([x_slices, swap(x_slices, "ch", 2)], axis=0)
    x_core = swap(x_slices, "ch", 1)
    g_pool = jnp.einsum("kf,kc->fc", proj_grad, pooled, precision=highest_precision)
    far = [after(near[1], *taps[:2], output, g_pool, g_gains, g_shifts, pooled_grad), after(near[2], *taps)]
    far_pairs = [swap(t, "sp", 1) for t in far]
    blocks = [cgt, pair, near[0], near_pair, far[0], far_pairs[0], far[1], far_pairs[1]]
    taps += [column_taps(t) for t in blocks[4:]]
    eighth = narrow // BLOCKS
    tap_scratch = pltpu.VMEM((10 * L, BLOCKS * cells), bf16)
    gw = pl.pallas_call(
        functools.partial(narrow_kernel, parts=images),
        in_specs=[SMEM] + [ANY] * (BLOCKS + 2),
        out_specs=pl.BlockSpec((28 * L, eighth), lambda i: (0, 0)),
        grid=(1,),
        out_shape=jax.ShapeDtypeStruct((28 * L, eighth), bf16),
        scratch_shapes=[
            tap_scratch,
            pltpu.VMEM((BLOCKS * cells, eighth), bf16),
            pltpu.SemaphoreType.DMA((BLOCKS,)),
            pltpu.SemaphoreType.DMA((images, BLOCKS)),
        ],
        compiler_params=params(),
        cost_estimate=cost(2 * cells * BLOCKS * 28 * L * eighth, 12e6),
        name="narrow_weight_grads",
    )(pos, *taps, x_slices, x_core)
    gw_all = lax.all_gather(gw, "sp", axis=0)
    pos, gw = lax.optimization_barrier((pos, gw))
    group = C // 4
    ig_keep, ig_give = pl.pallas_call(
        functools.partial(input_grad_kernel, slabs=slabs, cols=cols, rates=rates, images=images),
        grid_spec=pltpu.PrefetchScalarGridSpec(
            num_scalar_prefetch=2,
            grid=(4,),
            in_specs=[
                pl.BlockSpec((8, cells), lambda i, p, l: (0, 0)),
                pl.BlockSpec((27 * L, group), lambda i, p, l: (0, p[2] ^ i)),
                pl.BlockSpec((L, group), lambda i, p, l: (0, p[2] ^ i)),
                pl.BlockSpec((8, group), lambda i, p, l: (0, p[2] ^ i)),
            ]
            + [ANY] * BLOCKS,
            out_specs=[pl.BlockSpec((1, cells, group), lambda i, p, l: (i // 2, 0, 0))] * 2,
            scratch_shapes=[
                pltpu.VMEM((BLOCKS, W, cells), bf16),
                pltpu.VMEM((cells, 28 * L), bf16),
                pltpu.VMEM((28 * L, group), bf16),
                pltpu.SemaphoreType.DMA((BLOCKS,)),
            ],
        ),
        out_shape=[jax.ShapeDtypeStruct((2, cells, group), bf16)] * 2,
        compiler_params=params(),
        cost_estimate=cost(1e6, 1e6),
        name="input_grads",
    )(pos, lim, col_row, atrous_weight.reshape(27 * L, C), w_point,
      jnp.pad(pooled_grad, ((0, 8 - images), (0, 0))), *blocks)
    from_core = swap(ig_give, "ch", 1)

    from_core = from_core.astype(f32)
    keep = ig_keep[0].astype(f32) + from_core[0]
    give = (ig_keep[1].astype(f32) + from_core[1]).astype(bf16)
    given = swap(give, "ch", 2)
    pos = after(pos, give)
    g_wide, p_wide, g_proj = pl.pallas_call(
        wide_kernel,
        grid=(4,),
        in_specs=[SMEM, pl.BlockSpec((BLOCKS, 1, cells, wide_w), lambda i: (0, i, 0, 0))]
        + [ANY] * BLOCKS
        + [pl.BlockSpec((16, cells), lambda i: (W // 16, 0))] * BLOCKS,
        out_specs=[
            pl.BlockSpec((27 * L, wide_w), lambda i: (0, narrow // wide_w + i)),
            pl.BlockSpec((L, wide_w), lambda i: (0, narrow // wide_w + i)),
            pl.BlockSpec((5 * L, F), lambda i: (0, 0)),
        ],
        out_shape=[
            jax.ShapeDtypeStruct((27 * L, C), f32),
            jax.ShapeDtypeStruct((L, C), f32),
            jax.ShapeDtypeStruct((5 * L, F), f32),
        ],
        scratch_shapes=[tap_scratch, pltpu.SemaphoreType.DMA((BLOCKS,))],
        compiler_params=params(),
        cost_estimate=cost(1e6, 1e6),
        name="wide_weight_grads",
    )(pos, x_wide, *taps, *blocks)
    g_proj = g_proj.reshape(5, L, F)
    in_grad = (keep + after(given, p_wide).astype(f32)).astype(bf16)
    in_grad = in_grad.reshape(images, rows_dev, cols, group)

    step = 9 * L
    g_atrous, g_point = pl.pallas_call(
        widen_kernel,
        grid=(3,),
        in_specs=[
            pl.BlockSpec((BLOCKS, step, eighth), lambda i: (0, i, 0)),
            pl.BlockSpec((BLOCKS, L, eighth), lambda i: (0, 27, 0)),
            ANY,
            ANY,
        ],
        out_specs=[
            pl.BlockSpec((step, narrow), lambda i: (i, 0)),
            pl.BlockSpec((L, narrow), lambda i: (0, 0)),
        ],
        out_shape=[jax.ShapeDtypeStruct((27 * L, C), f32), jax.ShapeDtypeStruct((L, C), f32)],
        input_output_aliases={2: 0, 3: 1},
        compiler_params=params(),
        cost_estimate=cost(1e6, 20e6),
        name="widen",
    )(gw_all, gw_all, g_wide, p_wide)
    g_atrous = g_atrous.reshape(3, 3, 3, L, C)
    return (output, in_grad, g_point, g_atrous, g_pool, g_proj, g_gains, g_shifts)


def solution(mesh):
    placed = (
        P(None, "sp", None, None),
        P(),
        P(),
        P("ch", None),
        P(None, None, None, "ch", None),
        P("ch", None),
        P(None, "ch", None),
        P(None, "ch"),
        P(None, "ch"),
        P(None, "sp", None, None),
    )
    return jax.shard_map(
        body,
        mesh=mesh,
        in_specs=placed,
        out_specs=(
            P(None, "sp", None, "ch"),
            P(None, "sp", None, "ch"),
            P("ch", None),
            P(None, None, None, "ch", None),
            P("ch", None),
            P(None, "ch", None),
            P(None, "ch"),
            P(None, "ch"),
        ),
        check_vma=False,
    )
```
